256 devices in a mesh: grp: 8 (over z), shard: 32 (over x, y, core).
Axes of the slice: x: 4, y: 4, z: 8, core: 2. Of those that a mesh axis runs over, the one named last changes fastest.
Arguments:
- values: bfloat16 [32768, 2048], P(('grp', 'shard')), may hold values from -6 to 6
- state_input: float32 [32768, 64], P(('grp', 'shard')), may hold values from -0.0625 to 0.0625
- state_output: float32 [32768, 64], P(('grp', 'shard')), may hold values from -6 to 6
- log_decay: float32 [32768, 32], P(('grp', 'shard')), may hold values from -1 to 0, as said below
- level_lam: float32 [32768, 256], P(('grp', 'shard')), may hold values from 0.2 to 2
- level_ids: int32 [256, 8], P(('grp', 'shard')), may hold values from 0 to 7
- upstream: bfloat16 [32768, 2048], P(('grp', 'shard')), may hold values from -6 to 6
- final_upstream: float32 [32, 64, 64], replicated, may hold values from -6 to 6
Outputs:
- values_grad: bfloat16 [32768, 2048], P(('grp', 'shard'))
- input_grad: float32 [32768, 64], P(('grp', 'shard'))
- output_grad: float32 [32768, 64], P(('grp', 'shard'))
- decay_grad: float32 [32768, 32], P(('grp', 'shard'))
- lambda_grad: float32 [32768, 256], P(('grp', 'shard'))
The draws below stay inside these ranges and needn't reach their ends.
Inputs may be any that keep to these rules, and one draw needn't show every extreme that they name: `log_decay`: every log decay is negative.
All inputs are finite; a program needn't handle non-finite values.
Results may differ from the reference program's by a relative error of at most 0.018.
Values sent between devices are 32-bit elements; how exact they have to be, the bound alone decides.
A program may use at most 128 MiB of HBM per device.

```python
import math
import jax
import jax.numpy as jnp
from jax import lax

HEAD_TOTAL = 32
HDIM = 64
STATE = 64
LEVELS = 8
TOK_DEV = 128
STRETCHES = 256
TOKEN_TOTAL = 32768
N_GRP = 8
N_SHARD = 32


def draw_log_decay(key, part):
    key = jax.random.fold_in(key, 7)
    random_key_quick, random_key_rate, random_key_jitter, random_key_spike, random_key_depth = jax.random.split(key, 5)
    fast_share = 0.5
    fast_flag = jax.random.bernoulli(random_key_quick, fast_share, (HEAD_TOTAL,)).astype(jnp.float32)
    spread_draw = jax.random.uniform(random_key_rate, (HEAD_TOTAL,), jnp.float32)
    slow_rate = jnp.exp(jnp.log(0.3 / TOKEN_TOTAL) + spread_draw * (jnp.log(2.3 / TOKEN_TOTAL) - jnp.log(0.3 / TOKEN_TOTAL)))
    fast_rate = jnp.exp(jnp.log(1.0 / 50.0) + spread_draw * (jnp.log(1.0 / 30.0) - jnp.log(1.0 / 50.0)))
    per_head_rate = fast_flag * fast_rate + (1.0 - fast_flag) * slow_rate
    jitter_factor = jax.random.uniform(random_key_jitter, (TOKEN_TOTAL, HEAD_TOTAL), jnp.float32, 0.5, 1.5)
    spike_mask = jax.random.bernoulli(random_key_spike, 6.0 / TOKEN_TOTAL, (TOKEN_TOTAL, 1)).astype(jnp.float32)
    spike_levels_depth = jax.random.uniform(random_key_depth, (TOKEN_TOTAL, HEAD_TOTAL), jnp.float32, 0.22, 0.69)
    return (-(per_head_rate[None, :] * jitter_factor) - spike_mask * spike_levels_depth).astype(jnp.float32)


def place_ends(entries, rng, least, largest):
    index_at = [jax.random.randint(jax.random.fold_in(rng, axis), (), 0, length) for axis, length in enumerate(entries.shape)]
    main_axis = entries.shape.index(max(entries.shape))
    beside = index_at[:main_axis] + [(index_at[main_axis] + 1) % entries.shape[main_axis]] + index_at[main_axis + 1:]
    return entries.at[tuple(index_at)].set(least).at[tuple(beside)].set(largest)


def level_of(key, shape, cuts, least, largest):
    gain = 1.0
    for dim, blocks in cuts:
        heights = jax.random.uniform(jax.random.fold_in(jax.random.fold_in(key, 6), dim), (blocks,), jnp.float32, least / len(cuts), largest / len(cuts))
        gain = gain * jnp.repeat(jnp.exp(heights), shape[dim] // blocks).reshape((-1,) + (1,) * (len(shape) - 1 - dim))
    return gain


def scatter_about(own_key, shape, scale, reach, shards=(), kind=jnp.bfloat16):
    loudness = level_of(own_key, shape, shards, -0.22, 0.18) if shards else 1.0
    result = jax.random.normal(own_key, shape, jnp.float32) * scale * loudness
    return jnp.minimum(jnp.maximum(result, -reach), reach).astype(kind)


def setup_inputs(seed: int = 0) -> dict:
    splits = jax.random.split(jax.random.key(seed), 9)
    values = scatter_about(splits[0], (TOKEN_TOTAL, HEAD_TOTAL * HDIM), 1.0, 6.0, ((0, 256),))
    state_input = scatter_about(splits[1], (TOKEN_TOTAL, STATE), (STATE * TOK_DEV) ** -0.5, 0.0625, ((0, 256),), jnp.float32)
    state_output = scatter_about(splits[2], (TOKEN_TOTAL, STATE), 1.0, 6.0, ((0, 256),), jnp.float32)
    log_decay = draw_log_decay(jax.random.fold_in(splits[8], 71), 0)
    level_lam = jnp.clip(jnp.exp(math.log(2.0) - 2.3025851 * jax.random.uniform(splits[4], (TOKEN_TOTAL, LEVELS * HEAD_TOTAL), jnp.float32) ** level_of(splits[4], (TOKEN_TOTAL, LEVELS * HEAD_TOTAL), ((0, 256),), -0.2, 0.2)), 0.2, 2.0)
    level_ids = place_ends(jax.random.randint(splits[5], (STRETCHES, LEVELS), 0, LEVELS), jax.random.fold_in(splits[5], 1), 0, LEVELS - 1).astype(jnp.int32)
    upstream = scatter_about(splits[6], (TOKEN_TOTAL, HEAD_TOTAL * HDIM), 1.0, 6.0, ((0, 256),))
    final_upstream = scatter_about(splits[7], (HEAD_TOTAL, STATE, HDIM), 1.0, 6.0, (), jnp.float32)
    return {"values": values, "state_input": state_input, "state_output": state_output, "log_decay": log_decay, "level_lam": level_lam, "level_ids": level_ids, "upstream": upstream, "final_upstream": final_upstream}


highest = lax.Precision.HIGHEST

def low_copy(array):
    return array.astype(jnp.bfloat16).astype(jnp.float32)

def stretch_state(values, state_input, log_decay):
    cumlog = jnp.cumsum(log_decay, axis=0)
    tail_decay = jnp.exp(cumlog[-1][None, :] - cumlog)
    decayed = low_copy(values * tail_decay[:, :, None])
    stretch_sum = jnp.einsum('tn,thp->hnp', low_copy(state_input), decayed, precision=highest)
    return (stretch_sum, jnp.exp(cumlog[-1]))

def intra_output(values, state_input, state_output, log_decay):
    tok_count, head_count, head_dim = values.shape
    head_block = min(16, head_count)
    group_count = head_count // head_block
    cumlog = jnp.cumsum(log_decay, axis=0)
    scores = jnp.dot(state_output, state_input.T, precision=highest)
    causal = jnp.arange(tok_count)[:, None] >= jnp.arange(tok_count)[None, :]
    value_groups = values.reshape(tok_count, group_count, head_block, head_dim).transpose(1, 0, 2, 3)
    cum_groups = cumlog.reshape(tok_count, group_count, head_block).transpose(1, 2, 0)

    def head_group(pair):
        group_values, group_cum = pair
        log_gap = group_cum[:, :, None] - group_cum[:, None, :]
        weighted = low_copy(jnp.exp(jnp.where(causal[None], log_gap, -jnp.inf)) * scores[None])
        return jnp.einsum('hts,shp->thp', weighted, low_copy(group_values), precision=highest)
    mixed = lax.map(head_group, (value_groups, cum_groups))
    return mixed.transpose(1, 0, 2, 3).reshape(tok_count, head_count, head_dim)

def inter_output(state_output, log_decay, weights, level_states):
    growth = jnp.exp(jnp.cumsum(log_decay, axis=0))
    out_low = low_copy(state_output)
    inter_total = jnp.zeros((state_output.shape[0], level_states.shape[1], level_states.shape[3]), jnp.float32)
    for bit_no in range(level_states.shape[0]):
        read_out = jnp.einsum('tn,hnp->thp', out_low, low_copy(level_states[bit_no]), precision=highest)
        inter_total = inter_total + (growth * weights[:, bit_no])[:, :, None] * read_out
    return inter_total

def level_weights(level_lam, id_row, bit_count):
    head_count = level_lam.shape[1] // id_row.shape[0]
    table = level_lam.reshape(level_lam.shape[0], id_row.shape[0], head_count)
    onehot = (id_row[:bit_count, None] == jnp.arange(id_row.shape[0], dtype=jnp.int32)[None, :]).astype(jnp.float32)
    return jnp.einsum('tlh,bl->tbh', table, onehot, precision=highest)

def level_merge(own_agg, own_decay, own_prefix, far_agg, far_decay, upper_half):
    upper_state = upper_half[..., None, None]
    held_state = upper_state * own_prefix[..., None, None] * far_agg
    merged = upper_state * (own_decay[..., None, None] * far_agg + own_agg) + (1.0 - upper_state) * (far_decay[..., None, None] * own_agg + far_agg)
    return (held_state, merged, own_decay * far_decay, own_prefix * (upper_half * far_decay + 1.0 - upper_half))

def reference(values, state_input, state_output, log_decay, level_lam, level_ids, upstream, final_upstream):
    bit_count = (N_GRP * N_SHARD).bit_length() - 1
    stretch_total = N_GRP * N_SHARD

    def forward(values32, state_input, state_output, log_decay, level_lam):
        stretch_values = values32.reshape(stretch_total, TOK_DEV, HEAD_TOTAL, HDIM)
        stretch_in = state_input.reshape(stretch_total, TOK_DEV, STATE)
        stretch_out = state_output.reshape(stretch_total, TOK_DEV, STATE)
        stretch_log = log_decay.reshape(stretch_total, TOK_DEV, HEAD_TOTAL)
        stretch_lam = level_lam.reshape(stretch_total, TOK_DEV, LEVELS * HEAD_TOTAL)

        def state_piece(pieces):
            return stretch_state(pieces[0], pieces[1], pieces[2])
        block_agg, block_decay = lax.map(jax.checkpoint(state_piece), (stretch_values, stretch_in, stretch_log))
        prefix = jnp.ones((stretch_total, HEAD_TOTAL), jnp.float32)
        stretch_index = jnp.arange(stretch_total, dtype=jnp.int32)
        held_list = []
        for bit_no in range(bit_count):
            half_span = 2 ** bit_no
            far_agg = jnp.flip(block_agg.reshape(stretch_total // (2 * half_span), 2, half_span, HEAD_TOTAL, STATE, HDIM), axis=1).reshape(block_agg.shape)
            far_decay = jnp.flip(block_decay.reshape(stretch_total // (2 * half_span), 2, half_span, HEAD_TOTAL), axis=1).reshape(block_decay.shape)
            upper_half = (stretch_index >> bit_no & 1).astype(jnp.float32)[:, None]
            held_state, block_agg, block_decay, prefix = level_merge(block_agg, block_decay, prefix, far_agg, far_decay, upper_half)
            held_list.append(held_state)
        level_states = jnp.stack(held_list, axis=1)
        final_state = lax.optimization_barrier(jnp.mean(block_agg, axis=0))

        def output_piece(pieces):
            piece_values, piece_in, piece_out, piece_log, piece_lam, piece_ids, piece_states = pieces
            weights = level_weights(piece_lam, piece_ids, bit_count)
            return intra_output(piece_values, piece_in, piece_out, piece_log) + inter_output(piece_out, piece_log, weights, piece_states)
        output = lax.map(jax.checkpoint(output_piece), (stretch_values, stretch_in, stretch_out, stretch_log, stretch_lam, level_ids, level_states))
        return (output.reshape(TOKEN_TOTAL, HEAD_TOTAL * HDIM), final_state)
    primal, pull = jax.vjp(forward, values.astype(jnp.float32), state_input, state_output, log_decay, level_lam)
    grads = pull((upstream.astype(jnp.float32), final_upstream))
    return (grads[0].astype(jnp.bfloat16), grads[1], grads[2], grads[3], grads[4])
```

```python
from functools import partial

import jax
import jax.numpy as jnp
from jax import lax
from jax.experimental import pallas as pl
from jax.experimental.pallas import tpu as pltpu
from jax.sharding import PartitionSpec as P

highest = lax.Precision.HIGHEST
MESH = pl.DeviceIdType.MESH
F32 = jnp.float32
BF16 = jnp.bfloat16
TOK = 128
VMEM_CAP = 48 * 1024 * 1024


def log2(n):
    return n.bit_length() - 1


def vmem():
    return pl.BlockSpec(memory_space=pltpu.VMEM)


def f32(*shape):
    return jax.ShapeDtypeStruct(shape, F32)


def iota(shape, dim):
    return lax.broadcasted_iota(jnp.int32, shape, dim)


def dot(a, b, **kw):
    return jnp.dot(a, b, preferred_element_type=F32, **kw)


def place():
    group = lax.axis_index("grp")
    me = lax.axis_index("shard")
    return group, me, me // 2, me % 2


def remote(src, dst, send, recv, device):
    return pltpu.make_async_remote_copy(
        src_ref=src, dst_ref=dst, send_sem=send, recv_sem=recv, device_id=device, device_id_type=MESH
    )


def loop(start, stop, fn):
    def step(i, carry):
        fn(i)
        return carry

    lax.fori_loop(start, stop, step, 0)


def enter(group, me, shards, groups):
    barrier = pltpu.get_barrier_semaphore()

    def greet_shard(d):
        pl.semaphore_signal(
            barrier, inc=1, device_id=(group, (me + d) % shards), device_id_type=MESH
        )

    def greet_group(d):
        pl.semaphore_signal(
            barrier, inc=1, device_id=((group + d) % groups, me), device_id_type=MESH
        )

    loop(1, shards, greet_shard)
    loop(1, groups, greet_group)
    pl.semaphore_wait(barrier, shards + groups - 2)


def offsets(chips):
    offs, at, n = [], 0, chips
    while n >= 1:
        offs.append(at)
        at += n
        n //= 2
    return offs


def high_level(group, far, bits):
    level = jnp.int32(0)
    for b in range(1, bits):
        level = jnp.where(group // 2**b != far // 2**b, jnp.int32(b), level)
    return level


def bit_of(x, b):
    return (x // 2**b) % 2 == 1


def state_kernel(v_ref, k_ref, ld_ref, blk_ref, crow_ref, ccol_ref):
    heads = ld_ref.shape[1]
    pairs = heads // 2
    ld = ld_ref[...]
    row = iota((TOK, TOK), 0)
    col = iota((TOK, TOK), 1)
    ccol = dot((row >= col).astype(F32), ld, precision=highest)
    ccol_ref[...] = ccol
    crow = ccol.T
    crow_ref[...] = crow
    last = jnp.broadcast_to(crow[:, TOK - 1 : TOK], (heads, TOK))
    tail = jnp.exp(last - crow)
    whole = jnp.exp(last)
    kt = k_ref[...].T
    half = (col < 64).astype(F32)
    m0 = half.astype(BF16)
    m1 = (1.0 - half).astype(BF16)
    for p in range(pairs):
        k2 = jnp.concatenate(
            [kt * tail[2 * p : 2 * p + 1], kt * tail[2 * p + 1 : 2 * p + 2]], axis=1
        ).astype(BF16)
        vp = v_ref[:, p * 128 : (p + 1) * 128]
        s = dot(k2, jnp.concatenate([vp * m0, vp * m1], axis=0))
        blk_ref[2 * p, 0:4] = s[0:32].reshape(4, 8, 128)
        blk_ref[2 * p + 1, 0:4] = s[32:64].reshape(4, 8, 128)
        dec = half[0:8] * whole[2 * p : 2 * p + 1] + (1.0 - half[0:8]) * whole[2 * p + 1 : 2 * p + 2]
        blk_ref[2 * p, 4] = dec
        blk_ref[2 * p + 1, 4] = dec


def forward_kernel(
    shards,
    groups,
    blk,
    h,
    sib,
    r1,
    nd,
    zb,
    hz,
    stage,
    pin,
    coef,
    sib_sem,
    a_sem,
    z_send,
    z_recv,
    h_send,
    h_recv,
    f_send,
    f_recv,
):
    chips = shards // 2
    nb, nz = log2(chips), log2(groups)
    group, me, chip, core = place()
    mate = me + 1 - 2 * core
    offs = offsets(chips)
    top = offs[nb]
    enter(group, me, shards, groups)

    sib_copy = remote(blk, sib, sib_sem.at[0], sib_sem.at[1], (group, mate))

    @pl.when(core == 0)
    def _():
        sib_copy.start()

    def scatter(d):
        to = (me + d) % shards
        remote(blk.at[to], r1.at[me], a_sem.at[0], a_sem.at[1], (group, to)).start()

    loop(1, shards, scatter)
    r1[me] = blk[me]
    part = r1.at[pl.ds(0, shards - 1)]
    whole = remote(part, part, a_sem.at[0], a_sem.at[1], (group, mate))
    whole.wait_recv()

    for c in range(chips):
        right = r1[2 * c + 1, 4]
        nd[c, 0:4] = right[None] * r1[2 * c, 0:4] + r1[2 * c + 1, 0:4]
        nd[c, 4] = right * r1[2 * c, 4]
    for b in range(1, nb + 1):
        for i in range(chips >> b):
            lo = offs[b - 1] + 2 * i
            right = nd[lo + 1, 4]
            nd[offs[b] + i, 0:4] = right[None] * nd[lo, 0:4] + nd[lo + 1, 0:4]
            nd[offs[b] + i, 4] = right * nd[lo, 4]

    def spread(d):
        to = (group + d) % groups
        remote(nd.at[top], zb.at[group], z_send.at[0], z_recv.at[group], (to, me)).start()

    loop(1, groups, spread)

    for c in range(chips):
        pre = None
        for b in range(nb):
            if (c >> b) & 1:
                left = offs[b] + (c >> b) - 1
                far = nd[left, 0:4]
                stage[c, b] = far if pre is None else pre[None] * far
                pre = nd[left, 4] if pre is None else pre * nd[left, 4]
        pin[c] = jnp.ones((8, 128), F32) if pre is None else pre

    def send_level(lev, to):
        remote(
            stage.at[to, lev],
            h.at[lev, chip, core],
            h_send.at[lev],
            h_recv.at[lev],
            (group, 2 * to + core),
        ).start()

    def send_low(d):
        to = (chip + d) % chips
        for b in range(nb):

            @pl.when(bit_of(to, b))
            def _():
                send_level(b, to)

    loop(1, chips, send_low)
    for b in range(nb):

        @pl.when(bit_of(chip, b))
        def _():
            h[b, chip, core] = stage[chip, b]

    coef[...] = jnp.ones((8, 128), F32)
    hz[...] = jnp.zeros(hz.shape, F32)
    for d in range(1, groups):
        far = group - d

        @pl.when(far >= 0)
        def _():
            slot = zb.at[far]
            remote(slot, slot, z_send.at[0], z_recv.at[far], (group, mate)).wait_recv()
            level = high_level(group, far, nz)
            hz[level] = hz[level] + coef[...][None] * zb[far, 0:4]
            coef[...] = coef[...] * zb[far, 4]

    def stage_high(c):
        for l in range(nz):

            @pl.when(bit_of(group, l))
            def _():
                stage[c, nb + l] = pin[c][None] * hz[l]

    loop(0, chips, stage_high)

    def send_high(d):
        to = (chip + d) % chips
        for l in range(nz):

            @pl.when(bit_of(group, l))
            def _():
                send_level(nb + l, to)

    loop(1, chips, send_high)

    for lev in range(nb + nz):
        mine = bit_of(chip, lev) if lev < nb else bit_of(group, lev - nb)

        @pl.when(mine)
        def _():
            if lev >= nb:
                h[lev, chip, core] = stage[chip, lev]
            arrive = h.at[lev, pl.ds(0, chips - 1), core]
            remote(arrive, arrive, h_send.at[lev], h_recv.at[lev], (group, mate)).wait_recv()
            ours = h.at[lev, :, core]
            remote(ours, ours, f_send.at[lev], f_recv.at[lev], (group, mate)).start()

    for lev in range(nb + nz):
        mine = bit_of(chip, lev) if lev < nb else bit_of(group, lev - nb)

        @pl.when(mine)
        def _():
            theirs = h.at[lev, :, 1 - core]
            ours = remote(theirs, theirs, f_send.at[lev], f_recv.at[lev], (group, mate))
            ours.wait_recv()
            ours.wait_send()

    def sent(lev, count):
        out = stage.at[pl.ds(0, count), lev]
        remote(out, out, h_send.at[lev], h_recv.at[lev], (group, mate)).wait_send()

    for b in range(nb):

        @pl.when(bit_of(chip, b))
        def _():
            if chips // 2 > 1:
                sent(b, chips // 2 - 1)

        @pl.when(jnp.logical_not(bit_of(chip, b)))
        def _():
            sent(b, chips // 2)

    for l in range(nz):

        @pl.when(bit_of(group, l))
        def _():
            sent(nb + l, chips - 1)

    for d in range(1, groups):
        far = group + d

        @pl.when(far < groups)
        def _():
            slot = zb.at[far]
            remote(slot, slot, z_send.at[0], z_recv.at[far], (group, mate)).wait_recv()

    zpart = zb.at[pl.ds(0, groups - 1)]
    remote(zpart, zpart, z_send.at[0], z_recv.at[0], (group, mate)).wait_send()
    whole.wait_send()

    @pl.when(core == 0)
    def _():
        sib_copy.wait_send()

    @pl.when(core == 1)
    def _():
        sib_copy.wait_recv()


def backward_kernel(
    shards,
    groups,
    g,
    r1,
    nd,
    zb,
    hz,
    fu,
    ds,
    g0,
    x,
    st,
    rb,
    u,
    zu,
    ct,
    cown,
    coef,
    dn,
    rt,
    out,
    g0_sem,
    x_send,
    x_recv,
    b_send,
    b_recv,
    z_send,
    z_recv,
    c_send,
    c_recv,
    o_sem,
):
    chips = shards // 2
    nb, nz = log2(chips), log2(groups)
    group, me, chip, core = place()
    mate = me + 1 - 2 * core
    offs = offsets(chips)
    top = offs[nb]
    enter(group, me, shards, groups)

    order = [nb + l for l in range(nz)] + list(range(nb))

    def mine(lev):
        return bit_of(chip, lev) if lev < nb else bit_of(group, lev - nb)

    def swap(lev):
        return remote(
            g.at[lev + 1, :, 1 - core], x.at[lev], x_send.at[lev], x_recv.at[lev], (group, mate)
        )

    for lev in order:

        @pl.when(mine(lev))
        def _():
            swap(lev).start()

    g0_copy = remote(g.at[0], g0, g0_sem.at[0], g0_sem.at[1], (group, mate))

    @pl.when(core == 1)
    def _():
        g0_copy.start()

    for lev in order:

        @pl.when(mine(lev))
        def _():
            swap(lev).wait_recv()

            def add(c):
                st[lev, c] = g[lev + 1, c, core] + x[lev, c]

            loop(0, chips, add)

            def send(d):
                to = (chip + d) % chips
                remote(
                    st.at[lev, to],
                    rb.at[lev, chip],
                    b_send.at[lev],
                    b_recv.at[lev],
                    (group, 2 * to + core),
                ).start()

            loop(1, chips, send)
            rb[lev, chip] = st[lev, chip]

    def arrived(lev, count):
        part = rb.at[lev, pl.ds(0, count)]
        remote(part, part, b_send.at[lev], b_recv.at[lev], (group, mate)).wait_recv()

    pres = []
    pin = []
    for c in range(chips):
        pre = None
        mid = []
        for b in range(nb):
            if (c >> b) & 1:
                mid.append((b, offs[b] + (c >> b) - 1))
        pres.append(mid)

    def pin_of(c):
        pre = None
        for _, left in pres[c]:
            pre = nd[left, 4] if pre is None else pre * nd[left, 4]
        return jnp.ones((8, 128), F32) if pre is None else pre

    rt[...] = jnp.zeros(rt.shape, F32)
    for l in range(nz):

        @pl.when(bit_of(group, l))
        def _():
            arrived(nb + l, chips - 1)
            total = jnp.zeros((4, 8, 128), F32)
            for c in range(chips):
                w = pin_of(c)[None] * rb[nb + l, c]
                total = total + w
                rt[c] = rt[c] + jnp.sum(w * hz[l], axis=0)
            u[l] = total

    for d in range(1, groups):

        @pl.when(group - d >= 0)
        def _():
            level = high_level(group, group - d, nz)
            remote(u.at[level], zu.at[group], z_send.at[d], z_recv.at[group], (group - d, me)).start()

    coef[...] = jnp.ones((8, 128), F32)
    dn[top] = jnp.zeros((4, 8, 128), F32)
    for d in range(1, groups):

        @pl.when(group + d < groups)
        def _():
            slot = zu.at[group + d]
            remote(slot, slot, z_send.at[d], z_recv.at[group + d], (group, mate)).wait_recv()
            dn[top] = dn[top] + coef[...][None] * zu[group + d]
            coef[...] = coef[...] * zb[group + d, 4]

    dn[top] = dn[top] + coef[...][None] * fu[...]
    cown[...] = jnp.sum(nd[top, 0:4] * dn[top], axis=0)
    for l in range(nz):

        @pl.when(bit_of(group, l))
        def _():
            cown[...] = cown[...] - jnp.sum(u[l] * hz[l], axis=0)

    for d in range(1, groups):

        @pl.when(group + d < groups)
        def _():
            remote(cown, ct.at[group], c_send.at[d], c_recv.at[group], (group + d, me)).start()

    for b in range(nb):

        @pl.when(bit_of(chip, b))
        def _():
            if chips // 2 > 1:
                arrived(b, chips // 2 - 1)

        @pl.when(jnp.logical_not(bit_of(chip, b)))
        def _():
            arrived(b, chips // 2)

    for b in range(nb):
        for i in range(0, chips >> b, 2):
            left = offs[b] + i
            total = None
            for c in range((i + 1) << b, (i + 2) << b):
                w = rb[b, c]
                for bb, node in pres[c]:
                    if bb < b:
                        w = nd[node, 4][None] * w
                rt[c] = rt[c] + jnp.sum(w * nd[left, 0:4], axis=0)
                total = w if total is None else total + w
            dn[left] = total
    for b in reversed(range(nb)):
        for i in range(0, chips >> b, 2):
            left = offs[b] + i
            parent = dn[offs[b + 1] + i // 2]
            dn[left] = dn[left] + nd[left + 1, 4][None] * parent
            dn[left + 1] = parent

    carry = jnp.zeros((8, 128), F32)
    for c in range(chips):
        right = dn[c]
        left = r1[2 * c + 1, 4][None] * right
        out[2 * c, 0:4] = left
        out[2 * c + 1, 0:4] = right
        l0 = jnp.sum(r1[2 * c, 0:4] * left, axis=0)
        l1 = jnp.sum(r1[2 * c + 1, 0:4] * right, axis=0)
        out[2 * c, 4] = carry
        odd = carry + l0 - rt[c]
        out[2 * c + 1, 4] = odd
        carry = odd + l1

    coef[...] = jnp.zeros((8, 128), F32)
    for d in range(1, groups):

        @pl.when(group - d >= 0)
        def _():
            slot = ct.at[group - d]
            remote(slot, slot, c_send.at[d], c_recv.at[group - d], (group, mate)).wait_recv()
            coef[...] = coef[...] + ct[group - d]

    def carry_in(s):
        out[s, 4] = out[s, 4] + coef[...]

    loop(0, shards, carry_in)

    def give(d):
        to = (me + d) % shards
        remote(out.at[to], ds.at[me], o_sem.at[0], o_sem.at[1], (group, to)).start()

    loop(1, shards, give)
    ds[me] = out[me]

    for lev in range(nb + nz):

        @pl.when(mine(lev))
        def _():
            swap(lev).wait_send()
            part = st.at[lev, pl.ds(0, chips - 1)]
            remote(part, part, b_send.at[lev], b_recv.at[lev], (group, mate)).wait_send()

    for d in range(1, groups):

        @pl.when(group - d >= 0)
        def _():
            remote(u.at[0], u.at[0], z_send.at[d], z_recv.at[0], (group, mate)).wait_send()

        @pl.when(group + d < groups)
        def _():
            remote(cown, cown, c_send.at[d], c_recv.at[0], (group, mate)).wait_send()

    @pl.when(core == 1)
    def _():
        g0_copy.wait_send()

    @pl.when(core == 0)
    def _():
        g0_copy.wait_recv()

    part = out.at[pl.ds(0, shards - 1)]
    rest = remote(part, part, o_sem.at[0], o_sem.at[1], (group, mate))
    rest.wait_send()
    rest.wait_recv()


def middle_kernel(
    nb,
    nz,
    ids_ref,
    v_ref,
    do_ref,
    k_ref,
    q_ref,
    lam_ref,
    crow_ref,
    ccol_ref,
    sib_ref,
    h_ref,
    dv_ref,
    dq_ref,
    dk_ref,
    dlam_ref,
    dlog_ref,
    g_ref,
    bd_t,
    bd,
    lam_t,
    dlam_t,
    rint,
    dq_acc,
    dsc,
):
    heads = ccol_ref.shape[1]
    pairs = heads // 2
    columns = lam_t.shape[0]
    group, me, chip, core = place()
    row = iota((TOK, TOK), 0)
    col = iota((TOK, TOK), 1)
    half = (col < 64).astype(F32)
    m0 = half.astype(BF16)
    m1 = (1.0 - half).astype(BF16)
    t0 = (row < 64).astype(F32).astype(BF16)
    t1 = (row >= 64).astype(F32).astype(BF16)
    crow = crow_ref[...]
    ccol = ccol_ref[...]
    growth = jnp.exp(crow)
    q = q_ref[...]
    k = k_ref[...]
    qt = q.T
    kt = k.T
    causal = row <= col
    scores = jnp.where(causal, dot(k, qt, precision=highest), 0.0)
    mid = ccol[TOK // 2 - 1 : TOK // 2, :]
    b_col = jnp.exp(mid - ccol)
    a_row = jnp.exp(crow - crow[:, TOK // 2 - 1 : TOK // 2])
    suffix = (row >= col).astype(F32).astype(BF16)
    before = row < col
    wide = min(128, columns * heads)
    n = wide // heads
    for j in range(columns // n):
        lam_t[pl.ds(j * n, n)] = lam_ref[:, j * wide : (j + 1) * wide].T.reshape(n, heads, TOK)
    dlam_t[...] = jnp.zeros(dlam_t.shape, F32)
    rint[...] = jnp.zeros(rint.shape, F32)
    dq_acc[...] = jnp.zeros(dq_acc.shape, F32)
    dsc[...] = jnp.zeros(dsc.shape, F32)

    for p in range(pairs):
        sl = slice(p * 128, (p + 1) * 128)
        dop = do_ref[:, sl]
        dot_t = dop.astype(F32).T.astype(BF16)
        bdt = jnp.concatenate([dot_t * t0, dot_t * t1], axis=1)
        bdo = jnp.concatenate([dop * m0, dop * m1], axis=0)
        bd_t[p] = bdt
        bd[p] = bdo
        dmix = dot(v_ref[:, sl], bdt)
        xs = []
        for j in range(2):
            head = 2 * p + j
            dm = dmix[:, j * 128 : (j + 1) * 128]
            e = jnp.where(causal, b_col[:, head : head + 1] * a_row[head : head + 1, :], 0.0)
            x = e * scores
            dsc[...] += e * dm
            y = dot((x * dm).astype(BF16), suffix)
            dlog_ref[head : head + 1, :] = jnp.sum(
                jnp.where(before, y, 0.0), axis=0, keepdims=True
            )
            xs.append(x.astype(BF16))
        dv_ref[:, sl] = dot(jnp.concatenate(xs, axis=1), bdo)

    q_low = q.astype(BF16).astype(F32).T
    q2 = jnp.concatenate([q_low, q_low], axis=1)

    for b in range(1 + nb + nz):
        if b == 0:
            mine = core == 1
        elif b <= nb:
            mine = bit_of(chip, b - 1)
        else:
            mine = bit_of(group, b - 1 - nb)

        @pl.when(mine)
        def _():
            lev = ids_ref[0, b]

            def pair_step(p):
                if b == 0:
                    held = sib_ref[pl.ds(2 * p, 2), 0:4].reshape(64, 128)
                    scale = None
                else:
                    scale = jnp.where(core == 1, sib_ref[2 * p, 4, 0:1], jnp.ones((1, 128), F32))
                    held = h_ref[b - 1, p].reshape(64, 128) * scale
                m = dot(held.astype(BF16), bd_t[p])
                lam2 = lam_t[lev, pl.ds(2 * p, 2), :]
                gr2 = jnp.exp(crow_ref[pl.ds(2 * p, 2), :])
                w2 = lam2 * gr2
                w = jnp.concatenate([w2[0:1], w2[1:2]], axis=1)
                gsum = jnp.sum(q2 * m, axis=0, keepdims=True)
                dq_acc[...] += w * m
                grad = dot((w * q2).astype(BF16), bd[p])
                if scale is not None:
                    grad = grad * scale
                g_ref[b, p] = grad.reshape(2, 4, 8, 128)
                g2 = jnp.concatenate([gsum[:, 0:128], gsum[:, 128:256]], axis=0)
                dlam_t[lev, pl.ds(2 * p, 2), :] += gr2 * g2
                rint[pl.ds(2 * p, 2), :] += w2 * g2

            loop(0, pairs, pair_step)

    r = rint[...]
    tri = (row >= col).astype(F32)
    own = jnp.where(core == 0, 1.0, 0.0)
    dlog_ref[...] += dot(r, tri, precision=highest) - own * jnp.sum(r, axis=1, keepdims=True)
    dqi = (dq_acc[:, 0:128] + dq_acc[:, 128:256]).astype(BF16).astype(F32)
    dst = dsc[...]
    dq_ref[...] = (dqi + dot(kt, dst, precision=highest)).T
    dk_ref[...] = dot(dst, q, precision=highest)
    for j in range(columns // n):
        dlam_ref[:, j * wide : (j + 1) * wide] = dlam_t[pl.ds(j * n, n)].reshape(wide, TOK).T


def end_kernel(
    v_ref, k_ref, ccol_ref, ds_ref, g0_ref, dvp_ref, dkp_ref, dlogp_ref, dv_ref, dk_ref, dlog_ref
):
    heads = ccol_ref.shape[1]
    pairs = heads // 2
    group, me, chip, core = place()
    row = iota((TOK, TOK), 0)
    col = iota((TOK, TOK), 1)
    left = col < 64
    ccol = ccol_ref[...]
    tail = jnp.exp(ccol[TOK - 1 : TOK, :] - ccol)
    k_low = k_ref[...].astype(BF16)
    even = core == 0
    dk = jnp.zeros((TOK, 64), F32)
    ls = jnp.zeros((TOK, heads), F32)
    dd = jnp.zeros((8, heads), F32)
    lane_row = iota((TOK, heads), 0)
    lane_col = iota((TOK, heads), 1)
    for p in range(pairs):
        sl = slice(p * 128, (p + 1) * 128)
        pick = (lane_col == 2 * p + lane_row // 64).astype(F32)
        grad = ds_ref[2 * p : 2 * p + 2, 0:4].reshape(64, 128)
        grad = grad + jnp.where(even, g0_ref[p].reshape(64, 128), 0.0)
        low = grad.astype(BF16)
        scale = jnp.where(left, tail[:, 2 * p : 2 * p + 1], tail[:, 2 * p + 1 : 2 * p + 2])
        vp = v_ref[:, sl].astype(F32)
        dvs = scale * dot(k_low, low)
        decayed = (scale * vp).astype(BF16)
        dk += lax.dot_general(
            decayed, low, (((1,), (1,)), ((), ())), preferred_element_type=F32
        )
        dv_ref[:, sl] = (dvp_ref[:, sl] + dvs).astype(BF16)
        ls += dot((vp * dvs).astype(BF16), pick.astype(BF16))
        dd += dot(ds_ref[2 * p, 4] + ds_ref[2 * p + 1, 4], pick, precision=highest)
    dk_ref[...] = dkp_ref[...] + dk
    strict = (row > col).astype(F32)
    dlog_ref[...] = (
        dlogp_ref[...].T
        + dot(strict, ls, precision=highest)
        + jnp.sum(dd, axis=0, keepdims=True)
    )


def body(
    values, state_input, state_output, log_decay, level_lam, level_ids, upstream, final_upstream
):
    shards, groups = lax.axis_size("shard"), lax.axis_size("grp")
    chips = shards // 2
    nb, nz = log2(chips), log2(groups)
    heads = log_decay.shape[1]
    columns = level_lam.shape[1] // heads
    me = lax.axis_index("shard")
    params = partial(pltpu.CompilerParams, vmem_limit_bytes=VMEM_CAP)

    blk, crow, ccol = pl.pallas_call(
        state_kernel,
        out_shape=(f32(shards, 5, 8, 128), f32(heads, TOK), f32(TOK, heads)),
        in_specs=[vmem()] * 3,
        out_specs=(vmem(),) * 3,
        compiler_params=params(),
        name="state",
    )(values, state_input, log_decay)

    dma = pltpu.SemaphoreType.DMA
    h, sib, r1, nd, zb, hz = pl.pallas_call(
        partial(forward_kernel, shards, groups),
        out_shape=(
            f32(nb + nz, chips, 2, 4, 8, 128),
            f32(shards, 5, 8, 128),
            f32(shards, 5, 8, 128),
            f32(2 * chips, 5, 8, 128),
            f32(groups, 5, 8, 128),
            f32(nz, 4, 8, 128),
        ),
        in_specs=[vmem()],
        out_specs=(vmem(),) * 6,
        scratch_shapes=[
            pltpu.VMEM((chips, nb + nz, 4, 8, 128), F32),
            pltpu.VMEM((chips, 8, 128), F32),
            pltpu.VMEM((8, 128), F32),
            dma((2,)),
            dma((2,)),
            dma((1,)),
            dma((groups,)),
            dma((nb + nz,)),
            dma((nb + nz,)),
            dma((nb + nz,)),
            dma((nb + nz,)),
        ],
        compiler_params=params(collective_id=0, has_side_effects=True),
        name="forward",
    )(blk)

    dv, dq, dk, dlam, dlog, g = pl.pallas_call(
        partial(middle_kernel, nb, nz),
        out_shape=(
            f32(TOK, heads * 64),
            f32(TOK, 64),
            f32(TOK, 64),
            f32(TOK, columns * heads),
            f32(heads, TOK),
            f32(1 + nb + nz, chips, 2, 4, 8, 128),
        ),
        in_specs=[pl.BlockSpec(memory_space=pltpu.SMEM)] + [vmem()] * 9,
        out_specs=(vmem(),) * 6,
        scratch_shapes=[
            pltpu.VMEM((chips, 128, 256), BF16),
            pltpu.VMEM((chips, 256, 128), BF16),
            pltpu.VMEM((columns, heads, TOK), F32),
            pltpu.VMEM((columns, heads, TOK), F32),
            pltpu.VMEM((heads, TOK), F32),
            pltpu.VMEM((64, 256), F32),
            pltpu.VMEM((TOK, TOK), F32),
        ],
        compiler_params=params(),
        name="middle",
    )(
        level_ids,
        values,
        upstream,
        state_input,
        state_output,
        level_lam,
        crow,
        ccol,
        sib,
        h,
    )

    final = final_upstream.reshape(chips, 2, 2, 32, 64)[me // 2, :, me % 2]
    final = final.transpose(1, 0, 2).reshape(4, 8, 128)
    ds, g0 = pl.pallas_call(
        partial(backward_kernel, shards, groups),
        out_shape=(f32(shards, 5, 8, 128), f32(chips, 2, 4, 8, 128)),
        in_specs=[vmem()] * 6,
        out_specs=(vmem(),) * 2,
        scratch_shapes=[
            pltpu.VMEM((nb + nz, chips, 4, 8, 128), F32),
            pltpu.VMEM((nb + nz, chips, 4, 8, 128), F32),
            pltpu.VMEM((nb + nz, chips, 4, 8, 128), F32),
            pltpu.VMEM((nz, 4, 8, 128), F32),
            pltpu.VMEM((groups, 4, 8, 128), F32),
            pltpu.VMEM((groups, 8, 128), F32),
            pltpu.VMEM((8, 128), F32),
            pltpu.VMEM((8, 128), F32),
            pltpu.VMEM((2 * chips, 4, 8, 128), F32),
            pltpu.VMEM((chips, 8, 128), F32),
            pltpu.VMEM((shards, 5, 8, 128), F32),
            dma((2,)),
            dma((nb + nz,)),
            dma((nb + nz,)),
            dma((nb + nz,)),
            dma((nb + nz,)),
            dma((groups,)),
            dma((groups,)),
            dma((groups,)),
            dma((groups,)),
            dma((2,)),
        ],
        compiler_params=params(collective_id=1, has_side_effects=True),
        name="backward",
    )(g, r1, nd, zb, hz, final)

    dv, dk, dlog = pl.pallas_call(
        end_kernel,
        out_shape=(
            jax.ShapeDtypeStruct((TOK, heads * 64), BF16),
            f32(TOK, 64),
            f32(TOK, heads),
        ),
        in_specs=[vmem()] * 8,
        out_specs=(vmem(),) * 3,
        compiler_params=params(),
        name="end",
    )(values, state_input, ccol, ds, g0, dv, dk, dlog)
    return (dv, dk, dq, dlog, dlam)


def solution(mesh):
    spec = P(("grp", "shard"), None)
    return jax.shard_map(
        body,
        mesh=mesh,
        in_specs=(spec,) * 7 + (P(),),
        out_specs=(spec,) * 5,
        check_vma=False,
    )
```

```python
from functools import partial

import jax
import jax.numpy as jnp
from jax import lax
from jax.experimental import pallas as pl
from jax.experimental.pallas import tpu as pltpu
from jax.sharding import PartitionSpec as P

highest = lax.Precision.HIGHEST
MESH = pl.DeviceIdType.MESH
F32 = jnp.float32
BF16 = jnp.bfloat16
TOK = 128
VMEM_CAP = 48 * 1024 * 1024


def log2(n):
    return n.bit_length() - 1


def vmem():
    return pl.BlockSpec(memory_space=pltpu.VMEM)


def f32(*shape):
    return jax.ShapeDtypeStruct(shape, F32)


def iota(shape, dim):
    return lax.broadcasted_iota(jnp.int32, shape, dim)


def dot(a, b, **kw):
    return jnp.dot(a, b, preferred_element_type=F32, **kw)


def place():
    group = lax.axis_index("grp")
    me = lax.axis_index("shard")
    return group, me, me // 2, me % 2


def remote(src, dst, send, recv, device):
    return pltpu.make_async_remote_copy(
        src_ref=src, dst_ref=dst, send_sem=send, recv_sem=recv, device_id=device, device_id_type=MESH
    )


def loop(start, stop, fn):
    def step(i, carry):
        fn(i)
        return carry

    lax.fori_loop(start, stop, step, 0)


def enter(group, me, chip, core, chips, groups):
    barrier = pltpu.get_barrier_semaphore()

    def greet(shard, grp):
        pl.semaphore_signal(barrier, inc=1, device_id=(grp, shard), device_id_type=MESH)

    loop(1, chips, lambda d: greet(2 * ((chip + d) % chips) + core, group))
    loop(1, groups, lambda d: greet(me, (group + d) % groups))
    greet(me + 1 - 2 * core, group)
    return lambda: pl.semaphore_wait(barrier, chips + groups - 1)


def offsets(chips):
    offs, at, n = [], 0, chips
    while n >= 1:
        offs.append(at)
        at += n
        n //= 2
    return offs


def high_level(group, far, bits):
    level = jnp.int32(0)
    for b in range(1, bits):
        level = jnp.where(group // 2**b != far // 2**b, jnp.int32(b), level)
    return level


def bit_of(x, b):
    return (x // 2**b) % 2 == 1


def main_kernel(
    shards,
    groups,
    ids_ref,
    v_any,
    do_any,
    kt_any,
    qt_any,
    ldt_any,
    lam_any,
    fu_any,
    dv_ref,
    dqt_ref,
    dkt_ref,
    dlam_ref,
    dlogt_ref,
    crow_ref,
    low_ref,
    dld_ref,
    v_ref,
    do_ref,
    kt_ref,
    qt_ref,
    ldt_ref,
    lam_ref,
    fu_ref,
    in_sem,
    bd_t,
    bd,
    lam_t,
    glam,
    rint,
    dq_acc,
    dsc,
    g,
    own,
    dec,
    sib,
    sibd,
    blk,
    nd,
    zb,
    hz,
    stage,
    pin,
    coef,
    h,
    x,
    st,
    rb,
    u,
    zu,
    ct,
    cown,
    dn,
    rt,
    out,
    ds,
    g0,
    s_sem,
    a_sem,
    z_send,
    z_recv,
    h_send,
    h_recv,
    f_send,
    f_recv,
    g0_sem,
    x_send,
    x_recv,
    b_send,
    b_recv,
    u_send,
    u_recv,
    c_send,
    c_recv,
    o_sem,
    w_sem,
):
    chips = shards // 2
    pairs = chips
    heads = shards
    nb, nz = log2(chips), log2(groups)
    levels = nb + nz
    columns = lam_t.shape[0]
    ydim = 2 ** ((nb + 1) // 2)
    xdim = chips // ydim
    group, me, chip, core = place()
    mate = me + 1 - 2 * core
    xpos, ypos = chip // ydim, chip % ydim
    offs = offsets(chips)
    top = offs[nb]
    wide = min(128, columns * heads)
    per = wide // heads

    def shifted(i):
        return ((xpos + i // ydim) % xdim) * ydim + (ypos + i % ydim) % ydim

    def mine(lev):
        return bit_of(chip, lev) if lev < nb else bit_of(group, lev - nb)

    def near(src, dst, send, recv):
        return remote(src, dst, send, recv, (group, mate))

    loads = [
        pltpu.make_async_copy(a, b, in_sem.at[i])
        for i, (a, b) in enumerate(
            [
                (ldt_any, ldt_ref),
                (kt_any, kt_ref),
                (v_any, v_ref),
                (do_any, do_ref),
                (qt_any, qt_ref),
                (lam_any, lam_ref),
                (fu_any.at[chip, :, core], fu_ref),
            ]
        )
    ]
    for c in loads:
        c.start()
    wait_entry = enter(group, me, chip, core, chips, groups)

    row = iota((TOK, TOK), 0)
    col = iota((TOK, TOK), 1)
    upto = (row <= col).astype(F32)
    half = (col < 64).astype(F32)
    m0 = half.astype(BF16)
    m1 = (1.0 - half).astype(BF16)
    loads[0].wait()
    crow = dot(ldt_ref[...], upto, precision=highest)
    crow_ref[...] = crow
    last = jnp.broadcast_to(crow[:, TOK - 1 : TOK], (heads, TOK))
    tail = jnp.exp(last - crow)
    full = jnp.exp(last)
    loads[1].wait()
    kt = kt_ref[...]
    loads[2].wait()
    for p in range(pairs):
        k2 = jnp.concatenate(
            [kt * tail[2 * p : 2 * p + 1], kt * tail[2 * p + 1 : 2 * p + 2]], axis=1
        ).astype(BF16)
        vp = v_ref[:, p * 128 : (p + 1) * 128]
        s = dot(k2, jnp.concatenate([vp * m0, vp * m1], axis=0))
        own[p] = s.reshape(2, 4, 8, 128)
        dec[p] = (
            half[0:8] * full[2 * p : 2 * p + 1] + (1.0 - half[0:8]) * full[2 * p + 1 : 2 * p + 2]
        )

    wait_entry()
    swap_half = near(own.at[:, 1 - core], sib.at[:, 1 - core], s_sem.at[0], s_sem.at[1])
    swap_dec = near(dec, sibd, s_sem.at[2], s_sem.at[3])
    rest = near(own.at[:, core], sib.at[:, core], s_sem.at[4], s_sem.at[5])
    swap_half.start()
    swap_dec.start()

    @pl.when(core == 0)
    def _():
        rest.start()

    swap_dec.wait_recv()
    swap_half.wait_recv()

    def merge_cores(p):
        a = own[p, core]
        b = sib[p, core]
        left = jnp.where(core == 0, a, b)
        right = jnp.where(core == 0, b, a)
        drow = jnp.where(core == 0, sibd[p], dec[p])
        blk[p, 0:4] = drow[None] * left + right
        blk[p, 4] = dec[p] * sibd[p]

    loop(0, pairs, merge_cores)

    def scatter(i):
        to = shifted(i)
        remote(
            blk.at[to], nd.at[chip], a_sem.at[0], a_sem.at[1], (group, 2 * to + core)
        ).start()

    loop(1, chips, scatter)
    nd[chip] = blk[chip]

    loads[3].wait()
    loads[4].wait()
    qt = qt_ref[...]
    q = qt.T
    k = kt.T
    ccol = crow.T
    causal = row <= col
    scores = jnp.where(causal, dot(k, qt, precision=highest), 0.0)
    b_col = jnp.exp(ccol[TOK // 2 - 1 : TOK // 2, :] - ccol)
    a_row = jnp.exp(crow - crow[:, TOK // 2 - 1 : TOK // 2])
    suffix = (row >= col).astype(F32).astype(BF16)
    before = row < col
    t0 = (row < 64).astype(F32).astype(BF16)
    t1 = (row >= 64).astype(F32).astype(BF16)
    dsc[...] = jnp.zeros(dsc.shape, F32)

    def inside(p):
        sl = slice(p * 128, (p + 1) * 128)
        dop = do_ref[:, sl]
        dot_t = dop.astype(F32).T.astype(BF16)
        bdt = jnp.concatenate([dot_t * t0, dot_t * t1], axis=1)
        bdo = jnp.concatenate([dop * m0, dop * m1], axis=0)
        bd_t[p] = bdt
        bd[p] = bdo
        dmix = dot(v_ref[:, sl], bdt)
        xs = []
        for j in range(2):
            head = 2 * p + j
            dm = dmix[:, j * 128 : (j + 1) * 128]
            e = jnp.where(causal, b_col[:, head : head + 1] * a_row[head : head + 1, :], 0.0)
            mix = e * scores
            dsc[...] += e * dm
            y = dot((mix * dm).astype(BF16), suffix)
            dlogt_ref[head : head + 1, :] = jnp.sum(
                jnp.where(before, y, 0.0), axis=0, keepdims=True
            )
            xs.append(mix.astype(BF16))
        dv_ref[:, sl] = dot(jnp.concatenate(xs, axis=1), bdo)

    for p in range(pairs // 2):
        inside(p)

    part = nd.at[pl.ds(0, chips - 1)]
    scattered = near(part, part, a_sem.at[0], a_sem.at[1])
    scattered.wait_recv()
    for b in range(1, nb + 1):
        for i in range(chips >> b):
            lo = offs[b - 1] + 2 * i
            right = nd[lo + 1, 4]
            nd[offs[b] + i, 0:4] = right[None] * nd[lo, 0:4] + nd[lo + 1, 0:4]
            nd[offs[b] + i, 4] = right * nd[lo, 4]

    def up(d):
        return remote(
            nd.at[top], zb.at[group], z_send.at[d], z_recv.at[group], (group + d, me)
        )

    def down(d):
        return remote(
            nd.at[top, 4], zb.at[group, 4], z_send.at[d], z_recv.at[group], (group - d, me)
        )

    for d in range(1, groups):

        @pl.when(group + d < groups)
        def _():
            up(d).start()

    for d in range(1, groups):

        @pl.when(group - d >= 0)
        def _():
            remote(
                nd.at[top, 4],
                zb.at[group, 4],
                z_send.at[groups + d],
                z_recv.at[group],
                (group - d, me),
            ).start()

    for c in range(chips):
        pre = None
        for b in range(nb):
            if (c >> b) & 1:
                left = offs[b] + (c >> b) - 1
                far = nd[left, 0:4]
                stage[c, b] = far if pre is None else pre[None] * far
                pre = nd[left, 4] if pre is None else pre * nd[left, 4]
        pin[c] = jnp.ones((8, 128), F32) if pre is None else pre

    def send_level(lev, to):
        remote(
            stage.at[to, lev],
            h.at[lev, chip, core],
            h_send.at[lev],
            h_recv.at[lev],
            (group, 2 * to + core),
        ).start()

    def send_low(i):
        to = shifted(i)
        for b in reversed(range(nb)):

            @pl.when(bit_of(to, b))
            def _():
                send_level(b, to)

    loop(1, chips, send_low)
    for b in range(nb):

        @pl.when(bit_of(chip, b))
        def _():
            h[b, chip, core] = stage[chip, b]

    for p in range(pairs // 2, pairs):
        inside(p)

    coef[...] = jnp.ones((8, 128), F32)
    hz[...] = jnp.zeros(hz.shape, F32)
    for d in range(1, groups):
        far = group - d

        @pl.when(far >= 0)
        def _():
            slot = zb.at[far]
            near(slot, slot, z_send.at[0], z_recv.at[far]).wait_recv()
            level = high_level(group, far, nz)
            hz[level] = hz[level] + coef[...][None] * zb[far, 0:4]
            coef[...] = coef[...] * zb[far, 4]

    for l in range(nz):

        @pl.when(bit_of(group, l))
        def _():
            def fill(c):
                stage[c, nb + l] = pin[c][None] * hz[l]

            loop(0, chips, fill)
            loop(1, chips, lambda i: send_level(nb + l, shifted(i)))
            h[nb + l, chip, core] = stage[chip, nb + l]

    q_low = qt.astype(BF16).astype(F32)
    q2 = jnp.concatenate([q_low, q_low], axis=1)
    loads[5].wait()
    for j in range(columns // per):
        lam_t[pl.ds(j * per, per)] = lam_ref[:, j * wide : (j + 1) * wide].T.reshape(
            per, heads, TOK
        )
    glam[...] = jnp.zeros(glam.shape, F32)
    rint[...] = jnp.zeros(rint.shape, F32)
    dq_acc[...] = jnp.zeros(dq_acc.shape, F32)
    ids = [ids_ref[0, b] for b in range(1 + levels)]

    def levels_step(group_levels, p):
        gr2 = jnp.exp(crow_ref[pl.ds(2 * p, 2), :])
        scale = jnp.where(core == 1, sibd[p, 0:1], jnp.ones((1, 128), F32))
        helds, ws = [], []
        for b in group_levels:
            if b == 0:
                held = sib[p].reshape(64, 128)
            else:
                held = jnp.where(mine(b - 1), h[b - 1, p].reshape(64, 128) * scale, 0.0)
            helds.append(held.astype(BF16))
            ws.append(lam_t[ids[b], pl.ds(2 * p, 2), :] * gr2)
        m = dot(jnp.concatenate(helds, axis=0), bd_t[p])
        wqs = []
        acc = dq_acc[...]
        r2 = rint[pl.ds(2 * p, 2), :]
        for i, b in enumerate(group_levels):
            mi = m[64 * i : 64 * (i + 1)]
            w = jnp.concatenate([ws[i][0:1], ws[i][1:2]], axis=1)
            gsum = jnp.sum(q2 * mi, axis=0, keepdims=True)
            acc = acc + w * mi
            wqs.append((w * q2).astype(BF16))
            g2 = jnp.concatenate([gsum[:, 0:128], gsum[:, 128:256]], axis=0)
            glam[b, pl.ds(2 * p, 2), :] = gr2 * g2
            r2 = r2 + ws[i] * g2
        dq_acc[...] = acc
        rint[pl.ds(2 * p, 2), :] = r2
        grad = dot(jnp.concatenate(wqs, axis=0), bd[p])
        for i, b in enumerate(group_levels):
            gi = grad[64 * i : 64 * (i + 1)]
            g[b, p] = (gi if b == 0 else gi * scale).reshape(2, 4, 8, 128)

    def levels_pass(group_levels):
        def two(i):
            levels_step(group_levels, 2 * i)
            levels_step(group_levels, 2 * i + 1)

        loop(0, pairs // 2, two)

    g0_copy = near(g.at[0], g0, g0_sem.at[0], g0_sem.at[1])

    @pl.when(core == 1)
    def _():
        rest.wait_recv()
        levels_pass([0])
        g0_copy.start()

    def swap(lev):
        return near(g.at[lev + 1, :, 1 - core], x.at[lev], x_send.at[lev], x_recv.at[lev])

    def fetch(levs):
        for lev in levs:

            @pl.when(mine(lev))
            def _():
                part = h.at[lev, pl.ds(0, chips - 1), core]
                near(part, part, h_send.at[lev], h_recv.at[lev]).wait_recv()
                ours = h.at[lev, :, core]
                near(ours, ours, f_send.at[lev], f_recv.at[lev]).start()

        for lev in levs:

            @pl.when(mine(lev))
            def _():
                theirs = h.at[lev, :, 1 - core]
                near(theirs, theirs, f_send.at[lev], f_recv.at[lev]).wait_recv()

    def give_back(levs):
        for lev in levs:

            @pl.when(mine(lev))
            def _():
                swap(lev).start()

        for lev in levs:

            @pl.when(mine(lev))
            def _():
                swap(lev).wait_recv()

                def add(c):
                    st[lev, c] = g[lev + 1, c, core] + x[lev, c]

                loop(0, chips, add)

                def send(i):
                    to = shifted(i)
                    remote(
                        st.at[lev, to],
                        rb.at[lev, chip],
                        b_send.at[lev],
                        b_recv.at[lev],
                        (group, 2 * to + core),
                    ).start()

                loop(1, chips, send)
                rb[lev, chip] = st[lev, chip]

    low = list(range(nb))
    high = list(range(nb, levels))
    fetch(low)
    levels_pass([b + 1 for b in low])
    give_back(low)
    fetch(high)

    @pl.when(group > 0)
    def _():
        levels_pass([b + 1 for b in high])

    give_back(high)

    for p in range(columns):
        total = jnp.zeros((heads, TOK), F32)
        for b in range(1 + levels):
            total = total + jnp.where(ids[b] == p, glam[b], 0.0)
        dlam_ref[p] = total
    r = rint[...]
    even = jnp.where(core == 0, 1.0, 0.0)
    dlogt_ref[...] += dot(r, (row >= col).astype(F32), precision=highest) - even * jnp.sum(
        r, axis=1, keepdims=True
    )
    dqi = (dq_acc[:, 0:128] + dq_acc[:, 128:256]).astype(BF16).astype(F32)
    dst = dsc[...]
    dqt_ref[...] = dqi + dot(kt, dst, precision=highest)
    dkt_ref[...] = dot(dst, q, precision=highest).T

    def arrived(lev, count):
        part = rb.at[lev, pl.ds(0, count)]
        near(part, part, b_send.at[lev], b_recv.at[lev]).wait_recv()

    lefts = [
        [(b, offs[b] + (c >> b) - 1) for b in range(nb) if (c >> b) & 1] for c in range(chips)
    ]
    rt[...] = jnp.zeros(rt.shape, F32)
    for l in range(nz):

        @pl.when(bit_of(group, l))
        def _():
            arrived(nb + l, chips - 1)
            total = jnp.zeros((4, 8, 128), F32)
            for c in range(chips):
                w = pin[c][None] * rb[nb + l, c]
                total = total + w
                rt[c] = rt[c] + jnp.sum(w * hz[l], axis=0)
            u[l] = total

    for d in range(1, groups):

        @pl.when(group - d >= 0)
        def _():
            level = high_level(group, group - d, nz)
            remote(
                u.at[level], zu.at[group], u_send.at[d], u_recv.at[group], (group - d, me)
            ).start()

    for b in range(nb):

        @pl.when(bit_of(chip, b))
        def _():
            if chips // 2 > 1:
                arrived(b, chips // 2 - 1)

        @pl.when(jnp.logical_not(bit_of(chip, b)))
        def _():
            arrived(b, chips // 2)

    for b in range(nb):
        for i in range(0, chips >> b, 2):
            left = offs[b] + i
            total = None
            for c in range((i + 1) << b, (i + 2) << b):
                w = rb[b, c]
                for bb, node in lefts[c]:
                    if bb < b:
                        w = nd[node, 4][None] * w
                rt[c] = rt[c] + jnp.sum(w * nd[left, 0:4], axis=0)
                total = w if total is None else total + w
            dn[left] = total

    coef[...] = jnp.ones((8, 128), F32)
    dn[top] = jnp.zeros((4, 8, 128), F32)
    for d in range(1, groups):

        @pl.when(group + d < groups)
        def _():
            far = zb.at[group + d, 4]
            near(far, far, z_send.at[0], z_recv.at[group + d]).wait_recv()
            slot = zu.at[group + d]
            near(slot, slot, u_send.at[d], u_recv.at[group + d]).wait_recv()
            dn[top] = dn[top] + coef[...][None] * zu[group + d]
            coef[...] = coef[...] * zb[group + d, 4]

    loads[6].wait()
    fu = jnp.concatenate([fu_ref[0], fu_ref[1]], axis=1).reshape(4, 8, 128)
    dn[top] = dn[top] + coef[...][None] * fu
    cown[...] = jnp.sum(nd[top, 0:4] * dn[top], axis=0)
    for l in range(nz):

        @pl.when(bit_of(group, l))
        def _():
            cown[...] = cown[...] - jnp.sum(u[l] * hz[l], axis=0)

    for d in range(1, groups):

        @pl.when(group + d < groups)
        def _():
            remote(cown, ct.at[group], c_send.at[d], c_recv.at[group], (group + d, me)).start()

    for b in reversed(range(nb)):
        for i in range(0, chips >> b, 2):
            left = offs[b] + i
            parent = dn[offs[b + 1] + i // 2]
            dn[left] = dn[left] + nd[left + 1, 4][None] * parent
            dn[left + 1] = parent

    carry = jnp.zeros((8, 128), F32)
    for c in range(chips):
        out[c, 0:4] = dn[c]
        out[c, 4] = carry
        carry = carry + jnp.sum(nd[c, 0:4] * dn[c], axis=0) - rt[c]
        out[c, 5] = carry

    coef[...] = jnp.zeros((8, 128), F32)
    for d in range(1, groups):

        @pl.when(group - d >= 0)
        def _():
            slot = ct.at[group - d]
            near(slot, slot, c_send.at[d], c_recv.at[group - d]).wait_recv()
            coef[...] = coef[...] + ct[group - d]

    def carry_in(c):
        out[c, 4:6] = out[c, 4:6] + coef[...][None]

    loop(0, chips, carry_in)

    def give(i):
        to = shifted(i)
        remote(
            out.at[to], ds.at[chip, core], o_sem.at[0], o_sem.at[1], (group, 2 * to + core)
        ).start()

    loop(1, chips, give)
    ds[chip, core] = out[chip]
    part = ds.at[pl.ds(0, chips - 1), core]
    given = near(part, part, o_sem.at[0], o_sem.at[1])
    given.wait_recv()
    ours = ds.at[:, core]
    near(ours, ours, w_sem.at[0], w_sem.at[1]).start()

    def sent(lev, count):
        left = stage.at[pl.ds(0, count), lev]
        near(left, left, h_send.at[lev], h_recv.at[lev]).wait_send()

    for lev in range(levels):

        @pl.when(mine(lev))
        def _():
            ours = h.at[lev, :, core]
            near(ours, ours, f_send.at[lev], f_recv.at[lev]).wait_send()
            swap(lev).wait_send()
            part = st.at[lev, pl.ds(0, chips - 1)]
            near(part, part, b_send.at[lev], b_recv.at[lev]).wait_send()
            if lev >= nb:
                sent(lev, chips - 1)
            elif chips // 2 > 1:
                sent(lev, chips // 2 - 1)

        if lev < nb:

            @pl.when(jnp.logical_not(mine(lev)))
            def _():
                sent(lev, chips // 2)

    for d in range(1, groups):

        @pl.when(group + d < groups)
        def _():
            up(d).wait_send()
            near(cown, cown, c_send.at[d], c_recv.at[0]).wait_send()

        @pl.when(group - d >= 0)
        def _():
            line = nd.at[top, 4]
            near(line, line, z_send.at[groups + d], z_recv.at[0]).wait_send()
            near(u.at[0], u.at[0], u_send.at[d], u_recv.at[0]).wait_send()

    swap_half.wait_send()
    swap_dec.wait_send()
    scattered.wait_send()

    @pl.when(core == 1)
    def _():
        g0_copy.wait_send()

    @pl.when(core == 0)
    def _():
        rest.wait_send()
        g0_copy.wait_recv()

    given.wait_send()
    theirs = ds.at[:, 1 - core]
    both = near(theirs, theirs, w_sem.at[0], w_sem.at[1])
    both.wait_recv()
    both.wait_send()

    def finish(p):
        grad = ds[p, :, 0:4]
        dot_own = jnp.sum(own[p] * grad, axis=1)
        dld = jnp.where(core == 0, ds[p, :, 4], ds[p, :, 5] - dot_own)
        dld_ref[p] = dld[0] + dld[1]
        scale = jnp.where(core == 0, sibd[p], jnp.ones((8, 128), F32))
        extra = jnp.where(core == 0, g0[p], 0.0)
        low_ref[p] = (grad * scale[None, None] + extra).reshape(64, 128).astype(BF16)

    loop(0, pairs, finish)


def end_kernel(
    v_ref,
    kt_ref,
    crow_ref,
    low_ref,
    dld_ref,
    dvp_ref,
    dkp_ref,
    dlogp_ref,
    dqp_ref,
    dlamp_ref,
    dv_ref,
    dk_ref,
    dq_ref,
    dlog_ref,
    dlam_ref,
):
    heads = crow_ref.shape[0]
    pairs = heads // 2
    columns = dlamp_ref.shape[0]
    row = iota((TOK, TOK), 0)
    col = iota((TOK, TOK), 1)
    left = col < 64
    ccol = crow_ref[...].T
    tail = jnp.exp(ccol[TOK - 1 : TOK, :] - ccol)
    k_low = kt_ref[...].T.astype(BF16)
    dk = jnp.zeros((64, TOK), F32)
    ls = jnp.zeros((TOK, heads), F32)
    dd = jnp.zeros((8, heads), F32)
    lane_row = iota((TOK, heads), 0)
    lane_col = iota((TOK, heads), 1)
    for p in range(pairs):
        sl = slice(p * 128, (p + 1) * 128)
        pick = (lane_col == 2 * p + lane_row // 64).astype(F32)
        low = low_ref[p]
        scale = jnp.where(left, tail[:, 2 * p : 2 * p + 1], tail[:, 2 * p + 1 : 2 * p + 2])
        vp = v_ref[:, sl].astype(F32)
        dvs = scale * dot(k_low, low)
        decayed = (scale * vp).astype(BF16)
        dk += lax.dot_general(
            low, decayed, (((1,), (1,)), ((), ())), preferred_element_type=F32
        )
        dv_ref[:, sl] = (dvp_ref[:, sl] + dvs).astype(BF16)
        ls += dot((vp * dvs).astype(BF16), pick.astype(BF16))
        dd += dot(dld_ref[p], pick, precision=highest)
    dk_ref[...] = dkp_ref[...] + dk
    dq_ref[...] = dqp_ref[...]
    strict = (row > col).astype(F32)
    dlog_ref[...] = dlogp_ref[...] + (
        dot(strict, ls, precision=highest) + jnp.sum(dd, axis=0, keepdims=True)
    ).T
    wide = min(128, columns * heads)
    per = wide // heads
    for j in range(columns // per):
        dlam_ref[:, j * wide : (j + 1) * wide] = (
            dlamp_ref[pl.ds(j * per, per)].reshape(wide, TOK).T
        )


def body(
    values, state_input, state_output, log_decay, level_lam, level_ids, upstream, final_upstream
):
    shards, groups = lax.axis_size("shard"), lax.axis_size("grp")
    chips = shards // 2
    nb, nz = log2(chips), log2(groups)
    levels = nb + nz
    heads = log_decay.shape[1]
    columns = level_lam.shape[1] // heads
    params = partial(pltpu.CompilerParams, vmem_limit_bytes=VMEM_CAP)
    dma = pltpu.SemaphoreType.DMA
    tile = (4, 8, 128)
    kt = state_input.T

    dv, dqt, dkt, dlam, dlogt, crow, low, dld = pl.pallas_call(
        partial(main_kernel, shards, groups),
        out_shape=(
            f32(TOK, heads * 64),
            f32(64, TOK),
            f32(64, TOK),
            f32(columns, heads, TOK),
            f32(heads, TOK),
            f32(heads, TOK),
            jax.ShapeDtypeStruct((chips, 64, 128), BF16),
            f32(chips, 8, 128),
        ),
        in_specs=[pl.BlockSpec(memory_space=pltpu.SMEM)]
        + [pl.BlockSpec(memory_space=pl.ANY)] * 7,
        out_specs=(vmem(),) * 8,
        scratch_shapes=[
            pltpu.VMEM((TOK, heads * 64), BF16),
            pltpu.VMEM((TOK, heads * 64), BF16),
            pltpu.VMEM((64, TOK), F32),
            pltpu.VMEM((64, TOK), F32),
            pltpu.VMEM((heads, TOK), F32),
            pltpu.VMEM((TOK, columns * heads), F32),
            pltpu.VMEM((2, 32, 64), F32),
            dma((7,)),
            pltpu.VMEM((chips, 128, 256), BF16),
            pltpu.VMEM((chips, 256, 128), BF16),
            pltpu.VMEM((columns, heads, TOK), F32),
            pltpu.VMEM((1 + levels, heads, TOK), F32),
            pltpu.VMEM((heads, TOK), F32),
            pltpu.VMEM((64, 256), F32),
            pltpu.VMEM((TOK, TOK), F32),
            pltpu.VMEM((1 + levels, chips, 2) + tile, F32),
            pltpu.VMEM((chips, 2) + tile, F32),
            pltpu.VMEM((chips, 8, 128), F32),
            pltpu.VMEM((chips, 2) + tile, F32),
            pltpu.VMEM((chips, 8, 128), F32),
            pltpu.VMEM((chips, 5, 8, 128), F32),
            pltpu.VMEM((2 * chips, 5, 8, 128), F32),
            pltpu.VMEM((groups, 5, 8, 128), F32),
            pltpu.VMEM((nz,) + tile, F32),
            pltpu.VMEM((chips, levels) + tile, F32),
            pltpu.VMEM((chips, 8, 128), F32),
            pltpu.VMEM((8, 128), F32),
            pltpu.VMEM((levels, chips, 2) + tile, F32),
            pltpu.VMEM((levels, chips) + tile, F32),
            pltpu.VMEM((levels, chips) + tile, F32),
            pltpu.VMEM((levels, chips) + tile, F32),
            pltpu.VMEM((nz,) + tile, F32),
            pltpu.VMEM((groups,) + tile, F32),
            pltpu.VMEM((groups, 8, 128), F32),
            pltpu.VMEM((8, 128), F32),
            pltpu.VMEM((2 * chips,) + tile, F32),
            pltpu.VMEM((chips, 8, 128), F32),
            pltpu.VMEM((chips, 6, 8, 128), F32),
            pltpu.VMEM((chips, 2, 6, 8, 128), F32),
            pltpu.VMEM((chips, 2) + tile, F32),
            dma((6,)),
            dma((2,)),
            dma((2 * groups,)),
            dma((groups,)),
            dma((levels,)),
            dma((levels,)),
            dma((levels,)),
            dma((levels,)),
            dma((2,)),
            dma((levels,)),
            dma((levels,)),
            dma((levels,)),
            dma((levels,)),
            dma((groups,)),
            dma((groups,)),
            dma((groups,)),
            dma((groups,)),
            dma((2,)),
            dma((2,)),
        ],
        compiler_params=params(collective_id=0, has_side_effects=True),
        name="main",
    )(
        level_ids,
        values,
        upstream,
        kt,
        state_output.T,
        log_decay.T,
        level_lam,
        final_upstream.reshape(chips, 2, 2, 32, 64),
    )

    dv, dk, dq, dlog, dlam = pl.pallas_call(
        end_kernel,
        out_shape=(
            jax.ShapeDtypeStruct((TOK, heads * 64), BF16),
            f32(64, TOK),
            f32(64, TOK),
            f32(heads, TOK),
            f32(TOK, columns * heads),
        ),
        in_specs=[vmem()] * 10,
        out_specs=(vmem(),) * 5,
        compiler_params=params(),
        name="end",
    )(values, kt, crow, low, dld, dv, dkt, dlogt, dqt, dlam)
    return (dv, dk.T, dq.T, dlog.T, dlam)


def solution(mesh):
    spec = P(("grp", "shard"), None)
    return jax.shard_map(
        body,
        mesh=mesh,
        in_specs=(spec,) * 7 + (P(),),
        out_specs=(spec,) * 5,
        check_vma=False,
    )
```

```python
from functools import partial

import jax
import jax.numpy as jnp
from jax import lax
from jax.experimental import pallas as pl
from jax.experimental.pallas import tpu as pltpu
from jax.sharding import PartitionSpec as P

highest = lax.Precision.HIGHEST
MESH = pl.DeviceIdType.MESH
F32 = jnp.float32
BF16 = jnp.bfloat16
TOK = 128
VMEM_CAP = 48 * 1024 * 1024


def log2(n):
    return n.bit_length() - 1


def vmem():
    return pl.BlockSpec(memory_space=pltpu.VMEM)


def f32(*shape):
    return jax.ShapeDtypeStruct(shape, F32)


def iota(shape, dim):
    return lax.broadcasted_iota(jnp.int32, shape, dim)


def dot(a, b, **kw):
    return jnp.dot(a, b, preferred_element_type=F32, **kw)


def place():
    group = lax.axis_index("grp")
    me = lax.axis_index("shard")
    return group, me, me // 2, me % 2


def remote(src, dst, send, recv, device):
    return pltpu.make_async_remote_copy(
        src_ref=src, dst_ref=dst, send_sem=send, recv_sem=recv, device_id=device, device_id_type=MESH
    )


def loop(start, stop, fn):
    def step(i, carry):
        fn(i)
        return carry

    lax.fori_loop(start, stop, step, 0)


def enter(group, me, chip, core, chips, groups):
    barrier = pltpu.get_barrier_semaphore()

    def greet(shard, grp):
        pl.semaphore_signal(barrier, inc=1, device_id=(grp, shard), device_id_type=MESH)

    loop(1, chips, lambda d: greet(2 * ((chip + d) % chips) + core, group))
    loop(1, groups, lambda d: greet(me, (group + d) % groups))
    greet(me + 1 - 2 * core, group)
    return lambda: pl.semaphore_wait(barrier, chips + groups - 1)


def offsets(chips):
    offs, at, n = [], 0, chips
    while n >= 1:
        offs.append(at)
        at += n
        n //= 2
    return offs


def high_level(group, far, bits):
    level = jnp.int32(0)
    for b in range(1, bits):
        level = jnp.where(group // 2**b != far // 2**b, jnp.int32(b), level)
    return level


def bit_of(x, b):
    return (x // 2**b) % 2 == 1


def routes_of(nb, nz, xdim, ydim):
    routes, slot = [], 0
    for lev in range(nb + nz):
        ybits = log2(ydim)
        rows_first = lev < ybits or lev == nb
        first, second = (xdim, ydim) if rows_first else (ydim, xdim)
        if lev < nb:
            bit = lev if rows_first else lev - ybits
            users = [s for s in range(second) if (s >> bit) & 1]
            arrays = [[s for s in users if s >> (bit + 1) == a] for a in range(second >> (bit + 1))]
        else:
            users = list(range(second))
            arrays = [users]
        routes.append((rows_first, first, second, users, arrays, slot))
        slot += len(arrays)
    return routes


def main_kernel(
    shards,
    groups,
    ids_ref,
    v_any,
    do_any,
    kt_any,
    qt_any,
    ldt_any,
    lam_any,
    fu_any,
    dv_ref,
    dqt_ref,
    dkt_ref,
    dlam_ref,
    dlogt_ref,
    crow_ref,
    low_ref,
    dld_ref,
    v_ref,
    do_ref,
    kt_ref,
    qt_ref,
    ldt_ref,
    lam_ref,
    fu_ref,
    in_sem,
    bd_t,
    bd,
    lam_t,
    glam,
    rint,
    rnear,
    dq_acc,
    dsc,
    g,
    gn,
    own,
    dec,
    sib,
    sibd,
    blk,
    nd,
    zb,
    hz,
    pks,
    pk,
    coef,
    ring,
    h,
    x,
    st,
    back,
    q_sum,
    parts,
    rs,
    rr,
    u,
    zu,
    ct,
    cown,
    dn,
    carry_out,
    carry_in,
    ds,
    g0,
    s_sem,
    a_sem,
    z_send,
    z_recv,
    k_sem,
    r_send,
    r_recv,
    h_send,
    h_recv,
    f_send,
    f_recv,
    g0_sem,
    x_send,
    x_recv,
    b_send,
    b_recv,
    q_send,
    q_recv,
    t_sem,
    u_send,
    u_recv,
    c_send,
    c_recv,
    o_sem,
    w_sem,
):
    chips = shards // 2
    pairs = chips
    heads = shards
    nb, nz = log2(chips), log2(groups)
    levels = nb + nz
    columns = lam_t.shape[0]
    ydim = 2 ** ((nb + 1) // 2)
    xdim = chips // ydim
    group, me, chip, core = place()
    mate = me + 1 - 2 * core
    xpos, ypos = chip // ydim, chip % ydim
    offs = offsets(chips)
    top = offs[nb]
    wide = min(128, columns * heads)
    per = wide // heads

    routes = routes_of(nb, nz, xdim, ydim)

    def shifted(i):
        return ((xpos + i // ydim) % xdim) * ydim + (ypos + i % ydim) % ydim

    def near(src, dst, send, recv):
        return remote(src, dst, send, recv, (group, mate))

    loads = [
        pltpu.make_async_copy(a, b, in_sem.at[i])
        for i, (a, b) in enumerate(
            [
                (ldt_any, ldt_ref),
                (kt_any, kt_ref),
                (v_any, v_ref),
                (do_any, do_ref),
                (qt_any, qt_ref),
                (lam_any, lam_ref),
                (fu_any.at[chip, :, core], fu_ref),
            ]
        )
    ]
    for c in loads:
        c.start()
    wait_entry = enter(group, me, chip, core, chips, groups)

    row = iota((TOK, TOK), 0)
    col = iota((TOK, TOK), 1)
    upto = (row <= col).astype(F32)
    half = (col < 64).astype(F32)
    m0 = half.astype(BF16)
    m1 = (1.0 - half).astype(BF16)
    loads[0].wait()
    crow = dot(ldt_ref[...], upto, precision=highest)
    crow_ref[...] = crow
    last = jnp.broadcast_to(crow[:, TOK - 1 : TOK], (heads, TOK))
    tail = jnp.exp(last - crow)
    full = jnp.exp(last)
    loads[1].wait()
    kt = kt_ref[...]
    loads[2].wait()
    for p in range(pairs):
        k2 = jnp.concatenate(
            [kt * tail[2 * p : 2 * p + 1], kt * tail[2 * p + 1 : 2 * p + 2]], axis=1
        ).astype(BF16)
        vp = v_ref[:, p * 128 : (p + 1) * 128]
        s = dot(k2, jnp.concatenate([vp * m0, vp * m1], axis=0))
        own[p] = s.reshape(2, 4, 8, 128)
        dec[p] = (
            half[0:8] * full[2 * p : 2 * p + 1] + (1.0 - half[0:8]) * full[2 * p + 1 : 2 * p + 2]
        )

    wait_entry()
    swap_half = near(own.at[:, 1 - core], sib.at[:, 1 - core], s_sem.at[0], s_sem.at[1])
    swap_dec = near(dec, sibd, s_sem.at[2], s_sem.at[3])
    rest = near(own.at[:, core], sib.at[:, core], s_sem.at[4], s_sem.at[5])
    swap_half.start()
    swap_dec.start()

    @pl.when(core == 0)
    def _():
        rest.start()

    swap_dec.wait_recv()
    swap_half.wait_recv()

    def merge_cores(p):
        a = own[p, core]
        b = sib[p, core]
        left = jnp.where(core == 0, a, b)
        right = jnp.where(core == 0, b, a)
        drow = jnp.where(core == 0, sibd[p], dec[p])
        blk[p, 0:4] = drow[None] * left + right
        blk[p, 4] = dec[p] * sibd[p]

    loop(0, pairs, merge_cores)

    def scatter(i):
        to = shifted(i)
        remote(
            blk.at[to], nd.at[chip], a_sem.at[0], a_sem.at[1], (group, 2 * to + core)
        ).start()

    loop(1, chips, scatter)
    nd[chip] = blk[chip]

    loads[3].wait()
    loads[4].wait()
    qt = qt_ref[...]
    q = qt.T
    k = kt.T
    ccol = crow.T
    causal = row <= col
    scores = jnp.where(causal, dot(k, qt, precision=highest), 0.0)
    b_col = jnp.exp(ccol[TOK // 2 - 1 : TOK // 2, :] - ccol)
    a_row = jnp.exp(crow - crow[:, TOK // 2 - 1 : TOK // 2])
    suffix = (row >= col).astype(F32).astype(BF16)
    before = row < col
    t0 = (row < 64).astype(F32).astype(BF16)
    t1 = (row >= 64).astype(F32).astype(BF16)
    dsc[...] = jnp.zeros(dsc.shape, F32)

    def inside(p):
        sl = slice(p * 128, (p + 1) * 128)
        dop = do_ref[:, sl]
        dot_t = dop.astype(F32).T.astype(BF16)
        bdt = jnp.concatenate([dot_t * t0, dot_t * t1], axis=1)
        bdo = jnp.concatenate([dop * m0, dop * m1], axis=0)
        bd_t[p] = bdt
        bd[p] = bdo
        dmix = dot(v_ref[:, sl], bdt)
        xs = []
        for j in range(2):
            head = 2 * p + j
            dm = dmix[:, j * 128 : (j + 1) * 128]
            e = jnp.where(causal, b_col[:, head : head + 1] * a_row[head : head + 1, :], 0.0)
            mix = e * scores
            dsc[...] += e * dm
            y = dot((mix * dm).astype(BF16), suffix)
            dlogt_ref[head : head + 1, :] = jnp.sum(
                jnp.where(before, y, 0.0), axis=0, keepdims=True
            )
            xs.append(mix.astype(BF16))
        dv_ref[:, sl] = dot(jnp.concatenate(xs, axis=1), bdo)

    for p in range(pairs // 2):
        inside(p)

    part = nd.at[pl.ds(0, chips - 1)]
    scattered = near(part, part, a_sem.at[0], a_sem.at[1])
    scattered.wait_recv()
    for b in range(1, nb + 1):
        for i in range(chips >> b):
            lo = offs[b - 1] + 2 * i
            right = nd[lo + 1, 4]
            nd[offs[b] + i, 0:4] = right[None] * nd[lo, 0:4] + nd[lo + 1, 0:4]
            nd[offs[b] + i, 4] = right * nd[lo, 4]

    def up(d):
        return remote(
            nd.at[top], zb.at[group], z_send.at[d], z_recv.at[group], (group + d, me)
        )

    def down(d):
        return remote(
            nd.at[top, 4], zb.at[group, 4], z_send.at[d], z_recv.at[group], (group - d, me)
        )

    for d in range(1, groups):

        @pl.when(group + d < groups)
        def _():
            up(d).start()

    for d in range(1, groups):

        @pl.when(group - d >= 0)
        def _():
            remote(
                nd.at[top, 4],
                zb.at[group, 4],
                z_send.at[groups + d],
                z_recv.at[group],
                (group - d, me),
            ).start()

    sub = iota((8, 128), 0)
    for c in range(chips):
        pre = jnp.ones((8, 128), F32)
        rows = pre
        for b in range(nb):
            rows = jnp.where(sub >= b, pre, rows)
            if (c >> b) & 1:
                pre = pre * nd[offs[b] + (c >> b) - 1, 4]
        pks[c] = jnp.where(sub >= nb, pre, rows)

    def send_scales(i):
        to = shifted(i)
        remote(
            pks.at[to], pk.at[chip], k_sem.at[0], k_sem.at[1], (group, 2 * to + core)
        ).start()

    loop(1, chips, send_scales)
    pk[chip] = pks[chip]

    def where_on(lev):
        rows_first, first, second, users, arrays, slot = routes[lev]
        if rows_first:
            return xpos, ypos, lambda f, s: f * ydim + s
        return ypos, xpos, lambda f, s: s * ydim + f

    def reads(lev):
        if lev >= nb:
            return bit_of(group, lev - nb)
        return bit_of(chip, lev)

    def when_level(lev, fn):
        if lev >= nb:
            pl.when(bit_of(group, lev - nb))(fn)
        else:
            fn()

    def first_phase(lev):
        rows_first, first, second, users, arrays, slot = routes[lev]
        fpos, spos, at = where_on(lev)

        def source(a, f):
            if lev >= nb:
                return hz.at[lev - nb]
            if rows_first:
                return nd.at[offs[lev] + f * (ydim >> lev) + 2 * a, 0:4]
            return nd.at[offs[lev] + 2 * a, 0:4]

        def go():
            for d in range(1, first):
                f = (fpos + d) % first
                for a in range(len(arrays)):
                    remote(
                        source(a, f),
                        ring.at[slot + a, fpos],
                        r_send.at[slot + a],
                        r_recv.at[slot + a],
                        (group, 2 * at(f, spos) + core),
                    ).start()
            for a in range(len(arrays)):
                ring[slot + a, fpos] = source(a, fpos)[...]

        when_level(lev, go)

    def second_phase(lev):
        rows_first, first, second, users, arrays, slot = routes[lev]
        fpos, spos, at = where_on(lev)

        def go():
            if first > 1:
                for a in range(len(arrays)):
                    part = ring.at[slot + a, pl.ds(0, first - 1)]
                    near(part, part, r_send.at[slot + a], r_recv.at[slot + a]).wait_recv()
            for a, readers in enumerate(arrays):
                for s in readers:
                    there = h.at[lev, core, pl.ds(spos * first, first)]

                    @pl.when(spos != s)
                    def _():
                        remote(
                            ring.at[slot + a, pl.ds(0, first)],
                            there,
                            h_send.at[lev],
                            h_recv.at[lev],
                            (group, 2 * at(fpos, s) + core),
                        ).start()

                    @pl.when(spos == s)
                    def _():
                        there[...] = ring[slot + a, 0:first]

        when_level(lev, go)

    low = list(range(nb))
    high = list(range(nb, levels))
    for lev in low:
        first_phase(lev)

    for p in range(pairs // 2, 3 * pairs // 4):
        inside(p)
    for lev in low:
        second_phase(lev)
    for p in range(3 * pairs // 4, pairs):
        inside(p)

    coef[...] = jnp.ones((8, 128), F32)
    hz[...] = jnp.zeros(hz.shape, F32)
    for d in range(1, groups):
        far = group - d

        @pl.when(far >= 0)
        def _():
            slot = zb.at[far]
            near(slot, slot, z_send.at[0], z_recv.at[far]).wait_recv()
            level = high_level(group, far, nz)
            hz[level] = hz[level] + coef[...][None] * zb[far, 0:4]
            coef[...] = coef[...] * zb[far, 4]

    for lev in high:
        first_phase(lev)

    q_low = qt.astype(BF16).astype(F32)
    q2 = jnp.concatenate([q_low, q_low], axis=1)
    loads[5].wait()
    for j in range(columns // per):
        lam_t[pl.ds(j * per, per)] = lam_ref[:, j * wide : (j + 1) * wide].T.reshape(
            per, heads, TOK
        )
    glam[...] = jnp.zeros(glam.shape, F32)
    rint[...] = jnp.zeros(rint.shape, F32)
    rnear[...] = jnp.zeros(rnear.shape, F32)
    dq_acc[...] = jnp.zeros(dq_acc.shape, F32)
    ids = [ids_ref[0, b] for b in range(1 + levels)]

    def spot(lev, p):
        if routes[lev][0]:
            return (p % ydim) * xdim + p // ydim
        return p

    def levels_step(group_levels, p):
        gr2 = jnp.exp(crow_ref[pl.ds(2 * p, 2), :])
        mate_scale = jnp.where(core == 1, sibd[p, 0:1], jnp.ones((1, 128), F32))
        helds, ws, scales = [], [], []
        for b in group_levels:
            if b == 0:
                held = sib[p].reshape(64, 128)
                scales.append(None)
            else:
                scales.append(mate_scale * pk[p, b - 1 : b])
                at = spot(b - 1, p)
                held = jnp.concatenate([h[b - 1, 0, at], h[b - 1, 1, at]], axis=0)
                held = jnp.where(reads(b - 1), held.reshape(64, 128) * scales[-1], 0.0)
            helds.append(held.astype(BF16))
            ws.append(lam_t[ids[b], pl.ds(2 * p, 2), :] * gr2)
        m = dot(jnp.concatenate(helds, axis=0), bd_t[p])
        wqs = []
        acc = dq_acc[...]
        r2 = jnp.zeros((2, TOK), F32)
        for i, b in enumerate(group_levels):
            mi = m[64 * i : 64 * (i + 1)]
            w = jnp.concatenate([ws[i][0:1], ws[i][1:2]], axis=1)
            gsum = jnp.sum(q2 * mi, axis=0, keepdims=True)
            acc = acc + w * mi
            wqs.append((w * q2).astype(BF16))
            g2 = jnp.concatenate([gsum[:, 0:128], gsum[:, 128:256]], axis=0)
            glam[b, pl.ds(2 * p, 2), :] = gr2 * g2
            r2 = r2 + ws[i] * g2
        dq_acc[...] = acc
        if group_levels == [0]:
            rnear[pl.ds(2 * p, 2), :] = r2
        else:
            rint[pl.ds(2 * p, 2), :] += r2
        grad = dot(jnp.concatenate(wqs, axis=0), bd[p])
        for i, b in enumerate(group_levels):
            gi = grad[64 * i : 64 * (i + 1)]
            if b == 0:
                gn[p] = gi.reshape(2, 4, 8, 128)
            else:
                gi = (gi * scales[i]).reshape(2, 4, 8, 128)
                at = spot(b - 1, p)
                g[b - 1, 0, at] = gi[0]
                g[b - 1, 1, at] = gi[1]

    def levels_pass(group_levels):
        def two(i):
            levels_step(group_levels, 2 * i)
            levels_step(group_levels, 2 * i + 1)

        loop(0, pairs // 2, two)

    g0_copy = near(gn, g0, g0_sem.at[0], g0_sem.at[1])

    @pl.when(core == 1)
    def _():
        rest.wait_recv()
        levels_pass([0])
        g0_copy.start()

    for lev in high:
        second_phase(lev)

    def swap(lev):
        return near(g.at[lev, 1 - core], x.at[lev], x_send.at[lev], x_recv.at[lev])

    def fetch(levs):
        for lev in levs:
            rows_first, first, second, users, arrays, slot = routes[lev]

            @pl.when(reads(lev))
            def _():
                if second > 1:
                    part = h.at[lev, core, pl.ds(0, (second - 1) * first)]
                    near(part, part, h_send.at[lev], h_recv.at[lev]).wait_recv()
                ours = h.at[lev, core]
                near(ours, ours, f_send.at[lev], f_recv.at[lev]).start()

        for lev in levs:

            @pl.when(reads(lev))
            def _():
                theirs = h.at[lev, 1 - core]
                near(theirs, theirs, f_send.at[lev], f_recv.at[lev]).wait_recv()

    def give_back(levs):
        for lev in levs:

            @pl.when(reads(lev))
            def _():
                swap(lev).start()

        for lev in levs:
            rows_first, first, second, users, arrays, slot = routes[lev]
            fpos, spos, at = where_on(lev)

            @pl.when(reads(lev))
            def _():
                swap(lev).wait_recv()

                def add(c):
                    st[lev, c] = g[lev, core, c] + x[lev, c]

                loop(0, chips, add)
                for d in range(1, second):
                    s = (spos + d) % second
                    remote(
                        st.at[lev, pl.ds(s * first, first)],
                        back.at[lev, spos, pl.ds(0, first)],
                        b_send.at[lev],
                        b_recv.at[lev],
                        (group, 2 * at(fpos, s) + core),
                    ).start()
                back[lev, spos, 0:first] = st[lev, pl.ds(spos * first, first)]

    def gather_back(lev):
        rows_first, first, second, users, arrays, slot = routes[lev]
        fpos, spos, at = where_on(lev)

        def arrived(count):
            if count:
                part = back.at[lev, pl.ds(0, count), pl.ds(0, first)]
                near(part, part, b_send.at[lev], b_recv.at[lev]).wait_recv()

        def go():
            if lev >= nb:
                arrived(second - 1)
            else:

                @pl.when(reads(lev))
                def _():
                    arrived(len(users) - 1)

                @pl.when(jnp.logical_not(reads(lev)))
                def _():
                    arrived(len(users))

            for a, readers in enumerate(arrays):
                for f in range(first):
                    total = back[lev, readers[0], f]
                    for s in readers[1:]:
                        total = total + back[lev, s, f]
                    q_sum[slot + a, f] = total
                for d in range(1, first):
                    f = (fpos + d) % first
                    remote(
                        q_sum.at[slot + a, f],
                        parts.at[slot + a, fpos],
                        q_send.at[slot + a],
                        q_recv.at[slot + a],
                        (group, 2 * at(f, spos) + core),
                    ).start()
                parts[slot + a, fpos] = q_sum[slot + a, fpos]

        when_level(lev, go)

    def parts_in(lev):
        rows_first, first, second, users, arrays, slot = routes[lev]
        if first > 1:
            for a in range(len(arrays)):
                part = parts.at[slot + a, pl.ds(0, first - 1)]
                near(part, part, q_send.at[slot + a], q_recv.at[slot + a]).wait_recv()

    k_part = pk.at[pl.ds(0, chips - 1)]
    scales_in = near(k_part, k_part, k_sem.at[0], k_sem.at[1])
    scales_in.wait_recv()
    fetch(low)
    levels_pass([b + 1 for b in low])
    give_back(low)
    fetch(high)

    @pl.when(group > 0)
    def _():
        levels_pass([b + 1 for b in high])

    give_back(high)

    r = rint[...]
    rsum = jnp.broadcast_to(jnp.sum(r, axis=1, keepdims=True), (heads, TOK))
    lane = iota((8, 128), 1)
    first_lane = jnp.where((sub == 0) & (lane == 0), 1.0, 0.0)
    mid_lane = jnp.where((sub == 0) & (lane == 64), 1.0, 0.0)
    for p in range(pairs):
        rs[p] = first_lane * rsum[2 * p : 2 * p + 1] + mid_lane * rsum[2 * p + 1 : 2 * p + 2]

    def send_sums(i):
        to = shifted(i)
        remote(
            rs.at[to], rr.at[chip], t_sem.at[0], t_sem.at[1], (group, 2 * to + core)
        ).start()

    loop(1, chips, send_sums)
    rr[chip] = rs[chip]
    for lev in low:
        gather_back(lev)

    for p in range(columns):
        total = jnp.zeros((heads, TOK), F32)
        for b in range(1 + levels):
            total = total + jnp.where(ids[b] == p, glam[b], 0.0)
        dlam_ref[p] = total
    even = jnp.where(core == 0, 1.0, 0.0)
    dlogt_ref[...] += (
        dot(r + rnear[...], (row >= col).astype(F32), precision=highest) - even * rsum
    )
    dqi = (dq_acc[:, 0:128] + dq_acc[:, 128:256]).astype(BF16).astype(F32)
    dst = dsc[...]
    dqt_ref[...] = dqi + dot(kt, dst, precision=highest)
    dkt_ref[...] = dot(dst, q, precision=highest).T

    for lev in high:
        gather_back(lev)

    for lev in high:
        first, slot = routes[lev][1], routes[lev][5]

        @pl.when(reads(lev))
        def _():
            parts_in(lev)
            total = parts[slot, 0]
            for f in range(1, first):
                total = total + parts[slot, f]
            u[lev - nb] = total

    for d in range(1, groups):

        @pl.when(group - d >= 0)
        def _():
            level = high_level(group, group - d, nz)
            remote(
                u.at[level], zu.at[group], u_send.at[d], u_recv.at[group], (group - d, me)
            ).start()

    for lev in low:
        rows_first, first, second, users, arrays, slot = routes[lev]
        parts_in(lev)
        for a in range(len(arrays)):
            if rows_first:
                for f in range(first):
                    dn[offs[lev] + f * (ydim >> lev) + 2 * a] = parts[slot + a, f]
            else:
                total = parts[slot + a, 0]
                for f in range(1, first):
                    total = total + parts[slot + a, f]
                dn[offs[lev] + 2 * a] = total

    coef[...] = jnp.ones((8, 128), F32)
    dn[top] = jnp.zeros((4, 8, 128), F32)
    for d in range(1, groups):

        @pl.when(group + d < groups)
        def _():
            far = zb.at[group + d, 4]
            near(far, far, z_send.at[0], z_recv.at[group + d]).wait_recv()
            slot = zu.at[group + d]
            near(slot, slot, u_send.at[d], u_recv.at[group + d]).wait_recv()
            dn[top] = dn[top] + coef[...][None] * zu[group + d]
            coef[...] = coef[...] * zb[group + d, 4]

    loads[6].wait()
    fu = jnp.concatenate([fu_ref[0], fu_ref[1]], axis=1).reshape(4, 8, 128)
    dn[top] = dn[top] + coef[...][None] * fu
    cown[...] = jnp.sum(nd[top, 0:4] * dn[top], axis=0)
    for l in range(nz):

        @pl.when(bit_of(group, l))
        def _():
            cown[...] = cown[...] - jnp.sum(u[l] * hz[l], axis=0)

    for d in range(1, groups):

        @pl.when(group + d < groups)
        def _():
            remote(cown, ct.at[group], c_send.at[d], c_recv.at[group], (group + d, me)).start()

    for b in reversed(range(nb)):
        for i in range(0, chips >> b, 2):
            left = offs[b] + i
            parent = dn[offs[b + 1] + i // 2]
            dn[left] = dn[left] + nd[left + 1, 4][None] * parent
            dn[left + 1] = parent

    def give(i):
        to = shifted(i)
        remote(
            dn.at[to], ds.at[core, chip], o_sem.at[0], o_sem.at[1], (group, 2 * to + core)
        ).start()

    loop(1, chips, give)
    ds[core, chip] = dn[chip]

    t_part = rr.at[pl.ds(0, chips - 1)]
    sums_in = near(t_part, t_part, t_sem.at[0], t_sem.at[1])
    sums_in.wait_recv()
    coef[...] = jnp.zeros((8, 128), F32)
    for d in range(1, groups):

        @pl.when(group - d >= 0)
        def _():
            slot = ct.at[group - d]
            near(slot, slot, c_send.at[d], c_recv.at[group - d]).wait_recv()
            coef[...] = coef[...] + ct[group - d]

    carry = coef[...]
    for c in range(chips):
        carry_out[c, 0] = carry
        carry = carry + jnp.sum(nd[c, 0:4] * dn[c], axis=0) - rr[c]
        carry_out[c, 1] = carry

    def give_carry(i):
        to = shifted(i)
        remote(
            carry_out.at[to], carry_in.at[core, chip], o_sem.at[2], o_sem.at[3], (group, 2 * to + core)
        ).start()

    loop(1, chips, give_carry)
    carry_in[core, chip] = carry_out[chip]
    part = ds.at[core, pl.ds(0, chips - 1)]
    given = near(part, part, o_sem.at[0], o_sem.at[1])
    given.wait_recv()
    near(ds.at[core], ds.at[core], w_sem.at[0], w_sem.at[1]).start()
    c_part = carry_in.at[core, pl.ds(0, chips - 1)]
    carried = near(c_part, c_part, o_sem.at[2], o_sem.at[3])
    carried.wait_recv()
    near(carry_in.at[core], carry_in.at[core], w_sem.at[2], w_sem.at[3]).start()

    for lev in range(levels):
        rows_first, first, second, users, arrays, slot = routes[lev]

        def out_of_ring(count):
            if count:
                part = h.at[lev, core, pl.ds(0, count * first)]
                near(part, part, h_send.at[lev], h_recv.at[lev]).wait_send()

        def sends():
            if first > 1:
                for a in range(len(arrays)):
                    part = ring.at[slot + a, pl.ds(0, first - 1)]
                    near(part, part, r_send.at[slot + a], r_recv.at[slot + a]).wait_send()
                    near(part, part, q_send.at[slot + a], q_recv.at[slot + a]).wait_send()
            if lev >= nb:
                out_of_ring(second - 1)

        when_level(lev, sends)

        if lev < nb:

            @pl.when(jnp.logical_not(reads(lev)))
            def _():
                out_of_ring(len(users))

        @pl.when(reads(lev))
        def _():
            if lev < nb:
                out_of_ring(len(users) - 1)
            ours = h.at[lev, core]
            near(ours, ours, f_send.at[lev], f_recv.at[lev]).wait_send()
            swap(lev).wait_send()
            if second > 1:
                part = st.at[lev, pl.ds(0, (second - 1) * first)]
                near(part, part, b_send.at[lev], b_recv.at[lev]).wait_send()

    for d in range(1, groups):

        @pl.when(group + d < groups)
        def _():
            up(d).wait_send()
            near(cown, cown, c_send.at[d], c_recv.at[0]).wait_send()

        @pl.when(group - d >= 0)
        def _():
            line = nd.at[top, 4]
            near(line, line, z_send.at[groups + d], z_recv.at[0]).wait_send()
            near(u.at[0], u.at[0], u_send.at[d], u_recv.at[0]).wait_send()

    swap_half.wait_send()
    swap_dec.wait_send()
    scattered.wait_send()
    scales_in.wait_send()
    sums_in.wait_send()
    carried.wait_send()

    @pl.when(core == 1)
    def _():
        g0_copy.wait_send()

    @pl.when(core == 0)
    def _():
        rest.wait_send()
        g0_copy.wait_recv()

    given.wait_send()
    theirs = ds.at[1 - core]
    both = near(theirs, theirs, w_sem.at[0], w_sem.at[1])
    both.wait_recv()
    both.wait_send()
    theirs = carry_in.at[1 - core]
    both = near(theirs, theirs, w_sem.at[2], w_sem.at[3])
    both.wait_recv()
    both.wait_send()

    def finish(p):
        scale = jnp.where(core == 0, sibd[p], jnp.ones((8, 128), F32))
        dld = jnp.zeros((8, 128), F32)
        for j in range(2):
            grad = ds[j, p]
            dot_own = jnp.sum(own[p, j] * grad, axis=0)
            dld = dld + jnp.where(core == 0, carry_in[j, p, 0], carry_in[j, p, 1] - dot_own)
            extra = jnp.where(core == 0, g0[p, j], 0.0)
            low_ref[p, 32 * j : 32 * (j + 1)] = (
                (grad * scale[None] + extra).reshape(32, 128).astype(BF16)
            )
        dld_ref[pl.ds(p, 1), :] = jnp.sum(dld, axis=0, keepdims=True)

    loop(0, pairs, finish)


def end_kernel(
    v_ref,
    kt_ref,
    crow_ref,
    low_ref,
    dld_ref,
    dvp_ref,
    dkp_ref,
    dlogp_ref,
    dqp_ref,
    dlamp_ref,
    dv_ref,
    dk_ref,
    dq_ref,
    dlog_ref,
    dlam_ref,
):
    heads = crow_ref.shape[0]
    pairs = heads // 2
    columns = dlamp_ref.shape[0]
    row = iota((TOK, TOK), 0)
    col = iota((TOK, TOK), 1)
    left = col < 64
    ccol = crow_ref[...].T
    tail = jnp.exp(ccol[TOK - 1 : TOK, :] - ccol)
    k_low = kt_ref[...].T.astype(BF16)
    dk = jnp.zeros((64, TOK), F32)
    ls = jnp.zeros((TOK, heads), F32)
    lane_row = iota((TOK, heads), 0)
    lane_col = iota((TOK, heads), 1)
    for p in range(pairs):
        sl = slice(p * 128, (p + 1) * 128)
        pick = (lane_col == 2 * p + lane_row // 64).astype(F32)
        low = low_ref[p]
        scale = jnp.where(left, tail[:, 2 * p : 2 * p + 1], tail[:, 2 * p + 1 : 2 * p + 2])
        vp = v_ref[:, sl].astype(F32)
        dvs = scale * dot(k_low, low)
        decayed = (scale * vp).astype(BF16)
        dk += lax.dot_general(
            low, decayed, (((1,), (1,)), ((), ())), preferred_element_type=F32
        )
        dv_ref[:, sl] = (dvp_ref[:, sl] + dvs).astype(BF16)
        ls += dot((vp * dvs).astype(BF16), pick.astype(BF16))
    dk_ref[...] = dkp_ref[...] + dk
    dq_ref[...] = dqp_ref[...]
    strict = (row > col).astype(F32)
    head = iota((heads, pairs), 0)
    rows = dot((iota((heads, pairs), 1) == head // 2).astype(F32), dld_ref[...], precision=highest)
    side = iota((heads, TOK), 1) // 64 == iota((heads, TOK), 0) % 2
    dd = jnp.sum(jnp.where(side, rows, 0.0), axis=1, keepdims=True)
    dlog_ref[...] = dlogp_ref[...] + dot(strict, ls, precision=highest).T + dd
    wide = min(128, columns * heads)
    per = wide // heads
    for j in range(columns // per):
        dlam_ref[:, j * wide : (j + 1) * wide] = (
            dlamp_ref[pl.ds(j * per, per)].reshape(wide, TOK).T
        )


def body(
    values, state_input, state_output, log_decay, level_lam, level_ids, upstream, final_upstream
):
    shards, groups = lax.axis_size("shard"), lax.axis_size("grp")
    chips = shards // 2
    nb, nz = log2(chips), log2(groups)
    levels = nb + nz
    heads = log_decay.shape[1]
    columns = level_lam.shape[1] // heads
    params = partial(pltpu.CompilerParams, vmem_limit_bytes=VMEM_CAP)
    dma = pltpu.SemaphoreType.DMA
    tile = (4, 8, 128)
    kt = state_input.T
    ydim = 2 ** ((nb + 1) // 2)
    routes = routes_of(nb, nz, chips // ydim, ydim)
    slots = sum(len(route[4]) for route in routes)

    dv, dqt, dkt, dlam, dlogt, crow, low, dld = pl.pallas_call(
        partial(main_kernel, shards, groups),
        out_shape=(
            f32(TOK, heads * 64),
            f32(64, TOK),
            f32(64, TOK),
            f32(columns, heads, TOK),
            f32(heads, TOK),
            f32(heads, TOK),
            jax.ShapeDtypeStruct((chips, 64, 128), BF16),
            f32(chips, 128),
        ),
        in_specs=[pl.BlockSpec(memory_space=pltpu.SMEM)]
        + [pl.BlockSpec(memory_space=pltpu.HBM)] * 7,
        out_specs=(vmem(),) * 8,
        scratch_shapes=[
            pltpu.VMEM((TOK, heads * 64), BF16),
            pltpu.VMEM((TOK, heads * 64), BF16),
            pltpu.VMEM((64, TOK), F32),
            pltpu.VMEM((64, TOK), F32),
            pltpu.VMEM((heads, TOK), F32),
            pltpu.VMEM((TOK, columns * heads), F32),
            pltpu.VMEM((2, 32, 64), F32),
            dma((7,)),
            pltpu.VMEM((chips, 128, 256), BF16),
            pltpu.VMEM((chips, 256, 128), BF16),
            pltpu.VMEM((columns, heads, TOK), F32),
            pltpu.VMEM((1 + levels, heads, TOK), F32),
            pltpu.VMEM((heads, TOK), F32),
            pltpu.VMEM((heads, TOK), F32),
            pltpu.VMEM((64, 256), F32),
            pltpu.VMEM((TOK, TOK), F32),
            pltpu.VMEM((levels, 2, chips) + tile, F32),
            pltpu.VMEM((chips, 2) + tile, F32),
            pltpu.VMEM((chips, 2) + tile, F32),
            pltpu.VMEM((chips, 8, 128), F32),
            pltpu.VMEM((chips, 2) + tile, F32),
            pltpu.VMEM((chips, 8, 128), F32),
            pltpu.VMEM((chips, 5, 8, 128), F32),
            pltpu.VMEM((2 * chips, 5, 8, 128), F32),
            pltpu.VMEM((groups, 5, 8, 128), F32),
            pltpu.VMEM((nz,) + tile, F32),
            pltpu.VMEM((chips, 8, 128), F32),
            pltpu.VMEM((chips, 8, 128), F32),
            pltpu.VMEM((8, 128), F32),
            pltpu.VMEM((slots, ydim) + tile, F32),
            pltpu.VMEM((levels, 2, chips) + tile, F32),
            pltpu.VMEM((levels, chips) + tile, F32),
            pltpu.VMEM((levels, chips) + tile, F32),
            pltpu.VMEM((levels, ydim, ydim) + tile, F32),
            pltpu.VMEM((slots, ydim) + tile, F32),
            pltpu.VMEM((slots, ydim) + tile, F32),
            pltpu.VMEM((chips, 8, 128), F32),
            pltpu.VMEM((chips, 8, 128), F32),
            pltpu.VMEM((nz,) + tile, F32),
            pltpu.VMEM((groups,) + tile, F32),
            pltpu.VMEM((groups, 8, 128), F32),
            pltpu.VMEM((8, 128), F32),
            pltpu.VMEM((2 * chips,) + tile, F32),
            pltpu.VMEM((chips, 2, 8, 128), F32),
            pltpu.VMEM((2, chips, 2, 8, 128), F32),
            pltpu.VMEM((2, chips) + tile, F32),
            pltpu.VMEM((chips, 2) + tile, F32),
            dma((6,)),
            dma((2,)),
            dma((2 * groups,)),
            dma((groups,)),
            dma((2,)),
            dma((slots,)),
            dma((slots,)),
            dma((levels,)),
            dma((levels,)),
            dma((levels,)),
            dma((levels,)),
            dma((2,)),
            dma((levels,)),
            dma((levels,)),
            dma((levels,)),
            dma((levels,)),
            dma((slots,)),
            dma((slots,)),
            dma((2,)),
            dma((groups,)),
            dma((groups,)),
            dma((groups,)),
            dma((groups,)),
            dma((4,)),
            dma((4,)),
        ],
        compiler_params=params(collective_id=0, has_side_effects=True),
        name="main",
    )(
        level_ids,
        values,
        upstream,
        kt,
        state_output.T,
        log_decay.T,
        level_lam,
        final_upstream.reshape(chips, 2, 2, 32, 64),
    )

    dv, dk, dq, dlog, dlam = pl.pallas_call(
        end_kernel,
        out_shape=(
            jax.ShapeDtypeStruct((TOK, heads * 64), BF16),
            f32(64, TOK),
            f32(64, TOK),
            f32(heads, TOK),
            f32(TOK, columns * heads),
        ),
        in_specs=[vmem()] * 10,
        out_specs=(vmem(),) * 5,
        compiler_params=params(),
        name="end",
    )(values, kt, crow, low, dld, dv, dkt, dlogt, dqt, dlam)
    return (dv, dk.T, dq.T, dlog.T, dlam)


def solution(mesh):
    spec = P(("grp", "shard"), None)
    return jax.shard_map(
        body,
        mesh=mesh,
        in_specs=(spec,) * 7 + (P(),),
        out_specs=(spec,) * 5,
        check_vma=False,
    )
```

```python
from functools import partial

import jax
import jax.numpy as jnp
from jax import lax
from jax.experimental import pallas as pl
from jax.experimental.pallas import tpu as pltpu
from jax.sharding import PartitionSpec as P

highest = lax.Precision.HIGHEST
MESH = pl.DeviceIdType.MESH
F32 = jnp.float32
BF16 = jnp.bfloat16
TOK = 128
VMEM_CAP = 62 * 1024 * 1024


def log2(n):
    return n.bit_length() - 1


def f32(*shape):
    return jax.ShapeDtypeStruct(shape, F32)


def iota(shape, dim):
    return lax.broadcasted_iota(jnp.int32, shape, dim)


def dot(a, b, **kw):
    return jnp.dot(a, b, preferred_element_type=F32, **kw)


def place():
    group = lax.axis_index("grp")
    me = lax.axis_index("shard")
    return group, me, me // 2, me % 2


def remote(src, dst, send, recv, device):
    return pltpu.make_async_remote_copy(
        src_ref=src, dst_ref=dst, send_sem=send, recv_sem=recv, device_id=device, device_id_type=MESH
    )


def loop(start, stop, fn):
    def step(i, carry):
        fn(i)
        return carry

    lax.fori_loop(start, stop, step, 0)


def enter(group, me, chip, core, chips, groups):
    barrier = pltpu.get_barrier_semaphore()

    def greet(shard, grp):
        pl.semaphore_signal(barrier, inc=1, device_id=(grp, shard), device_id_type=MESH)

    loop(1, chips, lambda d: greet(2 * ((chip + d) % chips) + core, group))
    loop(1, groups, lambda d: greet(me, (group + d) % groups))
    greet(me + 1 - 2 * core, group)
    return lambda: pl.semaphore_wait(barrier, chips + groups - 1)


def offsets(chips):
    offs, at, n = [], 0, chips
    while n >= 1:
        offs.append(at)
        at += n
        n //= 2
    return offs


def high_level(group, far, bits):
    level = jnp.int32(0)
    for b in range(1, bits):
        level = jnp.where(group // 2**b != far // 2**b, jnp.int32(b), level)
    return level


def bit_of(x, b):
    return (x // 2**b) % 2 == 1


def routes_of(nb, nz, xdim, ydim):
    routes, slot = [], 0
    for lev in range(nb + nz):
        ybits = log2(ydim)
        rows_first = lev < ybits or lev == nb
        first, second = (xdim, ydim) if rows_first else (ydim, xdim)
        if lev < nb:
            bit = lev if rows_first else lev - ybits
            users = [s for s in range(second) if (s >> bit) & 1]
            arrays = [[s for s in users if s >> (bit + 1) == a] for a in range(second >> (bit + 1))]
        else:
            users = list(range(second))
            arrays = [users]
        routes.append((rows_first, first, second, users, arrays, slot))
        slot += len(arrays)
    return routes


def main_kernel(
    shards,
    groups,
    ids_ref,
    v_any,
    do_any,
    kt_any,
    qt_any,
    ldt_any,
    lam_any,
    fu_any,
    dv_any,
    dqt_any,
    dkt_any,
    dlam_any,
    dlogt_any,
    crow_any,
    low_any,
    dld_any,
    dv_ref,
    dqt_ref,
    dkt_ref,
    dlam_ref,
    dlogt_ref,
    crow_ref,
    low_ref,
    dld_ref,
    out_sem,
    v_ref,
    do_ref,
    kt_ref,
    qt_ref,
    ldt_ref,
    lam_ref,
    fu_ref,
    in_sem,
    bd_t,
    bd,
    lam_t,
    glam,
    rint,
    rnear,
    dq_acc,
    dsc,
    g,
    gn,
    own,
    dec,
    sib,
    sibd,
    blk,
    nd,
    zb,
    hz,
    pks,
    pk,
    coef,
    before_far,
    ring,
    h,
    x,
    st,
    back,
    q_sum,
    parts,
    rs,
    rr,
    u,
    zu,
    z_out,
    cown,
    dn,
    ds,
    g0,
    s_sem,
    a_sem,
    z_send,
    z_recv,
    k_sem,
    r_send,
    r_recv,
    h_send,
    h_recv,
    f_send,
    f_recv,
    g0_sem,
    x_send,
    x_recv,
    b_send,
    b_recv,
    q_send,
    q_recv,
    t_sem,
    u_send,
    u_recv,
    o_sem,
    w_sem,
):
    chips = shards // 2
    pairs = chips
    heads = shards
    nb, nz = log2(chips), log2(groups)
    levels = nb + nz
    columns = lam_t.shape[0]
    ydim = 2 ** ((nb + 1) // 2)
    xdim = chips // ydim
    group, me, chip, core = place()
    mate = me + 1 - 2 * core
    xpos, ypos = chip // ydim, chip % ydim
    offs = offsets(chips)
    top = offs[nb]
    wide = min(128, columns * heads)
    per = wide // heads

    routes = routes_of(nb, nz, xdim, ydim)

    def shifted(i):
        return ((xpos + i // ydim) % xdim) * ydim + (ypos + i % ydim) % ydim

    def near(src, dst, send, recv):
        return remote(src, dst, send, recv, (group, mate))

    loads = [
        pltpu.make_async_copy(a, b, in_sem.at[i])
        for i, (a, b) in enumerate(
            [
                (ldt_any, ldt_ref),
                (kt_any, kt_ref),
                (v_any, v_ref),
                (do_any, do_ref),
                (qt_any, qt_ref),
                (lam_any, lam_ref),
                (fu_any.at[chip, :, core], fu_ref),
            ]
        )
    ]
    for c in loads:
        c.start()
    results = [
        pltpu.make_async_copy(a, b, out_sem.at[i])
        for i, (a, b) in enumerate(
            [
                (dv_ref, dv_any),
                (dqt_ref, dqt_any),
                (dkt_ref, dkt_any),
                (dlam_ref, dlam_any),
                (dlogt_ref, dlogt_any),
                (crow_ref, crow_any),
                (low_ref, low_any),
                (dld_ref, dld_any),
            ]
        )
    ]
    wait_entry = enter(group, me, chip, core, chips, groups)

    row = iota((TOK, TOK), 0)
    col = iota((TOK, TOK), 1)
    upto = (row <= col).astype(F32)
    half = (col < 64).astype(F32)
    m0 = half.astype(BF16)
    m1 = (1.0 - half).astype(BF16)
    loads[0].wait()
    crow = dot(ldt_ref[...], upto, precision=highest)
    crow_ref[...] = crow
    results[5].start()
    last = jnp.broadcast_to(crow[:, TOK - 1 : TOK], (heads, TOK))
    tail = jnp.exp(last - crow)
    full = jnp.exp(last)
    loads[1].wait()
    kt = kt_ref[...]
    loads[2].wait()
    for p in range(pairs):
        k2 = jnp.concatenate(
            [kt * tail[2 * p : 2 * p + 1], kt * tail[2 * p + 1 : 2 * p + 2]], axis=1
        ).astype(BF16)
        vp = v_ref[:, p * 128 : (p + 1) * 128]
        s = dot(k2, jnp.concatenate([vp * m0, vp * m1], axis=0))
        own[p] = s.reshape(2, 4, 8, 128)
        dec[p] = (
            half[0:8] * full[2 * p : 2 * p + 1] + (1.0 - half[0:8]) * full[2 * p + 1 : 2 * p + 2]
        )

    wait_entry()
    swap_half = near(own.at[:, 1 - core], sib.at[:, 1 - core], s_sem.at[0], s_sem.at[1])
    swap_dec = near(dec, sibd, s_sem.at[2], s_sem.at[3])
    rest = near(own.at[:, core], sib.at[:, core], s_sem.at[4], s_sem.at[5])
    swap_half.start()
    swap_dec.start()

    @pl.when(core == 0)
    def _():
        rest.start()

    swap_dec.wait_recv()
    swap_half.wait_recv()

    def merge_cores(p):
        a = own[p, core]
        b = sib[p, core]
        left = jnp.where(core == 0, a, b)
        right = jnp.where(core == 0, b, a)
        drow = jnp.where(core == 0, sibd[p], dec[p])
        blk[p, 0:4] = drow[None] * left + right
        blk[p, 4] = dec[p] * sibd[p]

    loop(0, pairs, merge_cores)

    def scatter(i):
        to = shifted(i)
        remote(
            blk.at[to], nd.at[chip], a_sem.at[0], a_sem.at[1], (group, 2 * to + core)
        ).start()

    loop(1, chips, scatter)
    nd[chip] = blk[chip]

    loads[3].wait()
    loads[4].wait()
    qt = qt_ref[...]
    q = qt.T
    k = kt.T
    ccol = crow.T
    causal = row <= col
    scores = jnp.where(causal, dot(k, qt, precision=highest), 0.0)
    b_col = jnp.exp(ccol[TOK // 2 - 1 : TOK // 2, :] - ccol)
    a_row = jnp.exp(crow - crow[:, TOK // 2 - 1 : TOK // 2])
    suffix = (row >= col).astype(F32).astype(BF16)
    before = row < col
    t0 = (row < 64).astype(F32).astype(BF16)
    t1 = (row >= 64).astype(F32).astype(BF16)
    dsc[...] = jnp.zeros(dsc.shape, F32)

    def inside(p):
        sl = slice(p * 128, (p + 1) * 128)
        dop = do_ref[:, sl]
        dot_t = dop.astype(F32).T.astype(BF16)
        bdt = jnp.concatenate([dot_t * t0, dot_t * t1], axis=1)
        bdo = jnp.concatenate([dop * m0, dop * m1], axis=0)
        bd_t[p] = bdt
        bd[p] = bdo
        dmix = dot(v_ref[:, sl], bdt)
        xs = []
        for j in range(2):
            head = 2 * p + j
            dm = dmix[:, j * 128 : (j + 1) * 128]
            e = jnp.where(causal, b_col[:, head : head + 1] * a_row[head : head + 1, :], 0.0)
            mix = e * scores
            dsc[...] += e * dm
            y = dot((mix * dm).astype(BF16), suffix)
            dlogt_ref[head : head + 1, :] = jnp.sum(
                jnp.where(before, y, 0.0), axis=0, keepdims=True
            )
            xs.append(mix.astype(BF16))
        dv_ref[:, sl] = dot(jnp.concatenate(xs, axis=1), bdo)

    for p in range(pairs // 2):
        inside(p)

    part = nd.at[pl.ds(0, chips - 1)]
    scattered = near(part, part, a_sem.at[0], a_sem.at[1])
    scattered.wait_recv()
    for b in range(1, nb + 1):
        for i in range(chips >> b):
            lo = offs[b - 1] + 2 * i
            right = nd[lo + 1, 4]
            nd[offs[b] + i, 0:4] = right[None] * nd[lo, 0:4] + nd[lo + 1, 0:4]
            nd[offs[b] + i, 4] = right * nd[lo, 4]

    def up(d):
        return remote(
            nd.at[top], zb.at[group], z_send.at[d], z_recv.at[group], (group + d, me)
        )

    def down(d):
        return remote(
            nd.at[top, 4], zb.at[group, 4], z_send.at[d], z_recv.at[group], (group - d, me)
        )

    for d in range(1, groups):

        @pl.when(group + d < groups)
        def _():
            up(d).start()

    for d in range(1, groups):

        @pl.when(group - d >= 0)
        def _():
            remote(
                nd.at[top, 4],
                zb.at[group, 4],
                z_send.at[groups + d],
                z_recv.at[group],
                (group - d, me),
            ).start()

    sub = iota((8, 128), 0)
    for c in range(chips):
        pre = jnp.ones((8, 128), F32)
        rows = pre
        for b in range(nb):
            rows = jnp.where(sub >= b, pre, rows)
            if (c >> b) & 1:
                pre = pre * nd[offs[b] + (c >> b) - 1, 4]
        pks[c] = jnp.where(sub >= nb, pre, rows)

    def send_scales(i):
        to = shifted(i)
        remote(
            pks.at[to], pk.at[chip], k_sem.at[0], k_sem.at[1], (group, 2 * to + core)
        ).start()

    loop(1, chips, send_scales)
    pk[chip] = pks[chip]

    def where_on(lev):
        rows_first, first, second, users, arrays, slot = routes[lev]
        if rows_first:
            return xpos, ypos, lambda f, s: f * ydim + s
        return ypos, xpos, lambda f, s: s * ydim + f

    def reads(lev):
        if lev >= nb:
            return bit_of(group, lev - nb)
        return bit_of(chip, lev)

    def when_level(lev, fn):
        if lev >= nb:
            pl.when(bit_of(group, lev - nb))(fn)
        else:
            fn()

    def first_phase(lev):
        rows_first, first, second, users, arrays, slot = routes[lev]
        fpos, spos, at = where_on(lev)

        def source(a, f):
            if lev >= nb:
                return hz.at[lev - nb]
            if rows_first:
                return nd.at[offs[lev] + f * (ydim >> lev) + 2 * a, 0:4]
            return nd.at[offs[lev] + 2 * a, 0:4]

        def go():
            for d in range(1, first):
                f = (fpos + d) % first
                for a in range(len(arrays)):
                    remote(
                        source(a, f),
                        ring.at[slot + a, fpos],
                        r_send.at[slot + a],
                        r_recv.at[slot + a],
                        (group, 2 * at(f, spos) + core),
                    ).start()
            for a in range(len(arrays)):
                ring[slot + a, fpos] = source(a, fpos)[...]

        if lev >= nb:
            go()
        else:
            when_level(lev, go)

    def second_phase(lev):
        rows_first, first, second, users, arrays, slot = routes[lev]
        fpos, spos, at = where_on(lev)

        def go():
            if first > 1:
                for a in range(len(arrays)):
                    part = ring.at[slot + a, pl.ds(0, first - 1)]
                    near(part, part, r_send.at[slot + a], r_recv.at[slot + a]).wait_recv()
            for a, readers in enumerate(arrays):
                for s in readers:
                    there = h.at[lev, core, pl.ds(spos * first, first)]

                    @pl.when(spos != s)
                    def _():
                        remote(
                            ring.at[slot + a, pl.ds(0, first)],
                            there,
                            h_send.at[lev],
                            h_recv.at[lev],
                            (group, 2 * at(fpos, s) + core),
                        ).start()

                    @pl.when(spos == s)
                    def _():
                        there[...] = ring[slot + a, 0:first]

        when_level(lev, go)

    low = list(range(nb))
    high = list(range(nb, levels))
    for lev in low:
        first_phase(lev)

    for p in range(pairs // 2, 3 * pairs // 4):
        inside(p)
    for lev in low:
        second_phase(lev)
    for p in range(3 * pairs // 4, pairs):
        inside(p)
    results[0].start()

    coef[...] = jnp.ones((8, 128), F32)
    hz[...] = jnp.zeros(hz.shape, F32)
    for d in range(1, groups):
        far = group - d

        @pl.when(far >= 0)
        def _():
            slot = zb.at[far]
            near(slot, slot, z_send.at[0], z_recv.at[far]).wait_recv()
            level = high_level(group, far, nz)
            hz[level] = hz[level] + coef[...][None] * zb[far, 0:4]
            before_far[d] = coef[...]
            coef[...] = coef[...] * zb[far, 4]

        l = log2(d)

        @pl.when(bit_of(group, l) & (group % 2**l + 2**l == d))
        def _():
            first_phase(nb + l)

    q_low = qt.astype(BF16).astype(F32)
    q2 = jnp.concatenate([q_low, q_low], axis=1)
    loads[5].wait()
    for j in range(columns // per):
        lam_t[pl.ds(j * per, per)] = lam_ref[:, j * wide : (j + 1) * wide].T.reshape(
            per, heads, TOK
        )
    glam[...] = jnp.zeros(glam.shape, F32)
    rint[...] = jnp.zeros(rint.shape, F32)
    rnear[...] = jnp.zeros(rnear.shape, F32)
    dq_acc[...] = jnp.zeros(dq_acc.shape, F32)
    ids = [ids_ref[0, b] for b in range(1 + levels)]

    def spot(lev, p):
        if routes[lev][0]:
            return (p % ydim) * xdim + p // ydim
        return p

    def levels_step(group_levels, p):
        gr2 = jnp.exp(crow_ref[pl.ds(2 * p, 2), :])
        mate_scale = jnp.where(core == 1, sibd[p, 0:1], jnp.ones((1, 128), F32))
        helds, ws, scales = [], [], []
        for b in group_levels:
            if b == 0:
                held = sib[p].reshape(64, 128)
                scales.append(None)
            else:
                scales.append(mate_scale * pk[p, b - 1 : b])
                at = spot(b - 1, p)
                held = jnp.concatenate([h[b - 1, 0, at], h[b - 1, 1, at]], axis=0)
                held = jnp.where(reads(b - 1), held.reshape(64, 128) * scales[-1], 0.0)
            helds.append(held.astype(BF16))
            ws.append(lam_t[ids[b], pl.ds(2 * p, 2), :] * gr2)
        m = dot(jnp.concatenate(helds, axis=0), bd_t[p])
        wqs = []
        acc = dq_acc[...]
        r2 = jnp.zeros((2, TOK), F32)
        for i, b in enumerate(group_levels):
            mi = m[64 * i : 64 * (i + 1)]
            w = jnp.concatenate([ws[i][0:1], ws[i][1:2]], axis=1)
            gsum = jnp.sum(q2 * mi, axis=0, keepdims=True)
            acc = acc + w * mi
            wqs.append((w * q2).astype(BF16))
            g2 = jnp.concatenate([gsum[:, 0:128], gsum[:, 128:256]], axis=0)
            glam[b, pl.ds(2 * p, 2), :] = gr2 * g2
            r2 = r2 + ws[i] * g2
        dq_acc[...] = acc
        if group_levels == [0]:
            rnear[pl.ds(2 * p, 2), :] = r2
        else:
            rint[pl.ds(2 * p, 2), :] += r2
        grad = dot(jnp.concatenate(wqs, axis=0), bd[p])
        for i, b in enumerate(group_levels):
            gi = grad[64 * i : 64 * (i + 1)]
            if b == 0:
                gn[p] = gi.reshape(2, 4, 8, 128)
            else:
                gi = (gi * scales[i]).reshape(2, 4, 8, 128)
                at = spot(b - 1, p)
                g[b - 1, 0, at] = gi[0]
                g[b - 1, 1, at] = gi[1]

    def levels_pass(group_levels):
        def two(i):
            levels_step(group_levels, 2 * i)
            levels_step(group_levels, 2 * i + 1)

        loop(0, pairs // 2, two)

    g0_copy = near(gn, g0, g0_sem.at[0], g0_sem.at[1])

    @pl.when(core == 1)
    def _():
        rest.wait_recv()
        levels_pass([0])
        g0_copy.start()

    for lev in high:
        second_phase(lev)

    def swap(lev):
        return near(g.at[lev, 1 - core], x.at[lev], x_send.at[lev], x_recv.at[lev])

    def fetch(levs):
        for lev in levs:
            rows_first, first, second, users, arrays, slot = routes[lev]

            @pl.when(reads(lev))
            def _():
                if second > 1:
                    part = h.at[lev, core, pl.ds(0, (second - 1) * first)]
                    near(part, part, h_send.at[lev], h_recv.at[lev]).wait_recv()
                ours = h.at[lev, core]
                near(ours, ours, f_send.at[lev], f_recv.at[lev]).start()

        for lev in levs:

            @pl.when(reads(lev))
            def _():
                theirs = h.at[lev, 1 - core]
                near(theirs, theirs, f_send.at[lev], f_recv.at[lev]).wait_recv()

    def give_back(levs):
        for lev in levs:

            @pl.when(reads(lev))
            def _():
                swap(lev).start()

        for lev in levs:
            rows_first, first, second, users, arrays, slot = routes[lev]
            fpos, spos, at = where_on(lev)

            @pl.when(reads(lev))
            def _():
                swap(lev).wait_recv()

                def add(c):
                    st[lev, c] = g[lev, core, c] + x[lev, c]

                loop(0, chips, add)
                for d in range(1, second):
                    s = (spos + d) % second
                    remote(
                        st.at[lev, pl.ds(s * first, first)],
                        back.at[lev, spos, pl.ds(0, first)],
                        b_send.at[lev],
                        b_recv.at[lev],
                        (group, 2 * at(fpos, s) + core),
                    ).start()
                back[lev, spos, 0:first] = st[lev, pl.ds(spos * first, first)]

    def gather_back(lev):
        rows_first, first, second, users, arrays, slot = routes[lev]
        fpos, spos, at = where_on(lev)

        def arrived(count):
            if count:
                part = back.at[lev, pl.ds(0, count), pl.ds(0, first)]
                near(part, part, b_send.at[lev], b_recv.at[lev]).wait_recv()

        def go():
            if lev >= nb:
                arrived(second - 1)
            else:

                @pl.when(reads(lev))
                def _():
                    arrived(len(users) - 1)

                @pl.when(jnp.logical_not(reads(lev)))
                def _():
                    arrived(len(users))

            for a, readers in enumerate(arrays):
                for f in range(first):
                    total = back[lev, readers[0], f]
                    for s in readers[1:]:
                        total = total + back[lev, s, f]
                    q_sum[slot + a, f] = total
                for d in range(1, first):
                    f = (fpos + d) % first
                    remote(
                        q_sum.at[slot + a, f],
                        parts.at[slot + a, fpos],
                        q_send.at[slot + a],
                        q_recv.at[slot + a],
                        (group, 2 * at(f, spos) + core),
                    ).start()
                parts[slot + a, fpos] = q_sum[slot + a, fpos]

        when_level(lev, go)

    def parts_in(lev):
        rows_first, first, second, users, arrays, slot = routes[lev]
        if first > 1:
            for a in range(len(arrays)):
                part = parts.at[slot + a, pl.ds(0, first - 1)]
                near(part, part, q_send.at[slot + a], q_recv.at[slot + a]).wait_recv()

    k_part = pk.at[pl.ds(0, chips - 1)]
    scales_in = near(k_part, k_part, k_sem.at[0], k_sem.at[1])
    scales_in.wait_recv()
    fetch(low)
    levels_pass([b + 1 for b in low])
    fetch(high)

    @pl.when(group > 0)
    def _():
        levels_pass([b + 1 for b in high])

    give_back(high)
    give_back(low)

    r = rint[...]
    rsum = jnp.broadcast_to(jnp.sum(r, axis=1, keepdims=True), (heads, TOK))
    lane = iota((8, 128), 1)
    first_lane = jnp.where((sub == 0) & (lane == 0), 1.0, 0.0)
    mid_lane = jnp.where((sub == 0) & (lane == 64), 1.0, 0.0)
    for p in range(pairs):
        rs[p] = first_lane * rsum[2 * p : 2 * p + 1] + mid_lane * rsum[2 * p + 1 : 2 * p + 2]

    def send_sums(i):
        to = shifted(i)
        remote(
            rs.at[to], rr.at[chip], t_sem.at[0], t_sem.at[1], (group, 2 * to + core)
        ).start()

    loop(1, chips, send_sums)
    rr[chip] = rs[chip]
    for lev in high:
        gather_back(lev)

    for lev in high:
        first, slot = routes[lev][1], routes[lev][5]

        @pl.when(reads(lev))
        def _():
            parts_in(lev)
            total = parts[slot, 0]
            for f in range(1, first):
                total = total + parts[slot, f]
            u[lev - nb] = total

    coef[...] = jnp.zeros((8, 128), F32)
    for d in reversed(range(1, groups)):

        @pl.when(group - d >= 0)
        def _():
            level = high_level(group, group - d, nz)
            grad = u[level]
            z_out[d, 0:4] = grad
            z_out[d, 4] = coef[...]
            remote(
                z_out.at[d], zu.at[group], u_send.at[d], u_recv.at[group], (group - d, me)
            ).start()
            coef[...] = coef[...] + before_far[d] * jnp.sum(grad * zb[group - d, 0:4], axis=0)

    for lev in low:
        gather_back(lev)

    for p in range(columns):
        total = jnp.zeros((heads, TOK), F32)
        for b in range(1 + levels):
            total = total + jnp.where(ids[b] == p, glam[b], 0.0)
        dlam_ref[p] = total
    even = jnp.where(core == 0, 1.0, 0.0)
    dlogt_ref[...] += (
        dot(r + rnear[...], (row >= col).astype(F32), precision=highest) - even * rsum
    )
    dqi = (dq_acc[:, 0:128] + dq_acc[:, 128:256]).astype(BF16).astype(F32)
    dst = dsc[...]
    dqt_ref[...] = dqi + dot(kt, dst, precision=highest)
    dkt_ref[...] = dot(dst, q, precision=highest).T
    for i in range(1, 5):
        results[i].start()

    for lev in low:
        rows_first, first, second, users, arrays, slot = routes[lev]
        parts_in(lev)
        for a in range(len(arrays)):
            if rows_first:
                for f in range(first):
                    dn[offs[lev] + f * (ydim >> lev) + 2 * a, 0:4] = parts[slot + a, f]
            else:
                total = parts[slot + a, 0]
                for f in range(1, first):
                    total = total + parts[slot + a, f]
                dn[offs[lev] + 2 * a, 0:4] = total

    coef[...] = jnp.ones((8, 128), F32)
    dn[top, 0:4] = jnp.zeros((4, 8, 128), F32)
    cown[...] = jnp.zeros((8, 128), F32)
    for l in range(nz):

        @pl.when(bit_of(group, l))
        def _():
            cown[...] = cown[...] + jnp.sum(u[l] * hz[l], axis=0)

    for d in range(1, groups):

        @pl.when(group + d < groups)
        def _():
            far = zb.at[group + d, 4]
            near(far, far, z_send.at[0], z_recv.at[group + d]).wait_recv()
            slot = zu.at[group + d]
            near(slot, slot, u_send.at[d], u_recv.at[group + d]).wait_recv()
            dn[top, 0:4] = dn[top, 0:4] + coef[...][None] * zu[group + d, 0:4]
            cown[...] = cown[...] + zu[group + d, 4]
            coef[...] = coef[...] * zb[group + d, 4]

    loads[6].wait()
    fu = jnp.concatenate([fu_ref[0], fu_ref[1]], axis=1).reshape(4, 8, 128)
    dn[top, 0:4] = dn[top, 0:4] + coef[...][None] * fu
    earlier = hz[0]
    for l in range(1, nz):
        earlier = earlier + hz[l]
    carry = cown[...] + coef[...] * nd[top, 4] * jnp.sum(earlier * fu, axis=0)
    for b in reversed(range(nb)):
        for i in range(0, chips >> b, 2):
            left = offs[b] + i
            parent = dn[offs[b + 1] + i // 2, 0:4]
            dn[left, 0:4] = dn[left, 0:4] + nd[left + 1, 4][None] * parent
            dn[left + 1, 0:4] = parent

    t_part = rr.at[pl.ds(0, chips - 1)]
    sums_in = near(t_part, t_part, t_sem.at[0], t_sem.at[1])
    sums_in.wait_recv()
    now = jnp.sum(carry, axis=0, keepdims=True)
    for c in range(chips):
        step = jnp.sum(nd[c, 0:4] * dn[c, 0:4], axis=0) - rr[c]
        then = now + jnp.sum(step, axis=0, keepdims=True)
        dn[c, 4] = jnp.where(sub == 0, now, jnp.where(sub == 1, then, 0.0))
        now = then

    def give(i):
        to = shifted(i)
        remote(
            dn.at[to], ds.at[core, chip], o_sem.at[0], o_sem.at[1], (group, 2 * to + core)
        ).start()

    loop(1, chips, give)
    ds[core, chip] = dn[chip]

    part = ds.at[core, pl.ds(0, chips - 1)]
    given = near(part, part, o_sem.at[0], o_sem.at[1])
    given.wait_recv()
    near(ds.at[core], ds.at[core], w_sem.at[0], w_sem.at[1]).start()

    for lev in range(levels):
        rows_first, first, second, users, arrays, slot = routes[lev]

        def out_of_ring(count):
            if count:
                part = h.at[lev, core, pl.ds(0, count * first)]
                near(part, part, h_send.at[lev], h_recv.at[lev]).wait_send()

        def sends():
            if first > 1:
                for a in range(len(arrays)):
                    part = ring.at[slot + a, pl.ds(0, first - 1)]
                    near(part, part, r_send.at[slot + a], r_recv.at[slot + a]).wait_send()
                    near(part, part, q_send.at[slot + a], q_recv.at[slot + a]).wait_send()
            if lev >= nb:
                out_of_ring(second - 1)

        when_level(lev, sends)

        if lev < nb:

            @pl.when(jnp.logical_not(reads(lev)))
            def _():
                out_of_ring(len(users))

        @pl.when(reads(lev))
        def _():
            if lev < nb:
                out_of_ring(len(users) - 1)
            ours = h.at[lev, core]
            near(ours, ours, f_send.at[lev], f_recv.at[lev]).wait_send()
            swap(lev).wait_send()
            if second > 1:
                part = st.at[lev, pl.ds(0, (second - 1) * first)]
                near(part, part, b_send.at[lev], b_recv.at[lev]).wait_send()

    for d in range(1, groups):

        @pl.when(group + d < groups)
        def _():
            up(d).wait_send()

        @pl.when(group - d >= 0)
        def _():
            line = nd.at[top, 4]
            near(line, line, z_send.at[groups + d], z_recv.at[0]).wait_send()
            near(z_out.at[d], z_out.at[d], u_send.at[d], u_recv.at[0]).wait_send()

    swap_half.wait_send()
    swap_dec.wait_send()
    scattered.wait_send()
    scales_in.wait_send()
    sums_in.wait_send()

    @pl.when(core == 1)
    def _():
        g0_copy.wait_send()

    @pl.when(core == 0)
    def _():
        rest.wait_send()
        g0_copy.wait_recv()

    given.wait_send()
    theirs = ds.at[1 - core]
    both = near(theirs, theirs, w_sem.at[0], w_sem.at[1])
    both.wait_recv()
    both.wait_send()
    def finish(p):
        scale = jnp.where(core == 0, sibd[p], jnp.ones((8, 128), F32))
        dld = jnp.zeros((8, 128), F32)
        for j in range(2):
            grad = ds[j, p, 0:4]
            dot_own = jnp.sum(own[p, j] * grad, axis=0)
            dld = dld + jnp.where(sub == core, ds[j, p, 4], 0.0)
            dld = dld - jnp.where(core == 0, 0.0, dot_own)
            extra = jnp.where(core == 0, g0[p, j], 0.0)
            low_ref[p, 32 * j : 32 * (j + 1)] = (
                (grad * scale[None] + extra).reshape(32, 128).astype(BF16)
            )
        dld_ref[pl.ds(p, 1), :] = jnp.sum(dld, axis=0, keepdims=True)

    loop(0, pairs, finish)
    results[6].start()
    results[7].start()
    for c in results:
        c.wait()


def end_kernel(
    v_any,
    kt_any,
    crow_any,
    low_any,
    dld_any,
    dvp_any,
    dkp_any,
    dlogp_any,
    dqp_any,
    dlamp_any,
    dv_any,
    dk_any,
    dq_any,
    dlog_any,
    dlam_any,
    v_ref,
    kt_ref,
    crow_ref,
    low_ref,
    dld_ref,
    dvp_ref,
    dkp_ref,
    dlogp_ref,
    dlamp_ref,
    dv_ref,
    dk_ref,
    dlog_ref,
    dlam_ref,
    in_sem,
    out_sem,
):
    heads = crow_ref.shape[0]
    pairs = heads // 2
    columns = dlamp_ref.shape[0]
    loads = [
        pltpu.make_async_copy(a, b, in_sem.at[i])
        for i, (a, b) in enumerate(
            [
                (dlamp_any, dlamp_ref),
                (crow_any, crow_ref),
                (kt_any, kt_ref),
                (low_any, low_ref),
                (v_any, v_ref),
                (dvp_any, dvp_ref),
                (dld_any, dld_ref),
                (dkp_any, dkp_ref),
                (dlogp_any, dlogp_ref),
            ]
        )
    ]
    for c in loads:
        c.start()
    through = pltpu.make_async_copy(dqp_any, dq_any, out_sem.at[0])
    through.start()
    row = iota((TOK, TOK), 0)
    col = iota((TOK, TOK), 1)
    left = col < 64
    loads[0].wait()
    wide = min(128, columns * heads)
    per = wide // heads
    for j in range(columns // per):
        dlam_ref[:, j * wide : (j + 1) * wide] = (
            dlamp_ref[pl.ds(j * per, per)].reshape(wide, TOK).T
        )
    lam_out = pltpu.make_async_copy(dlam_ref, dlam_any, out_sem.at[1])
    lam_out.start()
    loads[1].wait()
    ccol = crow_ref[...].T
    tail = jnp.exp(ccol[TOK - 1 : TOK, :] - ccol)
    loads[2].wait()
    k_low = kt_ref[...].T.astype(BF16)
    dk = jnp.zeros((64, TOK), F32)
    ls = jnp.zeros((TOK, heads), F32)
    lane_row = iota((TOK, heads), 0)
    lane_col = iota((TOK, heads), 1)
    for i in range(3, 9):
        loads[i].wait()
    parts = []
    for p in range(pairs):
        sl = slice(p * 128, (p + 1) * 128)
        pick = (lane_col == 2 * p + lane_row // 64).astype(F32)
        low = low_ref[p]
        scale = jnp.where(left, tail[:, 2 * p : 2 * p + 1], tail[:, 2 * p + 1 : 2 * p + 2])
        vp = v_ref[:, sl].astype(F32)
        dvs = scale * dot(k_low, low)
        decayed = (scale * vp).astype(BF16)
        dk += lax.dot_general(
            low, decayed, (((1,), (1,)), ((), ())), preferred_element_type=F32
        )
        dv_ref[:, sl] = (dvp_ref[:, sl] + dvs).astype(BF16)
        ls += dot((vp * dvs).astype(BF16), pick.astype(BF16))
        if (p + 1) % (pairs // 2) == 0:
            cols = pl.ds((p + 1 - pairs // 2) * 128, pairs // 2 * 128)
            parts.append(
                pltpu.make_async_copy(
                    dv_ref.at[:, cols], dv_any.at[:, cols], out_sem.at[4 + len(parts)]
                )
            )
            parts[-1].start()
    dk_ref[...] = dkp_ref[...] + dk
    k_out = pltpu.make_async_copy(dk_ref, dk_any, out_sem.at[2])
    k_out.start()
    strict = (row > col).astype(F32)
    head = iota((heads, pairs), 0)
    rows = dot((iota((heads, pairs), 1) == head // 2).astype(F32), dld_ref[...], precision=highest)
    side = iota((heads, TOK), 1) // 64 == iota((heads, TOK), 0) % 2
    dd = jnp.sum(jnp.where(side, rows, 0.0), axis=1, keepdims=True)
    dlog_ref[...] = dlogp_ref[...] + dot(strict, ls, precision=highest).T + dd
    log_out = pltpu.make_async_copy(dlog_ref, dlog_any, out_sem.at[3])
    log_out.start()
    for c in [through, lam_out, k_out, log_out] + parts:
        c.wait()


def body(
    values, state_input, state_output, log_decay, level_lam, level_ids, upstream, final_upstream
):
    shards, groups = lax.axis_size("shard"), lax.axis_size("grp")
    chips = shards // 2
    nb, nz = log2(chips), log2(groups)
    levels = nb + nz
    heads = log_decay.shape[1]
    columns = level_lam.shape[1] // heads
    params = partial(pltpu.CompilerParams, vmem_limit_bytes=VMEM_CAP)
    dma = pltpu.SemaphoreType.DMA
    tile = (4, 8, 128)
    kt = state_input.T
    ydim = 2 ** ((nb + 1) // 2)
    routes = routes_of(nb, nz, chips // ydim, ydim)
    slots = sum(len(route[4]) for route in routes)

    dv, dqt, dkt, dlam, dlogt, crow, low, dld = pl.pallas_call(
        partial(main_kernel, shards, groups),
        out_shape=(
            f32(TOK, heads * 64),
            f32(64, TOK),
            f32(64, TOK),
            f32(columns, heads, TOK),
            f32(heads, TOK),
            f32(heads, TOK),
            jax.ShapeDtypeStruct((chips, 64, 128), BF16),
            f32(chips, 128),
        ),
        in_specs=[pl.BlockSpec(memory_space=pltpu.SMEM)]
        + [pl.BlockSpec(memory_space=pl.ANY)] * 7,
        out_specs=(pl.BlockSpec(memory_space=pl.ANY),) * 8,
        scratch_shapes=[
            pltpu.VMEM((TOK, heads * 64), F32),
            pltpu.VMEM((64, TOK), F32),
            pltpu.VMEM((64, TOK), F32),
            pltpu.VMEM((columns, heads, TOK), F32),
            pltpu.VMEM((heads, TOK), F32),
            pltpu.VMEM((heads, TOK), F32),
            pltpu.VMEM((chips, 64, 128), BF16),
            pltpu.VMEM((chips, 128), F32),
            dma((8,)),
            pltpu.VMEM((TOK, heads * 64), BF16),
            pltpu.VMEM((TOK, heads * 64), BF16),
            pltpu.VMEM((64, TOK), F32),
            pltpu.VMEM((64, TOK), F32),
            pltpu.VMEM((heads, TOK), F32),
            pltpu.VMEM((TOK, columns * heads), F32),
            pltpu.VMEM((2, 32, 64), F32),
            dma((7,)),
            pltpu.VMEM((chips, 128, 256), BF16),
            pltpu.VMEM((chips, 256, 128), BF16),
            pltpu.VMEM((columns, heads, TOK), F32),
            pltpu.VMEM((1 + levels, heads, TOK), F32),
            pltpu.VMEM((heads, TOK), F32),
            pltpu.VMEM((heads, TOK), F32),
            pltpu.VMEM((64, 256), F32),
            pltpu.VMEM((TOK, TOK), F32),
            pltpu.VMEM((levels, 2, chips) + tile, F32),
            pltpu.VMEM((chips, 2) + tile, F32),
            pltpu.VMEM((chips, 2) + tile, F32),
            pltpu.VMEM((chips, 8, 128), F32),
            pltpu.VMEM((chips, 2) + tile, F32),
            pltpu.VMEM((chips, 8, 128), F32),
            pltpu.VMEM((chips, 5, 8, 128), F32),
            pltpu.VMEM((2 * chips, 5, 8, 128), F32),
            pltpu.VMEM((groups, 5, 8, 128), F32),
            pltpu.VMEM((nz,) + tile, F32),
            pltpu.VMEM((chips, 8, 128), F32),
            pltpu.VMEM((chips, 8, 128), F32),
            pltpu.VMEM((8, 128), F32),
            pltpu.VMEM((groups, 8, 128), F32),
            pltpu.VMEM((slots, ydim) + tile, F32),
            pltpu.VMEM((levels, 2, chips) + tile, F32),
            pltpu.VMEM((levels, chips) + tile, F32),
            pltpu.VMEM((levels, chips) + tile, F32),
            pltpu.VMEM((levels, ydim, ydim) + tile, F32),
            pltpu.VMEM((slots, ydim) + tile, F32),
            pltpu.VMEM((slots, ydim) + tile, F32),
            pltpu.VMEM((chips, 8, 128), F32),
            pltpu.VMEM((chips, 8, 128), F32),
            pltpu.VMEM((nz,) + tile, F32),
            pltpu.VMEM((groups, 5, 8, 128), F32),
            pltpu.VMEM((groups, 5, 8, 128), F32),
            pltpu.VMEM((8, 128), F32),
            pltpu.VMEM((2 * chips, 5, 8, 128), F32),
            pltpu.VMEM((2, chips, 5, 8, 128), F32),
            pltpu.VMEM((chips, 2) + tile, F32),
            dma((6,)),
            dma((2,)),
            dma((2 * groups,)),
            dma((groups,)),
            dma((2,)),
            dma((slots,)),
            dma((slots,)),
            dma((levels,)),
            dma((levels,)),
            dma((levels,)),
            dma((levels,)),
            dma((2,)),
            dma((levels,)),
            dma((levels,)),
            dma((levels,)),
            dma((levels,)),
            dma((slots,)),
            dma((slots,)),
            dma((2,)),
            dma((groups,)),
            dma((groups,)),
            dma((2,)),
            dma((2,)),
        ],
        compiler_params=params(collective_id=0, has_side_effects=True),
        name="main",
    )(
        level_ids,
        values,
        upstream,
        kt,
        state_output.T,
        log_decay.T,
        level_lam,
        final_upstream.reshape(chips, 2, 2, 32, 64),
    )

    dv, dk, dq, dlog, dlam = pl.pallas_call(
        end_kernel,
        out_shape=(
            jax.ShapeDtypeStruct((TOK, heads * 64), BF16),
            f32(64, TOK),
            f32(64, TOK),
            f32(heads, TOK),
            f32(TOK, columns * heads),
        ),
        in_specs=[pl.BlockSpec(memory_space=pl.ANY)] * 10,
        out_specs=(pl.BlockSpec(memory_space=pl.ANY),) * 5,
        scratch_shapes=[
            pltpu.VMEM((TOK, heads * 64), BF16),
            pltpu.VMEM((64, TOK), F32),
            pltpu.VMEM((heads, TOK), F32),
            pltpu.VMEM((chips, 64, 128), BF16),
            pltpu.VMEM((chips, 128), F32),
            pltpu.VMEM((TOK, heads * 64), F32),
            pltpu.VMEM((64, TOK), F32),
            pltpu.VMEM((heads, TOK), F32),
            pltpu.VMEM((columns, heads, TOK), F32),
            pltpu.VMEM((TOK, heads * 64), BF16),
            pltpu.VMEM((64, TOK), F32),
            pltpu.VMEM((heads, TOK), F32),
            pltpu.VMEM((TOK, columns * heads), F32),
            dma((9,)),
            dma((6,)),
        ],
        compiler_params=params(),
        name="end",
    )(values, kt, crow, low, dld, dv, dkt, dlogt, dqt, dlam)
    return (dv, dk.T, dq.T, dlog.T, dlam)


def solution(mesh):
    spec = P(("grp", "shard"), None)
    return jax.shard_map(
        body,
        mesh=mesh,
        in_specs=(spec,) * 7 + (P(),),
        out_specs=(spec,) * 5,
        check_vma=False,
    )
```

```python
from functools import partial

import jax
import jax.numpy as jnp
from jax import lax
from jax.experimental import pallas as pl
from jax.experimental.pallas import tpu as pltpu
from jax.sharding import PartitionSpec as P

highest = lax.Precision.HIGHEST
MESH = pl.DeviceIdType.MESH
F32 = jnp.float32
BF16 = jnp.bfloat16
TOK = 128
VMEM_CAP = 62 * 1024 * 1024


def log2(n):
    return n.bit_length() - 1


def f32(*shape):
    return jax.ShapeDtypeStruct(shape, F32)


def iota(shape, dim):
    return lax.broadcasted_iota(jnp.int32, shape, dim)


def dot(a, b, **kw):
    return jnp.dot(a, b, preferred_element_type=F32, **kw)


def place():
    group = lax.axis_index("grp")
    me = lax.axis_index("shard")
    return group, me, me // 2, me % 2


def remote(src, dst, send, recv, device):
    return pltpu.make_async_remote_copy(
        src_ref=src, dst_ref=dst, send_sem=send, recv_sem=recv, device_id=device, device_id_type=MESH
    )


def loop(start, stop, fn):
    def step(i, carry):
        fn(i)
        return carry

    lax.fori_loop(start, stop, step, 0)


def enter(group, me, chip, core, chips, groups):
    barrier = pltpu.get_barrier_semaphore()

    def greet(shard, grp):
        pl.semaphore_signal(barrier, inc=1, device_id=(grp, shard), device_id_type=MESH)

    loop(1, chips, lambda d: greet(2 * ((chip + d) % chips) + core, group))
    loop(1, groups, lambda d: greet(me, (group + d) % groups))
    greet(me + 1 - 2 * core, group)
    return lambda: pl.semaphore_wait(barrier, chips + groups - 1)


def offsets(chips):
    offs, at, n = [], 0, chips
    while n >= 1:
        offs.append(at)
        at += n
        n //= 2
    return offs


def high_level(group, far, bits):
    level = jnp.int32(0)
    for b in range(1, bits):
        level = jnp.where(group // 2**b != far // 2**b, jnp.int32(b), level)
    return level


def bit_of(x, b):
    return (x // 2**b) % 2 == 1


def routes_of(nb, nz, xdim, ydim):
    routes, slot = [], 0
    ybits = log2(ydim)
    split = nb + min(1, nz - 1)
    for lev in range(nb + nz):
        if lev == split:
            ways = [(0, 2, True), (2, 4, False)]
        else:
            ways = [(0, 4, lev < ybits or nb <= lev < split)]
        for t0, t1, rows_first in ways:
            first, second = (xdim, ydim) if rows_first else (ydim, xdim)
            if lev < nb:
                bit = lev if rows_first else lev - ybits
                users = [s for s in range(second) if (s >> bit) & 1]
                arrays = [
                    [s for s in users if s >> (bit + 1) == a] for a in range(second >> (bit + 1))
                ]
            else:
                users = list(range(second))
                arrays = [users]
            routes.append((lev, slice(t0, t1), rows_first, first, second, users, arrays, slot))
            slot += len(arrays)
    return routes


def main_kernel(
    shards,
    groups,
    ids_ref,
    v_any,
    do_any,
    kt_any,
    qt_any,
    ldt_any,
    lam_any,
    fu_any,
    dv_any,
    dqt_any,
    dkt_any,
    dlam_any,
    dlogt_any,
    crow_any,
    low_any,
    dld_any,
    dv_ref,
    dqt_ref,
    dkt_ref,
    dlam_ref,
    dlogt_ref,
    crow_ref,
    low_ref,
    dld_ref,
    out_sem,
    v_ref,
    do_ref,
    kt_ref,
    qt_ref,
    ldt_ref,
    lam_ref,
    fu_ref,
    in_sem,
    bd_t,
    bd,
    lam_t,
    glam,
    rint,
    rnear,
    dq_acc,
    dsc,
    g,
    gn,
    own,
    dec,
    sib,
    sibd,
    blk,
    nd,
    zb,
    hz,
    pks,
    pk,
    coef,
    before_far,
    ring,
    h,
    x,
    st,
    back,
    q_sum,
    parts,
    rs,
    rr,
    u,
    zu,
    z_out,
    cown,
    dn,
    ds,
    g0,
    s_sem,
    a_sem,
    z_send,
    z_recv,
    k_sem,
    r_send,
    r_recv,
    h_send,
    h_recv,
    f_send,
    f_recv,
    g0_sem,
    x_send,
    x_recv,
    b_send,
    b_recv,
    q_send,
    q_recv,
    t_sem,
    u_send,
    u_recv,
    o_sem,
    w_sem,
):
    chips = shards // 2
    pairs = chips
    heads = shards
    nb, nz = log2(chips), log2(groups)
    levels = nb + nz
    columns = lam_t.shape[0]
    ydim = 2 ** ((nb + 1) // 2)
    xdim = chips // ydim
    group, me, chip, core = place()
    mate = me + 1 - 2 * core
    xpos, ypos = chip // ydim, chip % ydim
    offs = offsets(chips)
    top = offs[nb]
    wide = min(128, columns * heads)
    per = wide // heads

    routes = routes_of(nb, nz, xdim, ydim)
    ways = [[r for r in range(len(routes)) if routes[r][0] == lev] for lev in range(levels)]

    def shifted(i):
        return ((xpos + i // ydim) % xdim) * ydim + (ypos + i % ydim) % ydim

    def near(src, dst, send, recv):
        return remote(src, dst, send, recv, (group, mate))

    loads = [
        pltpu.make_async_copy(a, b, in_sem.at[i])
        for i, (a, b) in enumerate(
            [
                (ldt_any, ldt_ref),
                (kt_any, kt_ref),
                (v_any, v_ref),
                (do_any, do_ref),
                (qt_any, qt_ref),
                (lam_any, lam_ref),
                (fu_any.at[chip, :, core], fu_ref),
            ]
        )
    ]
    for c in loads:
        c.start()
    results = [
        pltpu.make_async_copy(a, b, out_sem.at[i])
        for i, (a, b) in enumerate(
            [
                (dv_ref, dv_any),
                (dqt_ref, dqt_any),
                (dkt_ref, dkt_any),
                (dlam_ref, dlam_any),
                (dlogt_ref, dlogt_any),
                (crow_ref, crow_any),
                (low_ref, low_any),
                (dld_ref, dld_any),
            ]
        )
    ]
    wait_entry = enter(group, me, chip, core, chips, groups)

    row = iota((TOK, TOK), 0)
    col = iota((TOK, TOK), 1)
    upto = (row <= col).astype(F32)
    half = (col < 64).astype(F32)
    m0 = half.astype(BF16)
    m1 = (1.0 - half).astype(BF16)
    loads[0].wait()
    crow = dot(ldt_ref[...], upto, precision=highest)
    crow_ref[...] = crow
    results[5].start()
    last = jnp.broadcast_to(crow[:, TOK - 1 : TOK], (heads, TOK))
    tail = jnp.exp(last - crow)
    full = jnp.exp(last)
    loads[1].wait()
    kt = kt_ref[...]
    loads[2].wait()
    for p in range(pairs):
        k2 = jnp.concatenate(
            [kt * tail[2 * p : 2 * p + 1], kt * tail[2 * p + 1 : 2 * p + 2]], axis=1
        ).astype(BF16)
        vp = v_ref[:, p * 128 : (p + 1) * 128]
        s = dot(k2, jnp.concatenate([vp * m0, vp * m1], axis=0))
        own[p] = s.reshape(2, 4, 8, 128)
        dec[p] = (
            half[0:8] * full[2 * p : 2 * p + 1] + (1.0 - half[0:8]) * full[2 * p + 1 : 2 * p + 2]
        )

    wait_entry()
    swap_half = near(own.at[:, 1 - core], sib.at[:, 1 - core], s_sem.at[0], s_sem.at[1])
    swap_dec = near(dec, sibd, s_sem.at[2], s_sem.at[3])
    rest = near(own.at[:, core], sib.at[:, core], s_sem.at[4], s_sem.at[5])
    swap_half.start()
    swap_dec.start()

    @pl.when(core == 0)
    def _():
        rest.start()

    swap_dec.wait_recv()
    swap_half.wait_recv()

    def merge_cores(p):
        a = own[p, core]
        b = sib[p, core]
        left = jnp.where(core == 0, a, b)
        right = jnp.where(core == 0, b, a)
        drow = jnp.where(core == 0, sibd[p], dec[p])
        blk[p, 0:4] = drow[None] * left + right
        blk[p, 4] = dec[p] * sibd[p]

    loop(0, pairs, merge_cores)

    def scatter(i):
        to = shifted(i)
        remote(
            blk.at[to], nd.at[chip], a_sem.at[0], a_sem.at[1], (group, 2 * to + core)
        ).start()

    loop(1, chips, scatter)
    nd[chip] = blk[chip]

    loads[3].wait()
    loads[4].wait()
    qt = qt_ref[...]
    q = qt.T
    k = kt.T
    ccol = crow.T
    causal = row <= col
    scores = jnp.where(causal, dot(k, qt, precision=highest), 0.0)
    b_col = jnp.exp(ccol[TOK // 2 - 1 : TOK // 2, :] - ccol)
    a_row = jnp.exp(crow - crow[:, TOK // 2 - 1 : TOK // 2])
    suffix = (row >= col).astype(F32).astype(BF16)
    before = row < col
    t0 = (row < 64).astype(F32).astype(BF16)
    t1 = (row >= 64).astype(F32).astype(BF16)
    dsc[...] = jnp.zeros(dsc.shape, F32)

    def inside(p):
        sl = slice(p * 128, (p + 1) * 128)
        dop = do_ref[:, sl]
        dot_t = dop.astype(F32).T.astype(BF16)
        bdt = jnp.concatenate([dot_t * t0, dot_t * t1], axis=1)
        bdo = jnp.concatenate([dop * m0, dop * m1], axis=0)
        bd_t[p] = bdt
        bd[p] = bdo
        dmix = dot(v_ref[:, sl], bdt)
        xs = []
        for j in range(2):
            head = 2 * p + j
            dm = dmix[:, j * 128 : (j + 1) * 128]
            e = jnp.where(causal, b_col[:, head : head + 1] * a_row[head : head + 1, :], 0.0)
            mix = e * scores
            dsc[...] += e * dm
            y = dot((mix * dm).astype(BF16), suffix)
            dlogt_ref[head : head + 1, :] = jnp.sum(
                jnp.where(before, y, 0.0), axis=0, keepdims=True
            )
            xs.append(mix.astype(BF16))
        dv_ref[:, sl] = dot(jnp.concatenate(xs, axis=1), bdo)

    for p in range(pairs // 2):
        inside(p)

    part = nd.at[pl.ds(0, chips - 1)]
    scattered = near(part, part, a_sem.at[0], a_sem.at[1])
    scattered.wait_recv()
    for b in range(1, nb + 1):
        for i in range(chips >> b):
            lo = offs[b - 1] + 2 * i
            right = nd[lo + 1, 4]
            nd[offs[b] + i, 0:4] = right[None] * nd[lo, 0:4] + nd[lo + 1, 0:4]
            nd[offs[b] + i, 4] = right * nd[lo, 4]

    def up(d):
        return remote(
            nd.at[top], zb.at[group], z_send.at[d], z_recv.at[group], (group + d, me)
        )

    def down(d):
        return remote(
            nd.at[top, 4], zb.at[group, 4], z_send.at[d], z_recv.at[group], (group - d, me)
        )

    for d in range(1, groups):

        @pl.when(group + d < groups)
        def _():
            up(d).start()

    for d in range(1, groups):

        @pl.when(group - d >= 0)
        def _():
            remote(
                nd.at[top, 4],
                zb.at[group, 4],
                z_send.at[groups + d],
                z_recv.at[group],
                (group - d, me),
            ).start()

    sub = iota((8, 128), 0)
    for c in range(chips):
        pre = jnp.ones((8, 128), F32)
        rows = pre
        for b in range(nb):
            rows = jnp.where(sub >= b, pre, rows)
            if (c >> b) & 1:
                pre = pre * nd[offs[b] + (c >> b) - 1, 4]
        pks[c] = jnp.where(sub >= nb, pre, rows)

    def send_scales(i):
        to = shifted(i)
        remote(
            pks.at[to], pk.at[chip], k_sem.at[0], k_sem.at[1], (group, 2 * to + core)
        ).start()

    loop(1, chips, send_scales)
    pk[chip] = pks[chip]

    def where_on(r):
        if routes[r][2]:
            return xpos, ypos, lambda f, s: f * ydim + s
        return ypos, xpos, lambda f, s: s * ydim + f

    def reads(lev):
        if lev >= nb:
            return bit_of(group, lev - nb)
        return bit_of(chip, lev)

    def when_level(lev, fn):
        if lev >= nb:
            pl.when(bit_of(group, lev - nb))(fn)
        else:
            fn()

    def first_phase(r):
        lev, tiles, rows_first, first, second, users, arrays, slot = routes[r]
        fpos, spos, at = where_on(r)

        def source(a, f):
            if lev >= nb:
                return hz.at[lev - nb, tiles]
            if rows_first:
                return nd.at[offs[lev] + f * (ydim >> lev) + 2 * a, 0:4]
            return nd.at[offs[lev] + 2 * a, 0:4]

        def go():
            for d in range(1, first):
                f = (fpos + d) % first
                for a in range(len(arrays)):
                    remote(
                        source(a, f),
                        ring.at[slot + a, fpos, tiles],
                        r_send.at[slot + a],
                        r_recv.at[slot + a],
                        (group, 2 * at(f, spos) + core),
                    ).start()
            for a in range(len(arrays)):
                ring[slot + a, fpos, tiles] = source(a, fpos)[...]

        if lev >= nb:
            go()
        else:
            when_level(lev, go)

    def second_phase(r):
        lev, tiles, rows_first, first, second, users, arrays, slot = routes[r]
        fpos, spos, at = where_on(r)

        def go():
            if first > 1:
                for a in range(len(arrays)):
                    part = ring.at[slot + a, pl.ds(0, first - 1), tiles]
                    near(part, part, r_send.at[slot + a], r_recv.at[slot + a]).wait_recv()
            for a, readers in enumerate(arrays):
                for s in readers:
                    there = h.at[lev, core, pl.ds(spos * first, first), tiles]

                    @pl.when(spos != s)
                    def _():
                        remote(
                            ring.at[slot + a, pl.ds(0, first), tiles],
                            there,
                            h_send.at[r],
                            h_recv.at[r],
                            (group, 2 * at(fpos, s) + core),
                        ).start()

                    @pl.when(spos == s)
                    def _():
                        there[...] = ring[slot + a, 0:first, tiles]

        when_level(lev, go)

    low = list(range(nb))
    high = list(range(nb, levels))
    low_ways = [r for lev in low for r in ways[lev]]
    high_ways = [r for lev in high for r in ways[lev]]
    for r in low_ways:
        first_phase(r)

    for p in range(pairs // 2, 3 * pairs // 4):
        inside(p)
    for r in low_ways:
        second_phase(r)
    for p in range(3 * pairs // 4, pairs):
        inside(p)
    results[0].start()

    coef[...] = jnp.ones((8, 128), F32)
    hz[...] = jnp.zeros(hz.shape, F32)
    for d in range(1, groups):
        far = group - d

        @pl.when(far >= 0)
        def _():
            slot = zb.at[far]
            near(slot, slot, z_send.at[0], z_recv.at[far]).wait_recv()
            level = high_level(group, far, nz)
            hz[level] = hz[level] + coef[...][None] * zb[far, 0:4]
            before_far[d] = coef[...]
            coef[...] = coef[...] * zb[far, 4]

        l = log2(d)

        @pl.when(bit_of(group, l) & (group % 2**l + 2**l == d))
        def _():
            for r in ways[nb + l]:
                first_phase(r)

    q_low = qt.astype(BF16).astype(F32)
    q2 = jnp.concatenate([q_low, q_low], axis=1)
    loads[5].wait()
    for j in range(columns // per):
        lam_t[pl.ds(j * per, per)] = lam_ref[:, j * wide : (j + 1) * wide].T.reshape(
            per, heads, TOK
        )
    glam[...] = jnp.zeros(glam.shape, F32)
    rint[...] = jnp.zeros(rint.shape, F32)
    rnear[...] = jnp.zeros(rnear.shape, F32)
    dq_acc[...] = jnp.zeros(dq_acc.shape, F32)
    ids = [ids_ref[0, b] for b in range(1 + levels)]

    def spot(r, p):
        if routes[r][2]:
            return (p % ydim) * xdim + p // ydim
        return p

    def levels_step(group_levels, p):
        gr2 = jnp.exp(crow_ref[pl.ds(2 * p, 2), :])
        mate_scale = jnp.where(core == 1, sibd[p, 0:1], jnp.ones((1, 128), F32))
        helds, ws, scales = [], [], []
        for b in group_levels:
            if b == 0:
                held = sib[p].reshape(64, 128)
                scales.append(None)
            else:
                scales.append(mate_scale * pk[p, b - 1 : b])
                held = jnp.concatenate(
                    [h[b - 1, j, spot(r, p), routes[r][1]] for j in range(2) for r in ways[b - 1]],
                    axis=0,
                )
                held = jnp.where(reads(b - 1), held.reshape(64, 128) * scales[-1], 0.0)
            helds.append(held.astype(BF16))
            ws.append(lam_t[ids[b], pl.ds(2 * p, 2), :] * gr2)
        m = dot(jnp.concatenate(helds, axis=0), bd_t[p])
        wqs = []
        acc = dq_acc[...]
        r2 = jnp.zeros((2, TOK), F32)
        for i, b in enumerate(group_levels):
            mi = m[64 * i : 64 * (i + 1)]
            w = jnp.concatenate([ws[i][0:1], ws[i][1:2]], axis=1)
            gsum = jnp.sum(q2 * mi, axis=0, keepdims=True)
            acc = acc + w * mi
            wqs.append((w * q2).astype(BF16))
            g2 = jnp.concatenate([gsum[:, 0:128], gsum[:, 128:256]], axis=0)
            glam[b, pl.ds(2 * p, 2), :] = gr2 * g2
            r2 = r2 + ws[i] * g2
        dq_acc[...] = acc
        if group_levels == [0]:
            rnear[pl.ds(2 * p, 2), :] = r2
        else:
            rint[pl.ds(2 * p, 2), :] += r2
        grad = dot(jnp.concatenate(wqs, axis=0), bd[p])
        for i, b in enumerate(group_levels):
            gi = grad[64 * i : 64 * (i + 1)]
            if b == 0:
                gn[p] = gi.reshape(2, 4, 8, 128)
            else:
                gi = (gi * scales[i]).reshape(2, 4, 8, 128)
                for r in ways[b - 1]:
                    tiles = routes[r][1]
                    for j in range(2):
                        g[b - 1, j, spot(r, p), tiles] = gi[j, tiles]

    def levels_pass(group_levels):
        def two(i):
            levels_step(group_levels, 2 * i)
            levels_step(group_levels, 2 * i + 1)

        loop(0, pairs // 2, two)

    g0_copy = near(gn, g0, g0_sem.at[0], g0_sem.at[1])

    @pl.when(core == 1)
    def _():
        rest.wait_recv()
        levels_pass([0])
        g0_copy.start()

    for r in high_ways:
        second_phase(r)

    def swap(lev):
        return near(g.at[lev, 1 - core], x.at[lev], x_send.at[lev], x_recv.at[lev])

    def fetch(levs):
        for lev in levs:

            @pl.when(reads(lev))
            def _():
                for r in ways[lev]:
                    _, tiles, _, first, second, _, _, _ = routes[r]
                    if second > 1:
                        part = h.at[lev, core, pl.ds(0, (second - 1) * first), tiles]
                        near(part, part, h_send.at[r], h_recv.at[r]).wait_recv()
                ours = h.at[lev, core]
                near(ours, ours, f_send.at[lev], f_recv.at[lev]).start()

        for lev in levs:

            @pl.when(reads(lev))
            def _():
                theirs = h.at[lev, 1 - core]
                near(theirs, theirs, f_send.at[lev], f_recv.at[lev]).wait_recv()

    def give_back(levs):
        for lev in levs:

            @pl.when(reads(lev))
            def _():
                swap(lev).start()

        def send_back(r):
            lev, tiles, _, first, second, _, _, _ = routes[r]
            fpos, spos, at = where_on(r)
            for d in range(1, second):
                s = (spos + d) % second
                remote(
                    st.at[lev, pl.ds(s * first, first), tiles],
                    back.at[lev, spos, pl.ds(0, first), tiles],
                    b_send.at[r],
                    b_recv.at[r],
                    (group, 2 * at(fpos, s) + core),
                ).start()
            back[lev, spos, 0:first, tiles] = st[lev, pl.ds(spos * first, first), tiles]

        for lev in levs:

            @pl.when(reads(lev))
            def _():
                swap(lev).wait_recv()

                def add(c):
                    st[lev, c] = g[lev, core, c] + x[lev, c]

                loop(0, chips, add)
                for r in ways[lev]:
                    send_back(r)

    def gather_back(r):
        lev, tiles, rows_first, first, second, users, arrays, slot = routes[r]
        fpos, spos, at = where_on(r)

        def arrived(count):
            if count:
                part = back.at[lev, pl.ds(0, count), pl.ds(0, first), tiles]
                near(part, part, b_send.at[r], b_recv.at[r]).wait_recv()

        def go():
            if lev >= nb:
                arrived(second - 1)
            else:

                @pl.when(reads(lev))
                def _():
                    arrived(len(users) - 1)

                @pl.when(jnp.logical_not(reads(lev)))
                def _():
                    arrived(len(users))

            for a, readers in enumerate(arrays):
                for f in range(first):
                    total = back[lev, readers[0], f, tiles]
                    for s in readers[1:]:
                        total = total + back[lev, s, f, tiles]
                    q_sum[slot + a, f, tiles] = total
                for d in range(1, first):
                    f = (fpos + d) % first
                    remote(
                        q_sum.at[slot + a, f, tiles],
                        parts.at[slot + a, fpos, tiles],
                        q_send.at[slot + a],
                        q_recv.at[slot + a],
                        (group, 2 * at(f, spos) + core),
                    ).start()
                parts[slot + a, fpos, tiles] = q_sum[slot + a, fpos, tiles]

        when_level(lev, go)

    def parts_in(r):
        lev, tiles, rows_first, first, second, users, arrays, slot = routes[r]
        if first > 1:
            for a in range(len(arrays)):
                part = parts.at[slot + a, pl.ds(0, first - 1), tiles]
                near(part, part, q_send.at[slot + a], q_recv.at[slot + a]).wait_recv()

    k_part = pk.at[pl.ds(0, chips - 1)]
    scales_in = near(k_part, k_part, k_sem.at[0], k_sem.at[1])
    scales_in.wait_recv()
    fetch(low)
    levels_pass([b + 1 for b in low])
    fetch(high)

    @pl.when(group > 0)
    def _():
        levels_pass([b + 1 for b in high])

    give_back(high)
    give_back(low)

    pulls = rint[...]
    rsum = jnp.broadcast_to(jnp.sum(pulls, axis=1, keepdims=True), (heads, TOK))
    lane = iota((8, 128), 1)
    first_lane = jnp.where((sub == 0) & (lane == 0), 1.0, 0.0)
    mid_lane = jnp.where((sub == 0) & (lane == 64), 1.0, 0.0)
    for p in range(pairs):
        rs[p] = first_lane * rsum[2 * p : 2 * p + 1] + mid_lane * rsum[2 * p + 1 : 2 * p + 2]

    def send_sums(i):
        to = shifted(i)
        remote(
            rs.at[to], rr.at[chip], t_sem.at[0], t_sem.at[1], (group, 2 * to + core)
        ).start()

    loop(1, chips, send_sums)
    rr[chip] = rs[chip]
    for r in high_ways:
        gather_back(r)

    def sum_high(r):
        lev, tiles, _, first, _, _, _, slot = routes[r]

        @pl.when(reads(lev))
        def _():
            parts_in(r)
            total = parts[slot, 0, tiles]
            for f in range(1, first):
                total = total + parts[slot, f, tiles]
            u[lev - nb, tiles] = total

    for r in high_ways:
        sum_high(r)

    coef[...] = jnp.zeros((8, 128), F32)
    for d in reversed(range(1, groups)):

        @pl.when(group - d >= 0)
        def _():
            level = high_level(group, group - d, nz)
            grad = u[level]
            z_out[d, 0:4] = grad
            z_out[d, 4] = coef[...]
            remote(
                z_out.at[d], zu.at[group], u_send.at[d], u_recv.at[group], (group - d, me)
            ).start()
            coef[...] = coef[...] + before_far[d] * jnp.sum(grad * zb[group - d, 0:4], axis=0)

    for r in low_ways:
        gather_back(r)

    for p in range(columns):
        total = jnp.zeros((heads, TOK), F32)
        for b in range(1 + levels):
            total = total + jnp.where(ids[b] == p, glam[b], 0.0)
        dlam_ref[p] = total
    even = jnp.where(core == 0, 1.0, 0.0)
    dlogt_ref[...] += (
        dot(pulls + rnear[...], (row >= col).astype(F32), precision=highest) - even * rsum
    )
    dqi = (dq_acc[:, 0:128] + dq_acc[:, 128:256]).astype(BF16).astype(F32)
    dst = dsc[...]
    dqt_ref[...] = dqi + dot(kt, dst, precision=highest)
    dkt_ref[...] = dot(dst, q, precision=highest).T
    for i in range(1, 5):
        results[i].start()

    for r in low_ways:
        lev, tiles, rows_first, first, second, users, arrays, slot = routes[r]
        parts_in(r)
        for a in range(len(arrays)):
            if rows_first:
                for f in range(first):
                    dn[offs[lev] + f * (ydim >> lev) + 2 * a, 0:4] = parts[slot + a, f]
            else:
                total = parts[slot + a, 0]
                for f in range(1, first):
                    total = total + parts[slot + a, f]
                dn[offs[lev] + 2 * a, 0:4] = total

    coef[...] = jnp.ones((8, 128), F32)
    dn[top, 0:4] = jnp.zeros((4, 8, 128), F32)
    cown[...] = jnp.zeros((8, 128), F32)
    for l in range(nz):

        @pl.when(bit_of(group, l))
        def _():
            cown[...] = cown[...] + jnp.sum(u[l] * hz[l], axis=0)

    for d in range(1, groups):

        @pl.when(group + d < groups)
        def _():
            far = zb.at[group + d, 4]
            near(far, far, z_send.at[0], z_recv.at[group + d]).wait_recv()
            slot = zu.at[group + d]
            near(slot, slot, u_send.at[d], u_recv.at[group + d]).wait_recv()
            dn[top, 0:4] = dn[top, 0:4] + coef[...][None] * zu[group + d, 0:4]
            cown[...] = cown[...] + zu[group + d, 4]
            coef[...] = coef[...] * zb[group + d, 4]

    loads[6].wait()
    fu = jnp.concatenate([fu_ref[0], fu_ref[1]], axis=1).reshape(4, 8, 128)
    dn[top, 0:4] = dn[top, 0:4] + coef[...][None] * fu
    earlier = hz[0]
    for l in range(1, nz):
        earlier = earlier + hz[l]
    carry = cown[...] + coef[...] * nd[top, 4] * jnp.sum(earlier * fu, axis=0)
    for b in reversed(range(nb)):
        for i in range(0, chips >> b, 2):
            left = offs[b] + i
            parent = dn[offs[b + 1] + i // 2, 0:4]
            dn[left, 0:4] = dn[left, 0:4] + nd[left + 1, 4][None] * parent
            dn[left + 1, 0:4] = parent

    t_part = rr.at[pl.ds(0, chips - 1)]
    sums_in = near(t_part, t_part, t_sem.at[0], t_sem.at[1])
    sums_in.wait_recv()
    now = jnp.sum(carry, axis=0, keepdims=True)
    for c in range(chips):
        step = jnp.sum(nd[c, 0:4] * dn[c, 0:4], axis=0) - rr[c]
        then = now + jnp.sum(step, axis=0, keepdims=True)
        dn[c, 4] = jnp.where(sub == 0, now, jnp.where(sub == 1, then, 0.0))
        now = then

    def give(i, half):
        to = shifted(i)
        remote(
            dn.at[to],
            ds.at[core, half, i % split_at],
            o_sem.at[0],
            o_sem.at[1 + half],
            (group, 2 * to + core),
        ).start()

    split_at = chips // 2
    loop(1, split_at, lambda i: give(i, 0))
    loop(split_at, chips, lambda i: give(i, 1))
    ds[core, 0, 0] = dn[chip, 0:5]
    if split_at > 1:
        part = ds.at[core, 0, pl.ds(0, split_at - 1)]
        near(part, part, o_sem.at[0], o_sem.at[1]).wait_recv()
    near(ds.at[core, 0], ds.at[core, 0], w_sem.at[0], w_sem.at[1]).start()
    part = ds.at[core, 1]
    near(part, part, o_sem.at[0], o_sem.at[2]).wait_recv()
    near(part, part, w_sem.at[2], w_sem.at[3]).start()

    def all_sent(r):
        lev, tiles, rows_first, first, second, users, arrays, slot = routes[r]

        def out_of_ring(count):
            if count:
                part = h.at[lev, core, pl.ds(0, count * first), tiles]
                near(part, part, h_send.at[r], h_recv.at[r]).wait_send()

        def sends():
            if first > 1:
                for a in range(len(arrays)):
                    part = ring.at[slot + a, pl.ds(0, first - 1), tiles]
                    near(part, part, r_send.at[slot + a], r_recv.at[slot + a]).wait_send()
                    near(part, part, q_send.at[slot + a], q_recv.at[slot + a]).wait_send()
            if lev >= nb:
                out_of_ring(second - 1)

        when_level(lev, sends)

        if lev < nb:

            @pl.when(jnp.logical_not(reads(lev)))
            def _():
                out_of_ring(len(users))

        @pl.when(reads(lev))
        def _():
            if lev < nb:
                out_of_ring(len(users) - 1)
            if second > 1:
                part = st.at[lev, pl.ds(0, (second - 1) * first), tiles]
                near(part, part, b_send.at[r], b_recv.at[r]).wait_send()

    for r in range(len(routes)):
        all_sent(r)
    for lev in range(levels):

        @pl.when(reads(lev))
        def _():
            ours = h.at[lev, core]
            near(ours, ours, f_send.at[lev], f_recv.at[lev]).wait_send()
            swap(lev).wait_send()

    for d in range(1, groups):

        @pl.when(group + d < groups)
        def _():
            up(d).wait_send()

        @pl.when(group - d >= 0)
        def _():
            line = nd.at[top, 4]
            near(line, line, z_send.at[groups + d], z_recv.at[0]).wait_send()
            near(z_out.at[d], z_out.at[d], u_send.at[d], u_recv.at[0]).wait_send()

    swap_half.wait_send()
    swap_dec.wait_send()
    scattered.wait_send()
    scales_in.wait_send()
    sums_in.wait_send()

    @pl.when(core == 1)
    def _():
        g0_copy.wait_send()

    @pl.when(core == 0)
    def _():
        rest.wait_send()
        g0_copy.wait_recv()

    part = dn.at[pl.ds(0, chips - 1)]
    near(part, part, o_sem.at[0], o_sem.at[1]).wait_send()

    def finish(half, i):
        at = i + half * split_at
        p = ((xpos + xdim - at // ydim) % xdim) * ydim + (ypos + ydim - at % ydim) % ydim
        scale = jnp.where(core == 0, sibd[p], jnp.ones((8, 128), F32))
        dld = jnp.zeros((8, 128), F32)
        lows = []
        for j in range(2):
            grad = ds[j, half, i, 0:4]
            dot_own = jnp.sum(own[p, j] * grad, axis=0)
            dld = dld + jnp.where(sub == core, ds[j, half, i, 4], 0.0)
            dld = dld - jnp.where(core == 0, 0.0, dot_own)
            extra = jnp.where(core == 0, g0[p, j], 0.0)
            lows.append(grad * scale[None] + extra)
        low_ref[p] = jnp.concatenate(lows, axis=0).reshape(64, 128).astype(BF16)
        dld_ref[pl.ds(p, 1), :] = jnp.sum(dld, axis=0, keepdims=True)

    for half in range(2):
        theirs = ds.at[1 - core, half]
        both = near(theirs, theirs, w_sem.at[2 * half], w_sem.at[2 * half + 1])
        both.wait_recv()
        both.wait_send()
        loop(0, split_at, partial(finish, half))
    results[6].start()
    results[7].start()
    for c in results:
        c.wait()


def end_kernel(
    v_any,
    kt_any,
    crow_any,
    low_any,
    dld_any,
    dvp_any,
    dkp_any,
    dlogp_any,
    dqp_any,
    dlamp_any,
    dv_any,
    dk_any,
    dq_any,
    dlog_any,
    dlam_any,
    v_ref,
    kt_ref,
    crow_ref,
    low_ref,
    dld_ref,
    dvp_ref,
    dkp_ref,
    dlogp_ref,
    dlamp_ref,
    dv_ref,
    dk_ref,
    dlog_ref,
    dlam_ref,
    in_sem,
    out_sem,
):
    heads = crow_ref.shape[0]
    pairs = heads // 2
    columns = dlamp_ref.shape[0]
    loads = [
        pltpu.make_async_copy(a, b, in_sem.at[i])
        for i, (a, b) in enumerate(
            [
                (dlamp_any, dlamp_ref),
                (crow_any, crow_ref),
                (kt_any, kt_ref),
                (low_any, low_ref),
                (v_any, v_ref),
                (dvp_any, dvp_ref),
                (dld_any, dld_ref),
                (dkp_any, dkp_ref),
                (dlogp_any, dlogp_ref),
            ]
        )
    ]
    for c in loads:
        c.start()
    through = pltpu.make_async_copy(dqp_any, dq_any, out_sem.at[0])
    through.start()
    row = iota((TOK, TOK), 0)
    col = iota((TOK, TOK), 1)
    left = col < 64
    loads[0].wait()
    wide = min(128, columns * heads)
    per = wide // heads
    for j in range(columns // per):
        dlam_ref[:, j * wide : (j + 1) * wide] = (
            dlamp_ref[pl.ds(j * per, per)].reshape(wide, TOK).T
        )
    lam_out = pltpu.make_async_copy(dlam_ref, dlam_any, out_sem.at[1])
    lam_out.start()
    loads[1].wait()
    ccol = crow_ref[...].T
    tail = jnp.exp(ccol[TOK - 1 : TOK, :] - ccol)
    loads[2].wait()
    k_low = kt_ref[...].T.astype(BF16)
    dk = jnp.zeros((64, TOK), F32)
    ls = jnp.zeros((TOK, heads), F32)
    lane_row = iota((TOK, heads), 0)
    lane_col = iota((TOK, heads), 1)
    for i in range(3, 9):
        loads[i].wait()
    parts = []
    for p in range(pairs):
        sl = slice(p * 128, (p + 1) * 128)
        pick = (lane_col == 2 * p + lane_row // 64).astype(F32)
        low = low_ref[p]
        scale = jnp.where(left, tail[:, 2 * p : 2 * p + 1], tail[:, 2 * p + 1 : 2 * p + 2])
        vp = v_ref[:, sl].astype(F32)
        dvs = scale * dot(k_low, low)
        decayed = (scale * vp).astype(BF16)
        dk += lax.dot_general(
            low, decayed, (((1,), (1,)), ((), ())), preferred_element_type=F32
        )
        dv_ref[:, sl] = (dvp_ref[:, sl] + dvs).astype(BF16)
        ls += dot((vp * dvs).astype(BF16), pick.astype(BF16))
        if (p + 1) % (pairs // 2) == 0:
            cols = pl.ds((p + 1 - pairs // 2) * 128, pairs // 2 * 128)
            parts.append(
                pltpu.make_async_copy(
                    dv_ref.at[:, cols], dv_any.at[:, cols], out_sem.at[4 + len(parts)]
                )
            )
            parts[-1].start()
    dk_ref[...] = dkp_ref[...] + dk
    k_out = pltpu.make_async_copy(dk_ref, dk_any, out_sem.at[2])
    k_out.start()
    strict = (row > col).astype(F32)
    head = iota((heads, pairs), 0)
    rows = dot((iota((heads, pairs), 1) == head // 2).astype(F32), dld_ref[...], precision=highest)
    side = iota((heads, TOK), 1) // 64 == iota((heads, TOK), 0) % 2
    dd = jnp.sum(jnp.where(side, rows, 0.0), axis=1, keepdims=True)
    dlog_ref[...] = dlogp_ref[...] + dot(strict, ls, precision=highest).T + dd
    log_out = pltpu.make_async_copy(dlog_ref, dlog_any, out_sem.at[3])
    log_out.start()
    for c in [through, lam_out, k_out, log_out] + parts:
        c.wait()


def body(
    values, state_input, state_output, log_decay, level_lam, level_ids, upstream, final_upstream
):
    shards, groups = lax.axis_size("shard"), lax.axis_size("grp")
    chips = shards // 2
    nb, nz = log2(chips), log2(groups)
    levels = nb + nz
    heads = log_decay.shape[1]
    columns = level_lam.shape[1] // heads
    params = partial(pltpu.CompilerParams, vmem_limit_bytes=VMEM_CAP)
    dma = pltpu.SemaphoreType.DMA
    tile = (4, 8, 128)
    kt = state_input.T
    ydim = 2 ** ((nb + 1) // 2)
    routes = routes_of(nb, nz, chips // ydim, ydim)
    slots = sum(len(route[6]) for route in routes)
    count = len(routes)

    dv, dqt, dkt, dlam, dlogt, crow, low, dld = pl.pallas_call(
        partial(main_kernel, shards, groups),
        out_shape=(
            f32(TOK, heads * 64),
            f32(64, TOK),
            f32(64, TOK),
            f32(columns, heads, TOK),
            f32(heads, TOK),
            f32(heads, TOK),
            jax.ShapeDtypeStruct((chips, 64, 128), BF16),
            f32(chips, 128),
        ),
        in_specs=[pl.BlockSpec(memory_space=pltpu.SMEM)]
        + [pl.BlockSpec(memory_space=pl.ANY)] * 7,
        out_specs=(pl.BlockSpec(memory_space=pl.ANY),) * 8,
        scratch_shapes=[
            pltpu.VMEM((TOK, heads * 64), F32),
            pltpu.VMEM((64, TOK), F32),
            pltpu.VMEM((64, TOK), F32),
            pltpu.VMEM((columns, heads, TOK), F32),
            pltpu.VMEM((heads, TOK), F32),
            pltpu.VMEM((heads, TOK), F32),
            pltpu.VMEM((chips, 64, 128), BF16),
            pltpu.VMEM((chips, 128), F32),
            dma((8,)),
            pltpu.VMEM((TOK, heads * 64), BF16),
            pltpu.VMEM((TOK, heads * 64), BF16),
            pltpu.VMEM((64, TOK), F32),
            pltpu.VMEM((64, TOK), F32),
            pltpu.VMEM((heads, TOK), F32),
            pltpu.VMEM((TOK, columns * heads), F32),
            pltpu.VMEM((2, 32, 64), F32),
            dma((7,)),
            pltpu.VMEM((chips, 128, 256), BF16),
            pltpu.VMEM((chips, 256, 128), BF16),
            pltpu.VMEM((columns, heads, TOK), F32),
            pltpu.VMEM((1 + levels, heads, TOK), F32),
            pltpu.VMEM((heads, TOK), F32),
            pltpu.VMEM((heads, TOK), F32),
            pltpu.VMEM((64, 256), F32),
            pltpu.VMEM((TOK, TOK), F32),
            pltpu.VMEM((levels, 2, chips) + tile, F32),
            pltpu.VMEM((chips, 2) + tile, F32),
            pltpu.VMEM((chips, 2) + tile, F32),
            pltpu.VMEM((chips, 8, 128), F32),
            pltpu.VMEM((chips, 2) + tile, F32),
            pltpu.VMEM((chips, 8, 128), F32),
            pltpu.VMEM((chips, 5, 8, 128), F32),
            pltpu.VMEM((2 * chips, 5, 8, 128), F32),
            pltpu.VMEM((groups, 5, 8, 128), F32),
            pltpu.VMEM((nz,) + tile, F32),
            pltpu.VMEM((chips, 8, 128), F32),
            pltpu.VMEM((chips, 8, 128), F32),
            pltpu.VMEM((8, 128), F32),
            pltpu.VMEM((groups, 8, 128), F32),
            pltpu.VMEM((slots, ydim) + tile, F32),
            pltpu.VMEM((levels, 2, chips) + tile, F32),
            pltpu.VMEM((levels, chips) + tile, F32),
            pltpu.VMEM((levels, chips) + tile, F32),
            pltpu.VMEM((levels, ydim, ydim) + tile, F32),
            pltpu.VMEM((slots, ydim) + tile, F32),
            pltpu.VMEM((slots, ydim) + tile, F32),
            pltpu.VMEM((chips, 8, 128), F32),
            pltpu.VMEM((chips, 8, 128), F32),
            pltpu.VMEM((nz,) + tile, F32),
            pltpu.VMEM((groups, 5, 8, 128), F32),
            pltpu.VMEM((groups, 5, 8, 128), F32),
            pltpu.VMEM((8, 128), F32),
            pltpu.VMEM((2 * chips, 5, 8, 128), F32),
            pltpu.VMEM((2, 2, chips // 2, 5, 8, 128), F32),
            pltpu.VMEM((chips, 2) + tile, F32),
            dma((6,)),
            dma((2,)),
            dma((2 * groups,)),
            dma((groups,)),
            dma((2,)),
            dma((slots,)),
            dma((slots,)),
            dma((count,)),
            dma((count,)),
            dma((levels,)),
            dma((levels,)),
            dma((2,)),
            dma((levels,)),
            dma((levels,)),
            dma((count,)),
            dma((count,)),
            dma((slots,)),
            dma((slots,)),
            dma((2,)),
            dma((groups,)),
            dma((groups,)),
            dma((3,)),
            dma((4,)),
        ],
        compiler_params=params(collective_id=0, has_side_effects=True),
        name="main",
    )(
        level_ids,
        values,
        upstream,
        kt,
        state_output.T,
        log_decay.T,
        level_lam,
        final_upstream.reshape(chips, 2, 2, 32, 64),
    )

    dv, dk, dq, dlog, dlam = pl.pallas_call(
        end_kernel,
        out_shape=(
            jax.ShapeDtypeStruct((TOK, heads * 64), BF16),
            f32(64, TOK),
            f32(64, TOK),
            f32(heads, TOK),
            f32(TOK, columns * heads),
        ),
        in_specs=[pl.BlockSpec(memory_space=pl.ANY)] * 10,
        out_specs=(pl.BlockSpec(memory_space=pl.ANY),) * 5,
        scratch_shapes=[
            pltpu.VMEM((TOK, heads * 64), BF16),
            pltpu.VMEM((64, TOK), F32),
            pltpu.VMEM((heads, TOK), F32),
            pltpu.VMEM((chips, 64, 128), BF16),
            pltpu.VMEM((chips, 128), F32),
            pltpu.VMEM((TOK, heads * 64), F32),
            pltpu.VMEM((64, TOK), F32),
            pltpu.VMEM((heads, TOK), F32),
            pltpu.VMEM((columns, heads, TOK), F32),
            pltpu.VMEM((TOK, heads * 64), BF16),
            pltpu.VMEM((64, TOK), F32),
            pltpu.VMEM((heads, TOK), F32),
            pltpu.VMEM((TOK, columns * heads), F32),
            dma((9,)),
            dma((6,)),
        ],
        compiler_params=params(),
        name="end",
    )(values, kt, crow, low, dld, dv, dkt, dlogt, dqt, dlam)
    return (dv, dk.T, dq.T, dlog.T, dlam)


def solution(mesh):
    spec = P(("grp", "shard"), None)
    return jax.shard_map(
        body,
        mesh=mesh,
        in_specs=(spec,) * 7 + (P(),),
        out_specs=(spec,) * 5,
        check_vma=False,
    )
```

```python
from functools import partial

import jax
import jax.numpy as jnp
from jax import lax
from jax.experimental import pallas as pl
from jax.experimental.pallas import tpu as pltpu
from jax.sharding import PartitionSpec as P

highest = lax.Precision.HIGHEST
MESH = pl.DeviceIdType.MESH
F32 = jnp.float32
BF16 = jnp.bfloat16
TOK = 128
VMEM_CAP = 62 * 1024 * 1024


def log2(n):
    return n.bit_length() - 1


def f32(*shape):
    return jax.ShapeDtypeStruct(shape, F32)


def iota(shape, dim):
    return lax.broadcasted_iota(jnp.int32, shape, dim)


def dot(a, b, **kw):
    return jnp.dot(a, b, preferred_element_type=F32, **kw)


def place():
    group = lax.axis_index("grp")
    me = lax.axis_index("shard")
    return group, me, me // 2, me % 2


def remote(src, dst, send, recv, device):
    return pltpu.make_async_remote_copy(
        src_ref=src, dst_ref=dst, send_sem=send, recv_sem=recv, device_id=device, device_id_type=MESH
    )


def loop(start, stop, fn):
    def step(i, carry):
        fn(i)
        return carry

    lax.fori_loop(start, stop, step, 0)


def enter(group, me, chip, core, chips, groups):
    barrier = pltpu.get_barrier_semaphore()

    def greet(shard, grp):
        pl.semaphore_signal(barrier, inc=1, device_id=(grp, shard), device_id_type=MESH)

    loop(1, chips, lambda d: greet(2 * ((chip + d) % chips) + core, group))
    loop(1, groups, lambda d: greet(me, (group + d) % groups))
    greet(me + 1 - 2 * core, group)
    return lambda: pl.semaphore_wait(barrier, chips + groups - 1)


def offsets(chips):
    offs, at, n = [], 0, chips
    while n >= 1:
        offs.append(at)
        at += n
        n //= 2
    return offs


def high_level(group, far, bits):
    level = jnp.int32(0)
    for b in range(1, bits):
        level = jnp.where(group // 2**b != far // 2**b, jnp.int32(b), level)
    return level


def bit_of(x, b):
    return (x // 2**b) % 2 == 1


def routes_of(nb, nz, xdim, ydim):
    routes, slot = [], 0
    ybits = log2(ydim)
    split = nb + min(1, nz - 1)
    for lev in range(nb + nz):
        if lev == split:
            ways = [(0, 2, True), (2, 4, False)]
        else:
            ways = [(0, 4, lev < ybits or nb <= lev < split)]
        for t0, t1, rows_first in ways:
            first, second = (xdim, ydim) if rows_first else (ydim, xdim)
            if lev < nb:
                bit = lev if rows_first else lev - ybits
                users = [s for s in range(second) if (s >> bit) & 1]
                arrays = [
                    [s for s in users if s >> (bit + 1) == a] for a in range(second >> (bit + 1))
                ]
            else:
                users = list(range(second))
                arrays = [users]
            routes.append((lev, slice(t0, t1), rows_first, first, second, users, arrays, slot))
            slot += len(arrays)
    return routes


def main_kernel(
    shards,
    groups,
    ids_ref,
    v_any,
    do_any,
    kt_any,
    qt_any,
    ldt_any,
    lam_any,
    fu_any,
    dv_any,
    dkt_any,
    dqt_any,
    dlogt_any,
    dlam_any,
    dv_out,
    dkt_ref,
    dqt_ref,
    dlogt_ref,
    dlam_ref,
    out_sem,
    dv_ref,
    crow_ref,
    dld_ref,
    tails,
    decayed,
    lrow,
    v_ref,
    do_ref,
    kt_ref,
    qt_ref,
    ldt_ref,
    lam_ref,
    fu_ref,
    in_sem,
    bd_t,
    bd,
    lam_t,
    glam,
    rint,
    rnear,
    dq_acc,
    dsc,
    g,
    gn,
    own,
    dec,
    sib,
    sibd,
    blk,
    nd,
    zb,
    hz,
    pks,
    pk,
    coef,
    before_far,
    ring,
    h,
    x,
    st,
    back,
    q_sum,
    parts,
    rs,
    rr,
    u,
    zu,
    z_out,
    cown,
    dn,
    ds,
    g0,
    s_sem,
    a_sem,
    z_send,
    z_recv,
    k_sem,
    r_send,
    r_recv,
    h_send,
    h_recv,
    f_send,
    f_recv,
    g0_sem,
    x_send,
    x_recv,
    b_send,
    b_recv,
    q_send,
    q_recv,
    t_sem,
    u_send,
    u_recv,
    o_sem,
    w_sem,
):
    chips = shards // 2
    pairs = chips
    heads = shards
    nb, nz = log2(chips), log2(groups)
    levels = nb + nz
    columns = lam_t.shape[0]
    ydim = 2 ** ((nb + 1) // 2)
    xdim = chips // ydim
    group, me, chip, core = place()
    mate = me + 1 - 2 * core
    xpos, ypos = chip // ydim, chip % ydim
    offs = offsets(chips)
    top = offs[nb]
    wide = min(128, columns * heads)
    per = wide // heads

    routes = routes_of(nb, nz, xdim, ydim)
    ways = [[r for r in range(len(routes)) if routes[r][0] == lev] for lev in range(levels)]

    def shifted(i):
        return ((xpos + i // ydim) % xdim) * ydim + (ypos + i % ydim) % ydim

    def near(src, dst, send, recv):
        return remote(src, dst, send, recv, (group, mate))

    loads = [
        pltpu.make_async_copy(a, b, in_sem.at[i])
        for i, (a, b) in enumerate(
            [
                (ldt_any, ldt_ref),
                (kt_any, kt_ref),
                (v_any, v_ref),
                (do_any, do_ref),
                (qt_any, qt_ref),
                (lam_any, lam_ref),
                (fu_any.at[chip, :, core], fu_ref),
            ]
        )
    ]
    for c in loads:
        c.start()
    results = [
        pltpu.make_async_copy(a, b, out_sem.at[i])
        for i, (a, b) in enumerate(
            [
                (dkt_ref, dkt_any),
                (dqt_ref, dqt_any),
                (dlogt_ref, dlogt_any),
                (dlam_ref, dlam_any),
            ]
        )
    ]
    wait_entry = enter(group, me, chip, core, chips, groups)

    row = iota((TOK, TOK), 0)
    col = iota((TOK, TOK), 1)
    upto = (row <= col).astype(F32)
    half = (col < 64).astype(F32)
    m0 = half.astype(BF16)
    m1 = (1.0 - half).astype(BF16)
    loads[0].wait()
    crow = dot(ldt_ref[...], upto, precision=highest)
    crow_ref[...] = crow
    last = jnp.broadcast_to(crow[:, TOK - 1 : TOK], (heads, TOK))
    tail = jnp.exp(last - crow)
    full = jnp.exp(last)
    loads[1].wait()
    kt = kt_ref[...]
    loads[2].wait()
    for p in range(pairs):
        k2 = jnp.concatenate(
            [kt * tail[2 * p : 2 * p + 1], kt * tail[2 * p + 1 : 2 * p + 2]], axis=1
        ).astype(BF16)
        vp = v_ref[:, p * 128 : (p + 1) * 128]
        s = dot(k2, jnp.concatenate([vp * m0, vp * m1], axis=0))
        own[p] = s.reshape(2, 4, 8, 128)
        dec[p] = (
            half[0:8] * full[2 * p : 2 * p + 1] + (1.0 - half[0:8]) * full[2 * p + 1 : 2 * p + 2]
        )

    wait_entry()
    swap_half = near(own.at[:, 1 - core], sib.at[:, 1 - core], s_sem.at[0], s_sem.at[1])
    swap_dec = near(dec, sibd, s_sem.at[2], s_sem.at[3])
    rest = near(own.at[:, core], sib.at[:, core], s_sem.at[4], s_sem.at[5])
    swap_half.start()
    swap_dec.start()

    @pl.when(core == 0)
    def _():
        rest.start()

    swap_dec.wait_recv()
    swap_half.wait_recv()

    def merge_cores(p):
        a = own[p, core]
        b = sib[p, core]
        left = jnp.where(core == 0, a, b)
        right = jnp.where(core == 0, b, a)
        drow = jnp.where(core == 0, sibd[p], dec[p])
        blk[p, 0:4] = drow[None] * left + right
        blk[p, 4] = dec[p] * sibd[p]

    loop(0, pairs, merge_cores)

    def scatter(i):
        to = shifted(i)
        remote(
            blk.at[to], nd.at[chip], a_sem.at[0], a_sem.at[1], (group, 2 * to + core)
        ).start()

    loop(1, chips, scatter)
    nd[chip] = blk[chip]

    loads[3].wait()
    loads[4].wait()
    qt = qt_ref[...]
    q = qt.T
    k = kt.T
    ccol = crow.T
    causal = row <= col
    scores = jnp.where(causal, dot(k, qt, precision=highest), 0.0)
    b_col = jnp.exp(ccol[TOK // 2 - 1 : TOK // 2, :] - ccol)
    a_row = jnp.exp(crow - crow[:, TOK // 2 - 1 : TOK // 2])
    suffix = (row >= col).astype(F32).astype(BF16)
    before = row < col
    t0 = (row < 64).astype(F32).astype(BF16)
    t1 = (row >= 64).astype(F32).astype(BF16)
    dsc[...] = jnp.zeros(dsc.shape, F32)

    def inside(p):
        sl = slice(p * 128, (p + 1) * 128)
        dop = do_ref[:, sl]
        dot_t = dop.astype(F32).T.astype(BF16)
        bdt = jnp.concatenate([dot_t * t0, dot_t * t1], axis=1)
        bdo = jnp.concatenate([dop * m0, dop * m1], axis=0)
        bd_t[p] = bdt
        bd[p] = bdo
        dmix = dot(v_ref[:, sl], bdt)
        xs = []
        for j in range(2):
            head = 2 * p + j
            dm = dmix[:, j * 128 : (j + 1) * 128]
            e = jnp.where(causal, b_col[:, head : head + 1] * a_row[head : head + 1, :], 0.0)
            mix = e * scores
            dsc[...] += e * dm
            y = dot((mix * dm).astype(BF16), suffix)
            dlogt_ref[head : head + 1, :] = jnp.sum(
                jnp.where(before, y, 0.0), axis=0, keepdims=True
            )
            xs.append(mix.astype(BF16))
        dv_ref[:, sl] = dot(jnp.concatenate(xs, axis=1), bdo)

    for p in range(pairs // 2):
        inside(p)

    part = nd.at[pl.ds(0, chips - 1)]
    scattered = near(part, part, a_sem.at[0], a_sem.at[1])
    scattered.wait_recv()
    for b in range(1, nb + 1):
        for i in range(chips >> b):
            lo = offs[b - 1] + 2 * i
            right = nd[lo + 1, 4]
            nd[offs[b] + i, 0:4] = right[None] * nd[lo, 0:4] + nd[lo + 1, 0:4]
            nd[offs[b] + i, 4] = right * nd[lo, 4]

    def up(d):
        return remote(
            nd.at[top], zb.at[group], z_send.at[d], z_recv.at[group], (group + d, me)
        )

    def down(d):
        return remote(
            nd.at[top, 4], zb.at[group, 4], z_send.at[d], z_recv.at[group], (group - d, me)
        )

    for d in range(1, groups):

        @pl.when(group + d < groups)
        def _():
            up(d).start()

    for d in range(1, groups):

        @pl.when(group - d >= 0)
        def _():
            remote(
                nd.at[top, 4],
                zb.at[group, 4],
                z_send.at[groups + d],
                z_recv.at[group],
                (group - d, me),
            ).start()

    sub = iota((8, 128), 0)
    for c in range(chips):
        pre = jnp.ones((8, 128), F32)
        rows = pre
        for b in range(nb):
            rows = jnp.where(sub >= b, pre, rows)
            if (c >> b) & 1:
                pre = pre * nd[offs[b] + (c >> b) - 1, 4]
        pks[c] = jnp.where(sub >= nb, pre, rows)

    def send_scales(i):
        to = shifted(i)
        remote(
            pks.at[to], pk.at[chip], k_sem.at[0], k_sem.at[1], (group, 2 * to + core)
        ).start()

    loop(1, chips, send_scales)
    pk[chip] = pks[chip]

    def where_on(r):
        if routes[r][2]:
            return xpos, ypos, lambda f, s: f * ydim + s
        return ypos, xpos, lambda f, s: s * ydim + f

    def reads(lev):
        if lev >= nb:
            return bit_of(group, lev - nb)
        return bit_of(chip, lev)

    def when_level(lev, fn):
        if lev >= nb:
            pl.when(bit_of(group, lev - nb))(fn)
        else:
            fn()

    def first_phase(r):
        lev, tiles, rows_first, first, second, users, arrays, slot = routes[r]
        fpos, spos, at = where_on(r)

        def source(a, f):
            if lev >= nb:
                return hz.at[lev - nb, tiles]
            if rows_first:
                return nd.at[offs[lev] + f * (ydim >> lev) + 2 * a, 0:4]
            return nd.at[offs[lev] + 2 * a, 0:4]

        def go():
            for d in range(1, first):
                f = (fpos + d) % first
                for a in range(len(arrays)):
                    remote(
                        source(a, f),
                        ring.at[slot + a, fpos, tiles],
                        r_send.at[slot + a],
                        r_recv.at[slot + a],
                        (group, 2 * at(f, spos) + core),
                    ).start()
            for a in range(len(arrays)):
                ring[slot + a, fpos, tiles] = source(a, fpos)[...]

        if lev >= nb:
            go()
        else:
            when_level(lev, go)

    def second_phase(r):
        lev, tiles, rows_first, first, second, users, arrays, slot = routes[r]
        fpos, spos, at = where_on(r)

        def go():
            if first > 1:
                for a in range(len(arrays)):
                    part = ring.at[slot + a, pl.ds(0, first - 1), tiles]
                    near(part, part, r_send.at[slot + a], r_recv.at[slot + a]).wait_recv()
            for a, readers in enumerate(arrays):
                for s in readers:
                    there = h.at[lev, core, pl.ds(spos * first, first), tiles]

                    @pl.when(spos != s)
                    def _():
                        remote(
                            ring.at[slot + a, pl.ds(0, first), tiles],
                            there,
                            h_send.at[r],
                            h_recv.at[r],
                            (group, 2 * at(fpos, s) + core),
                        ).start()

                    @pl.when(spos == s)
                    def _():
                        there[...] = ring[slot + a, 0:first, tiles]

        when_level(lev, go)

    low = list(range(nb))
    high = list(range(nb, levels))
    low_ways = [r for lev in low for r in ways[lev]]
    high_ways = [r for lev in high for r in ways[lev]]
    for r in low_ways:
        first_phase(r)

    for p in range(pairs // 2, 3 * pairs // 4):
        inside(p)
    for r in low_ways:
        second_phase(r)
    for p in range(3 * pairs // 4, pairs):
        inside(p)

    coef[...] = jnp.ones((8, 128), F32)
    hz[...] = jnp.zeros(hz.shape, F32)
    for d in range(1, groups):
        far = group - d

        @pl.when(far >= 0)
        def _():
            slot = zb.at[far]
            near(slot, slot, z_send.at[0], z_recv.at[far]).wait_recv()
            level = high_level(group, far, nz)
            hz[level] = hz[level] + coef[...][None] * zb[far, 0:4]
            before_far[d] = coef[...]
            coef[...] = coef[...] * zb[far, 4]

        l = log2(d)

        @pl.when(bit_of(group, l) & (group % 2**l + 2**l == d))
        def _():
            for r in ways[nb + l]:
                first_phase(r)

    q_low = qt.astype(BF16).astype(F32)
    q2 = jnp.concatenate([q_low, q_low], axis=1)
    loads[5].wait()
    for j in range(columns // per):
        lam_t[pl.ds(j * per, per)] = lam_ref[:, j * wide : (j + 1) * wide].T.reshape(
            per, heads, TOK
        )
    glam[...] = jnp.zeros(glam.shape, F32)
    rint[...] = jnp.zeros(rint.shape, F32)
    rnear[...] = jnp.zeros(rnear.shape, F32)
    dq_acc[...] = jnp.zeros(dq_acc.shape, F32)
    ids = [ids_ref[0, b] for b in range(1 + levels)]

    def spot(r, p):
        if routes[r][2]:
            return (p % ydim) * xdim + p // ydim
        return p

    def levels_step(group_levels, p):
        gr2 = jnp.exp(crow_ref[pl.ds(2 * p, 2), :])
        mate_scale = jnp.where(core == 1, sibd[p, 0:1], jnp.ones((1, 128), F32))
        helds, ws, scales = [], [], []
        for b in group_levels:
            if b == 0:
                held = sib[p].reshape(64, 128)
                scales.append(None)
            else:
                scales.append(mate_scale * pk[p, b - 1 : b])
                held = jnp.concatenate(
                    [h[b - 1, j, spot(r, p), routes[r][1]] for j in range(2) for r in ways[b - 1]],
                    axis=0,
                )
                held = jnp.where(reads(b - 1), held.reshape(64, 128) * scales[-1], 0.0)
            helds.append(held.astype(BF16))
            ws.append(lam_t[ids[b], pl.ds(2 * p, 2), :] * gr2)
        m = dot(jnp.concatenate(helds, axis=0), bd_t[p])
        wqs = []
        acc = dq_acc[...]
        r2 = jnp.zeros((2, TOK), F32)
        for i, b in enumerate(group_levels):
            mi = m[64 * i : 64 * (i + 1)]
            w = jnp.concatenate([ws[i][0:1], ws[i][1:2]], axis=1)
            gsum = jnp.sum(q2 * mi, axis=0, keepdims=True)
            acc = acc + w * mi
            wqs.append((w * q2).astype(BF16))
            g2 = jnp.concatenate([gsum[:, 0:128], gsum[:, 128:256]], axis=0)
            glam[b, pl.ds(2 * p, 2), :] = gr2 * g2
            r2 = r2 + ws[i] * g2
        dq_acc[...] = acc
        if group_levels == [0]:
            rnear[pl.ds(2 * p, 2), :] = r2
        else:
            rint[pl.ds(2 * p, 2), :] += r2
        grad = dot(jnp.concatenate(wqs, axis=0), bd[p])
        for i, b in enumerate(group_levels):
            gi = grad[64 * i : 64 * (i + 1)]
            if b == 0:
                gn[p] = gi.reshape(2, 4, 8, 128)
            else:
                gi = (gi * scales[i]).reshape(2, 4, 8, 128)
                for r in ways[b - 1]:
                    tiles = routes[r][1]
                    for j in range(2):
                        g[b - 1, j, spot(r, p), tiles] = gi[j, tiles]

    def levels_pass(group_levels):
        def two(i):
            levels_step(group_levels, 2 * i)
            levels_step(group_levels, 2 * i + 1)

        loop(0, pairs // 2, two)

    g0_copy = near(gn, g0, g0_sem.at[0], g0_sem.at[1])

    @pl.when(core == 1)
    def _():
        rest.wait_recv()
        levels_pass([0])
        g0_copy.start()

    for r in high_ways:
        second_phase(r)

    def swap(lev):
        return near(g.at[lev, 1 - core], x.at[lev], x_send.at[lev], x_recv.at[lev])

    def fetch(levs):
        for lev in levs:

            @pl.when(reads(lev))
            def _():
                for r in ways[lev]:
                    _, tiles, _, first, second, _, _, _ = routes[r]
                    if second > 1:
                        part = h.at[lev, core, pl.ds(0, (second - 1) * first), tiles]
                        near(part, part, h_send.at[r], h_recv.at[r]).wait_recv()
                ours = h.at[lev, core]
                near(ours, ours, f_send.at[lev], f_recv.at[lev]).start()

        for lev in levs:

            @pl.when(reads(lev))
            def _():
                theirs = h.at[lev, 1 - core]
                near(theirs, theirs, f_send.at[lev], f_recv.at[lev]).wait_recv()

    def give_back(levs):
        for lev in levs:

            @pl.when(reads(lev))
            def _():
                swap(lev).start()

        def send_back(r):
            lev, tiles, _, first, second, _, _, _ = routes[r]
            fpos, spos, at = where_on(r)
            for d in range(1, second):
                s = (spos + d) % second
                remote(
                    st.at[lev, pl.ds(s * first, first), tiles],
                    back.at[lev, spos, pl.ds(0, first), tiles],
                    b_send.at[r],
                    b_recv.at[r],
                    (group, 2 * at(fpos, s) + core),
                ).start()
            back[lev, spos, 0:first, tiles] = st[lev, pl.ds(spos * first, first), tiles]

        for lev in levs:

            @pl.when(reads(lev))
            def _():
                swap(lev).wait_recv()

                def add(c):
                    st[lev, c] = g[lev, core, c] + x[lev, c]

                loop(0, chips, add)
                for r in ways[lev]:
                    send_back(r)

    def gather_back(r):
        lev, tiles, rows_first, first, second, users, arrays, slot = routes[r]
        fpos, spos, at = where_on(r)

        def arrived(count):
            if count:
                part = back.at[lev, pl.ds(0, count), pl.ds(0, first), tiles]
                near(part, part, b_send.at[r], b_recv.at[r]).wait_recv()

        def go():
            if lev >= nb:
                arrived(second - 1)
            else:

                @pl.when(reads(lev))
                def _():
                    arrived(len(users) - 1)

                @pl.when(jnp.logical_not(reads(lev)))
                def _():
                    arrived(len(users))

            for a, readers in enumerate(arrays):
                for f in range(first):
                    total = back[lev, readers[0], f, tiles]
                    for s in readers[1:]:
                        total = total + back[lev, s, f, tiles]
                    q_sum[slot + a, f, tiles] = total
                for d in range(1, first):
                    f = (fpos + d) % first
                    remote(
                        q_sum.at[slot + a, f, tiles],
                        parts.at[slot + a, fpos, tiles],
                        q_send.at[slot + a],
                        q_recv.at[slot + a],
                        (group, 2 * at(f, spos) + core),
                    ).start()
                parts[slot + a, fpos, tiles] = q_sum[slot + a, fpos, tiles]

        when_level(lev, go)

    def parts_in(r):
        lev, tiles, rows_first, first, second, users, arrays, slot = routes[r]
        if first > 1:
            for a in range(len(arrays)):
                part = parts.at[slot + a, pl.ds(0, first - 1), tiles]
                near(part, part, q_send.at[slot + a], q_recv.at[slot + a]).wait_recv()

    tail_col = jnp.exp(ccol[TOK - 1 : TOK, :] - ccol)
    for p in range(pairs):
        tails[p] = jnp.where(
            col < 64, tail_col[:, 2 * p : 2 * p + 1], tail_col[:, 2 * p + 1 : 2 * p + 2]
        )
        vp = v_ref[:, p * 128 : (p + 1) * 128].astype(F32)
        decayed[p] = (tails[p] * vp).astype(BF16)
    k_low = k.astype(BF16)
    kt_low = kt.astype(BF16).astype(F32)

    k_part = pk.at[pl.ds(0, chips - 1)]
    scales_in = near(k_part, k_part, k_sem.at[0], k_sem.at[1])
    scales_in.wait_recv()
    fetch(low)
    levels_pass([b + 1 for b in low])
    fetch(high)

    @pl.when(group > 0)
    def _():
        levels_pass([b + 1 for b in high])

    give_back(high)

    pulls = rint[...]
    rsum = jnp.broadcast_to(jnp.sum(pulls, axis=1, keepdims=True), (heads, TOK))
    lane = iota((8, 128), 1)
    first_lane = jnp.where((sub == 0) & (lane == 0), 1.0, 0.0)
    mid_lane = jnp.where((sub == 0) & (lane == 64), 1.0, 0.0)
    for p in range(pairs):
        rs[p] = first_lane * rsum[2 * p : 2 * p + 1] + mid_lane * rsum[2 * p + 1 : 2 * p + 2]

    def send_sums(i):
        to = shifted(i)
        remote(
            rs.at[to], rr.at[chip], t_sem.at[0], t_sem.at[1], (group, 2 * to + core)
        ).start()

    loop(1, chips, send_sums)
    rr[chip] = rs[chip]
    for r in high_ways:
        gather_back(r)
    give_back(low)

    def sum_high(r):
        lev, tiles, _, first, _, _, _, slot = routes[r]

        @pl.when(reads(lev))
        def _():
            parts_in(r)
            total = parts[slot, 0, tiles]
            for f in range(1, first):
                total = total + parts[slot, f, tiles]
            u[lev - nb, tiles] = total

    for r in high_ways:
        sum_high(r)

    coef[...] = jnp.zeros((8, 128), F32)
    for d in reversed(range(1, groups)):

        @pl.when(group - d >= 0)
        def _():
            level = high_level(group, group - d, nz)
            grad = u[level]
            z_out[d, 0:4] = grad
            z_out[d, 4] = coef[...]
            remote(
                z_out.at[d], zu.at[group], u_send.at[d], u_recv.at[group], (group - d, me)
            ).start()
            coef[...] = coef[...] + before_far[d] * jnp.sum(grad * zb[group - d, 0:4], axis=0)

    for r in low_ways:
        gather_back(r)

    for j in range(columns // per):
        slabs = []
        for p in range(j * per, (j + 1) * per):
            total = jnp.zeros((heads, TOK), F32)
            for b in range(1 + levels):
                total = total + jnp.where(ids[b] == p, glam[b], 0.0)
            slabs.append(total)
        dlam_ref[:, j * wide : (j + 1) * wide] = jnp.concatenate(slabs, axis=0).T
    results[3].start()
    even = jnp.where(core == 0, 1.0, 0.0)
    dlogt_ref[...] += (
        dot(pulls + rnear[...], (row >= col).astype(F32), precision=highest) - even * rsum
    )
    dqi = (dq_acc[:, 0:128] + dq_acc[:, 128:256]).astype(BF16).astype(F32)
    dst = dsc[...]
    dqt_ref[...] = dqi + dot(kt, dst, precision=highest)
    dkt_ref[...] = dot(dst, q, precision=highest).T
    results[1].start()

    for r in low_ways:
        lev, tiles, rows_first, first, second, users, arrays, slot = routes[r]
        parts_in(r)
        for a in range(len(arrays)):
            if rows_first:
                for f in range(first):
                    dn[offs[lev] + f * (ydim >> lev) + 2 * a, 0:4] = parts[slot + a, f]
            else:
                total = parts[slot + a, 0]
                for f in range(1, first):
                    total = total + parts[slot + a, f]
                dn[offs[lev] + 2 * a, 0:4] = total

    coef[...] = jnp.ones((8, 128), F32)
    dn[top, 0:4] = jnp.zeros((4, 8, 128), F32)
    cown[...] = jnp.zeros((8, 128), F32)
    for l in range(nz):

        @pl.when(bit_of(group, l))
        def _():
            cown[...] = cown[...] + jnp.sum(u[l] * hz[l], axis=0)

    for d in range(1, groups):

        @pl.when(group + d < groups)
        def _():
            far = zb.at[group + d, 4]
            near(far, far, z_send.at[0], z_recv.at[group + d]).wait_recv()
            slot = zu.at[group + d]
            near(slot, slot, u_send.at[d], u_recv.at[group + d]).wait_recv()
            dn[top, 0:4] = dn[top, 0:4] + coef[...][None] * zu[group + d, 0:4]
            cown[...] = cown[...] + zu[group + d, 4]
            coef[...] = coef[...] * zb[group + d, 4]

    loads[6].wait()
    fu = jnp.concatenate([fu_ref[0], fu_ref[1]], axis=1).reshape(4, 8, 128)
    dn[top, 0:4] = dn[top, 0:4] + coef[...][None] * fu
    earlier = hz[0]
    for l in range(1, nz):
        earlier = earlier + hz[l]
    carry = cown[...] + coef[...] * nd[top, 4] * jnp.sum(earlier * fu, axis=0)
    for b in reversed(range(nb)):
        for i in range(0, chips >> b, 2):
            left = offs[b] + i
            parent = dn[offs[b + 1] + i // 2, 0:4]
            dn[left, 0:4] = dn[left, 0:4] + nd[left + 1, 4][None] * parent
            dn[left + 1, 0:4] = parent

    t_part = rr.at[pl.ds(0, chips - 1)]
    sums_in = near(t_part, t_part, t_sem.at[0], t_sem.at[1])
    sums_in.wait_recv()
    now = jnp.sum(carry, axis=0, keepdims=True)
    for c in range(chips):
        step = jnp.sum(nd[c, 0:4] * dn[c, 0:4], axis=0) - rr[c]
        then = now + jnp.sum(step, axis=0, keepdims=True)
        dn[c, 4] = jnp.where(sub == 0, now, jnp.where(sub == 1, then, 0.0))
        now = then

    def give(i, half):
        to = shifted(i)
        remote(
            dn.at[to],
            ds.at[core, half, i % split_at],
            o_sem.at[0],
            o_sem.at[1 + half],
            (group, 2 * to + core),
        ).start()

    split_at = chips // 2
    loop(1, split_at, lambda i: give(i, 0))
    loop(split_at, chips, lambda i: give(i, 1))
    ds[core, 0, 0] = dn[chip, 0:5]
    if split_at > 1:
        part = ds.at[core, 0, pl.ds(0, split_at - 1)]
        near(part, part, o_sem.at[0], o_sem.at[1]).wait_recv()
    near(ds.at[core, 0], ds.at[core, 0], w_sem.at[0], w_sem.at[1]).start()
    part = ds.at[core, 1]
    near(part, part, o_sem.at[0], o_sem.at[2]).wait_recv()
    near(part, part, w_sem.at[2], w_sem.at[3]).start()

    def all_sent(r):
        lev, tiles, rows_first, first, second, users, arrays, slot = routes[r]

        def out_of_ring(count):
            if count:
                part = h.at[lev, core, pl.ds(0, count * first), tiles]
                near(part, part, h_send.at[r], h_recv.at[r]).wait_send()

        def sends():
            if first > 1:
                for a in range(len(arrays)):
                    part = ring.at[slot + a, pl.ds(0, first - 1), tiles]
                    near(part, part, r_send.at[slot + a], r_recv.at[slot + a]).wait_send()
                    near(part, part, q_send.at[slot + a], q_recv.at[slot + a]).wait_send()
            if lev >= nb:
                out_of_ring(second - 1)

        when_level(lev, sends)

        if lev < nb:

            @pl.when(jnp.logical_not(reads(lev)))
            def _():
                out_of_ring(len(users))

        @pl.when(reads(lev))
        def _():
            if lev < nb:
                out_of_ring(len(users) - 1)
            if second > 1:
                part = st.at[lev, pl.ds(0, (second - 1) * first), tiles]
                near(part, part, b_send.at[r], b_recv.at[r]).wait_send()

    for r in range(len(routes)):
        all_sent(r)
    for lev in range(levels):

        @pl.when(reads(lev))
        def _():
            ours = h.at[lev, core]
            near(ours, ours, f_send.at[lev], f_recv.at[lev]).wait_send()
            swap(lev).wait_send()

    for d in range(1, groups):

        @pl.when(group + d < groups)
        def _():
            up(d).wait_send()

        @pl.when(group - d >= 0)
        def _():
            line = nd.at[top, 4]
            near(line, line, z_send.at[groups + d], z_recv.at[0]).wait_send()
            near(z_out.at[d], z_out.at[d], u_send.at[d], u_recv.at[0]).wait_send()

    swap_half.wait_send()
    swap_dec.wait_send()
    scattered.wait_send()
    scales_in.wait_send()
    sums_in.wait_send()

    @pl.when(core == 1)
    def _():
        g0_copy.wait_send()

    @pl.when(core == 0)
    def _():
        rest.wait_send()
        g0_copy.wait_recv()

    part = dn.at[pl.ds(0, chips - 1)]
    near(part, part, o_sem.at[0], o_sem.at[1]).wait_send()

    def finish(a, i):
        at = a * ydim + i
        half, slot = at // split_at, at % split_at
        p = ((xpos + xdim - a) % xdim) * ydim + (ypos + ydim - i) % ydim
        scale = jnp.where(core == 0, sibd[p], jnp.ones((8, 128), F32))
        dld = jnp.zeros((8, 128), F32)
        lows = []
        for j in range(2):
            grad = ds[j, half, slot, 0:4]
            dot_own = jnp.sum(own[p, j] * grad, axis=0)
            dld = dld + jnp.where(sub == core, ds[j, half, slot, 4], 0.0)
            dld = dld - jnp.where(core == 0, 0.0, dot_own)
            extra = jnp.where(core == 0, g0[p, j], 0.0)
            lows.append(grad * scale[None] + extra)
        low = jnp.concatenate(lows, axis=0).reshape(64, 128).astype(BF16)
        dld_ref[pl.ds(p, 1), :] = jnp.sum(dld, axis=0, keepdims=True)
        cols = pl.ds(pl.multiple_of(p * 128, 128), 128)
        dv_out[:, cols] = (dv_ref[:, cols] + tails[p] * dot(k_low, low)).astype(BF16)
        both_heads = jnp.concatenate([low * m0[0:64], low * m1[0:64]], axis=0)
        dk = lax.dot_general(
            both_heads, decayed[p], (((1,), (1,)), ((), ())), preferred_element_type=F32
        )
        dkt_ref[...] += dk[0:64] + dk[64:128]
        lrow[pl.ds(2 * p, 1), :] = jnp.sum(kt_low * dk[0:64], axis=0, keepdims=True)
        lrow[pl.ds(2 * p + 1, 1), :] = jnp.sum(kt_low * dk[64:128], axis=0, keepdims=True)

    def half_in(half):
        theirs = ds.at[1 - core, half]
        both = near(theirs, theirs, w_sem.at[2 * half], w_sem.at[2 * half + 1])
        both.wait_recv()
        both.wait_send()

    for a in range(xdim):
        if a == 0:
            half_in(0)
        if a == xdim // 2:
            half_in(1)
        for i in range(ydim):
            finish(a, i)
        cols = pl.ds(pl.multiple_of(((xpos + xdim - a) % xdim) * ydim * 128, 128), ydim * 128)
        results.append(
            pltpu.make_async_copy(dv_out.at[:, cols], dv_any.at[:, cols], out_sem.at[4 + a])
        )
        results[-1].start()
    results[0].start()
    head = iota((heads, pairs), 0)
    rows = dot((iota((heads, pairs), 1) == head // 2).astype(F32), dld_ref[...], precision=highest)
    side = iota((heads, TOK), 1) // 64 == iota((heads, TOK), 0) % 2
    dd = jnp.sum(jnp.where(side, rows, 0.0), axis=1, keepdims=True)
    dlogt_ref[...] += dot(lrow[...], (row < col).astype(F32), precision=highest) + dd
    results[2].start()
    for c in results:
        c.wait()


def end_kernel(*refs):
    n = (len(refs) - 1) // 2
    sem = refs[-1]
    copies = []
    for i in range(n):
        src, dst = refs[i], refs[n + i]
        cuts = 4 if i == 0 else 1
        step = src.shape[0] // cuts
        for j in range(cuts):
            part = pl.ds(j * step, step)
            copies.append(
                pltpu.make_async_copy(src.at[part], dst.at[part], sem.at[len(copies)])
            )
    for c in copies:
        c.start()
    for c in copies:
        c.wait()


def body(
    values, state_input, state_output, log_decay, level_lam, level_ids, upstream, final_upstream
):
    shards, groups = lax.axis_size("shard"), lax.axis_size("grp")
    chips = shards // 2
    nb, nz = log2(chips), log2(groups)
    levels = nb + nz
    heads = log_decay.shape[1]
    columns = level_lam.shape[1] // heads
    params = partial(pltpu.CompilerParams, vmem_limit_bytes=VMEM_CAP)
    dma = pltpu.SemaphoreType.DMA
    tile = (4, 8, 128)
    kt = state_input.T
    ydim = 2 ** ((nb + 1) // 2)
    routes = routes_of(nb, nz, chips // ydim, ydim)
    slots = sum(len(route[6]) for route in routes)
    count = len(routes)

    shapes = (
        jax.ShapeDtypeStruct((TOK, heads * 64), BF16),
        f32(64, TOK),
        f32(64, TOK),
        f32(heads, TOK),
        f32(TOK, columns * heads),
    )
    anywhere = pl.BlockSpec(memory_space=pl.ANY)
    parts = pl.pallas_call(
        partial(main_kernel, shards, groups),
        out_shape=shapes,
        in_specs=[pl.BlockSpec(memory_space=pltpu.SMEM)]
        + [anywhere] * 7,
        out_specs=(anywhere,) * 5,
        scratch_shapes=[
            pltpu.VMEM((TOK, heads * 64), BF16),
            pltpu.VMEM((64, TOK), F32),
            pltpu.VMEM((64, TOK), F32),
            pltpu.VMEM((heads, TOK), F32),
            pltpu.VMEM((TOK, columns * heads), F32),
            dma((4 + chips // ydim,)),
            pltpu.VMEM((TOK, heads * 64), F32),
            pltpu.VMEM((heads, TOK), F32),
            pltpu.VMEM((chips, 128), F32),
            pltpu.VMEM((chips, TOK, 128), F32),
            pltpu.VMEM((chips, TOK, 128), BF16),
            pltpu.VMEM((heads, TOK), F32),
            pltpu.VMEM((TOK, heads * 64), BF16),
            pltpu.VMEM((TOK, heads * 64), BF16),
            pltpu.VMEM((64, TOK), F32),
            pltpu.VMEM((64, TOK), F32),
            pltpu.VMEM((heads, TOK), F32),
            pltpu.VMEM((TOK, columns * heads), F32),
            pltpu.VMEM((2, 32, 64), F32),
            dma((7,)),
            pltpu.VMEM((chips, 128, 256), BF16),
            pltpu.VMEM((chips, 256, 128), BF16),
            pltpu.VMEM((columns, heads, TOK), F32),
            pltpu.VMEM((1 + levels, heads, TOK), F32),
            pltpu.VMEM((heads, TOK), F32),
            pltpu.VMEM((heads, TOK), F32),
            pltpu.VMEM((64, 256), F32),
            pltpu.VMEM((TOK, TOK), F32),
            pltpu.VMEM((levels, 2, chips) + tile, F32),
            pltpu.VMEM((chips, 2) + tile, F32),
            pltpu.VMEM((chips, 2) + tile, F32),
            pltpu.VMEM((chips, 8, 128), F32),
            pltpu.VMEM((chips, 2) + tile, F32),
            pltpu.VMEM((chips, 8, 128), F32),
            pltpu.VMEM((chips, 5, 8, 128), F32),
            pltpu.VMEM((2 * chips, 5, 8, 128), F32),
            pltpu.VMEM((groups, 5, 8, 128), F32),
            pltpu.VMEM((nz,) + tile, F32),
            pltpu.VMEM((chips, 8, 128), F32),
            pltpu.VMEM((chips, 8, 128), F32),
            pltpu.VMEM((8, 128), F32),
            pltpu.VMEM((groups, 8, 128), F32),
            pltpu.VMEM((slots, ydim) + tile, F32),
            pltpu.VMEM((levels, 2, chips) + tile, F32),
            pltpu.VMEM((levels, chips) + tile, F32),
            pltpu.VMEM((levels, chips) + tile, F32),
            pltpu.VMEM((levels, ydim, ydim) + tile, F32),
            pltpu.VMEM((slots, ydim) + tile, F32),
            pltpu.VMEM((slots, ydim) + tile, F32),
            pltpu.VMEM((chips, 8, 128), F32),
            pltpu.VMEM((chips, 8, 128), F32),
            pltpu.VMEM((nz,) + tile, F32),
            pltpu.VMEM((groups, 5, 8, 128), F32),
            pltpu.VMEM((groups, 5, 8, 128), F32),
            pltpu.VMEM((8, 128), F32),
            pltpu.VMEM((2 * chips, 5, 8, 128), F32),
            pltpu.VMEM((2, 2, chips // 2, 5, 8, 128), F32),
            pltpu.VMEM((chips, 2) + tile, F32),
            dma((6,)),
            dma((2,)),
            dma((2 * groups,)),
            dma((groups,)),
            dma((2,)),
            dma((slots,)),
            dma((slots,)),
            dma((count,)),
            dma((count,)),
            dma((levels,)),
            dma((levels,)),
            dma((2,)),
            dma((levels,)),
            dma((levels,)),
            dma((count,)),
            dma((count,)),
            dma((slots,)),
            dma((slots,)),
            dma((2,)),
            dma((groups,)),
            dma((groups,)),
            dma((3,)),
            dma((4,)),
        ],
        compiler_params=params(collective_id=0, has_side_effects=True),
        name="main",
    )(
        level_ids,
        values,
        upstream,
        kt,
        state_output.T,
        log_decay.T,
        level_lam,
        final_upstream.reshape(chips, 2, 2, 32, 64),
    )

    dv, dk, dq, dlog, dlam = pl.pallas_call(
        end_kernel,
        out_shape=shapes,
        in_specs=[anywhere] * 5,
        out_specs=(anywhere,) * 5,
        scratch_shapes=[dma((8,))],
        compiler_params=params(),
        name="end",
    )(*parts)
    return (dv, dk.T, dq.T, dlog.T, dlam)


def solution(mesh):
    spec = P(("grp", "shard"), None)
    return jax.shard_map(
        body,
        mesh=mesh,
        in_specs=(spec,) * 7 + (P(),),
        out_specs=(spec,) * 5,
        check_vma=False,
    )
```

```python
from functools import partial

import jax
import jax.numpy as jnp
from jax import lax
from jax.experimental import pallas as pl
from jax.experimental.pallas import tpu as pltpu
from jax.sharding import PartitionSpec as P

highest = lax.Precision.HIGHEST
MESH = pl.DeviceIdType.MESH
F32 = jnp.float32
BF16 = jnp.bfloat16
TOK = 128
VMEM_CAP = 62 * 1024 * 1024


def log2(n):
    return n.bit_length() - 1


def f32(*shape):
    return jax.ShapeDtypeStruct(shape, F32)


def iota(shape, dim):
    return lax.broadcasted_iota(jnp.int32, shape, dim)


def dot(a, b, **kw):
    return jnp.dot(a, b, preferred_element_type=F32, **kw)


def place():
    group = lax.axis_index("grp")
    me = lax.axis_index("shard")
    return group, me, me // 2, me % 2


def remote(src, dst, send, recv, device):
    return pltpu.make_async_remote_copy(
        src_ref=src, dst_ref=dst, send_sem=send, recv_sem=recv, device_id=device, device_id_type=MESH
    )


def loop(start, stop, fn):
    def step(i, carry):
        fn(i)
        return carry

    lax.fori_loop(start, stop, step, 0)


def enter(group, me, chip, core, chips, groups):
    barrier = pltpu.get_barrier_semaphore()

    def greet(shard, grp):
        pl.semaphore_signal(barrier, inc=1, device_id=(grp, shard), device_id_type=MESH)

    loop(1, chips, lambda d: greet(2 * ((chip + d) % chips) + core, group))
    loop(1, groups, lambda d: greet(me, (group + d) % groups))
    greet(me + 1 - 2 * core, group)
    return lambda: pl.semaphore_wait(barrier, chips + groups - 1)


def offsets(chips):
    offs, at, n = [], 0, chips
    while n >= 1:
        offs.append(at)
        at += n
        n //= 2
    return offs


def high_level(group, far, bits):
    level = jnp.int32(0)
    for b in range(1, bits):
        level = jnp.where(group // 2**b != far // 2**b, jnp.int32(b), level)
    return level


def bit_of(x, b):
    return (x // 2**b) % 2 == 1


def routes_of(nb, nz, xdim, ydim):
    routes, slot = [], 0
    ybits = log2(ydim)
    split = nb + min(1, nz - 1)
    for lev in range(nb + nz):
        if lev == split:
            ways = [(0, 2, True), (2, 4, False)]
        else:
            ways = [(0, 4, lev < ybits or nb <= lev < split)]
        for t0, t1, rows_first in ways:
            first, second = (xdim, ydim) if rows_first else (ydim, xdim)
            if lev < nb:
                bit = lev if rows_first else lev - ybits
                users = [s for s in range(second) if (s >> bit) & 1]
                arrays = [
                    [s for s in users if s >> (bit + 1) == a] for a in range(second >> (bit + 1))
                ]
            else:
                users = list(range(second))
                arrays = [users]
            routes.append((lev, slice(t0, t1), rows_first, first, second, users, arrays, slot))
            slot += len(arrays)
    return routes


def main_kernel(
    shards,
    groups,
    ids_ref,
    v_any,
    do_any,
    kt_any,
    qt_any,
    ldt_any,
    lam_any,
    fu_any,
    dv_any,
    dkt_any,
    dqt_any,
    dlogt_any,
    dlam_any,
    dv_out,
    dkt_ref,
    dqt_ref,
    dlogt_ref,
    dlam_ref,
    out_sem,
    dv_ref,
    crow_ref,
    dld_ref,
    tails,
    decayed,
    lrow,
    v_ref,
    do_ref,
    kt_ref,
    qt_ref,
    ldt_ref,
    lam_ref,
    fu_ref,
    in_sem,
    bd_t,
    bd,
    lam_t,
    glam,
    rint,
    rnear,
    dq_acc,
    dsc,
    g,
    gn,
    own,
    dec,
    sib,
    sibd,
    blk,
    nd,
    zb,
    hz,
    pks,
    pk,
    coef,
    before_far,
    ring,
    h,
    x,
    st,
    back,
    q_sum,
    parts,
    rs,
    rr,
    u,
    zu,
    z_out,
    cown,
    dn,
    ds,
    g0,
    s_sem,
    a_sem,
    z_send,
    z_recv,
    k_sem,
    r_send,
    r_recv,
    h_send,
    h_recv,
    f_send,
    f_recv,
    g0_sem,
    x_send,
    x_recv,
    b_send,
    b_recv,
    q_send,
    q_recv,
    t_sem,
    u_send,
    u_recv,
    o_sem,
    w_sem,
):
    chips = shards // 2
    pairs = chips
    heads = shards
    nb, nz = log2(chips), log2(groups)
    levels = nb + nz
    columns = lam_t.shape[0]
    ydim = 2 ** ((nb + 1) // 2)
    xdim = chips // ydim
    group, me, chip, core = place()
    mate = me + 1 - 2 * core
    xpos, ypos = chip // ydim, chip % ydim
    offs = offsets(chips)
    top = offs[nb]
    wide = min(128, columns * heads)
    per = wide // heads

    routes = routes_of(nb, nz, xdim, ydim)
    ways = [[r for r in range(len(routes)) if routes[r][0] == lev] for lev in range(levels)]

    def shifted(i):
        return ((xpos + i // ydim) % xdim) * ydim + (ypos + i % ydim) % ydim

    def near(src, dst, send, recv):
        return remote(src, dst, send, recv, (group, mate))

    loads = [
        pltpu.make_async_copy(a, b, in_sem.at[i])
        for i, (a, b) in enumerate(
            [
                (ldt_any, ldt_ref),
                (kt_any, kt_ref),
                (v_any, v_ref),
                (do_any, do_ref),
                (qt_any, qt_ref),
                (lam_any, lam_ref),
                (fu_any.at[chip, :, core], fu_ref),
            ]
        )
    ]
    for c in loads:
        c.start()
    results = [
        pltpu.make_async_copy(a, b, out_sem.at[i])
        for i, (a, b) in enumerate(
            [
                (dkt_ref, dkt_any),
                (dqt_ref, dqt_any),
                (dlogt_ref, dlogt_any),
                (dlam_ref, dlam_any),
            ]
        )
    ]
    wait_entry = enter(group, me, chip, core, chips, groups)

    row = iota((TOK, TOK), 0)
    col = iota((TOK, TOK), 1)
    upto = (row <= col).astype(F32)
    half = (col < 64).astype(F32)
    m0 = half.astype(BF16)
    m1 = (1.0 - half).astype(BF16)
    loads[0].wait()
    crow = dot(ldt_ref[...], upto, precision=highest)
    crow_ref[...] = crow
    last = jnp.broadcast_to(crow[:, TOK - 1 : TOK], (heads, TOK))
    tail = jnp.exp(last - crow)
    full = jnp.exp(last)
    loads[1].wait()
    kt = kt_ref[...]
    loads[2].wait()
    for p in range(pairs):
        k2 = jnp.concatenate(
            [kt * tail[2 * p : 2 * p + 1], kt * tail[2 * p + 1 : 2 * p + 2]], axis=1
        ).astype(BF16)
        vp = v_ref[:, p * 128 : (p + 1) * 128]
        s = dot(k2, jnp.concatenate([vp * m0, vp * m1], axis=0))
        own[p] = s.reshape(2, 4, 8, 128)
        dec[p] = (
            half[0:8] * full[2 * p : 2 * p + 1] + (1.0 - half[0:8]) * full[2 * p + 1 : 2 * p + 2]
        )

    wait_entry()
    swap_half = near(own.at[:, 1 - core], sib.at[:, 1 - core], s_sem.at[0], s_sem.at[1])
    swap_dec = near(dec, sibd, s_sem.at[2], s_sem.at[3])
    rest = near(own.at[:, core], sib.at[:, core], s_sem.at[4], s_sem.at[5])
    swap_half.start()
    swap_dec.start()

    @pl.when(core == 0)
    def _():
        rest.start()

    swap_dec.wait_recv()
    swap_half.wait_recv()

    def merge_cores(p):
        a = own[p, core]
        b = sib[p, core]
        left = jnp.where(core == 0, a, b)
        right = jnp.where(core == 0, b, a)
        drow = jnp.where(core == 0, sibd[p], dec[p])
        blk[p, 0:4] = drow[None] * left + right
        blk[p, 4] = dec[p] * sibd[p]

    loop(0, pairs, merge_cores)

    def scatter(i):
        to = shifted(i)
        remote(
            blk.at[to], nd.at[chip], a_sem.at[0], a_sem.at[1], (group, 2 * to + core)
        ).start()

    loop(1, chips, scatter)
    nd[chip] = blk[chip]

    loads[3].wait()
    loads[4].wait()
    qt = qt_ref[...]
    q = qt.T
    k = kt.T
    ccol = crow.T
    causal = row <= col
    scores = jnp.where(causal, dot(k, qt, precision=highest), 0.0)
    b_col = jnp.exp(ccol[TOK // 2 - 1 : TOK // 2, :] - ccol)
    a_row = jnp.exp(crow - crow[:, TOK // 2 - 1 : TOK // 2])
    suffix = (row >= col).astype(F32).astype(BF16)
    before = row < col
    t0 = (row < 64).astype(F32).astype(BF16)
    t1 = (row >= 64).astype(F32).astype(BF16)
    dsc[...] = jnp.zeros(dsc.shape, F32)

    def inside(p):
        sl = slice(p * 128, (p + 1) * 128)
        dop = do_ref[:, sl]
        dot_t = dop.astype(F32).T.astype(BF16)
        bdt = jnp.concatenate([dot_t * t0, dot_t * t1], axis=1)
        bdo = jnp.concatenate([dop * m0, dop * m1], axis=0)
        bd_t[p] = bdt
        bd[p] = bdo
        dmix = dot(v_ref[:, sl], bdt)
        xs = []
        for j in range(2):
            head = 2 * p + j
            dm = dmix[:, j * 128 : (j + 1) * 128]
            e = jnp.where(causal, b_col[:, head : head + 1] * a_row[head : head + 1, :], 0.0)
            mix = e * scores
            dsc[...] += e * dm
            y = dot((mix * dm).astype(BF16), suffix)
            dlogt_ref[head : head + 1, :] = jnp.sum(
                jnp.where(before, y, 0.0), axis=0, keepdims=True
            )
            xs.append(mix.astype(BF16))
        dv_ref[:, sl] = dot(jnp.concatenate(xs, axis=1), bdo)

    for p in range(pairs // 2):
        inside(p)

    part = nd.at[pl.ds(0, chips - 1)]
    scattered = near(part, part, a_sem.at[0], a_sem.at[1])
    scattered.wait_recv()
    for b in range(1, nb + 1):
        for i in range(chips >> b):
            lo = offs[b - 1] + 2 * i
            right = nd[lo + 1, 4]
            nd[offs[b] + i, 0:4] = right[None] * nd[lo, 0:4] + nd[lo + 1, 0:4]
            nd[offs[b] + i, 4] = right * nd[lo, 4]

    def up(d):
        return remote(
            nd.at[top], zb.at[group], z_send.at[d], z_recv.at[group], (group + d, me)
        )

    def down(d):
        return remote(
            nd.at[top, 4], zb.at[group, 4], z_send.at[d], z_recv.at[group], (group - d, me)
        )

    for d in range(1, groups):

        @pl.when(group + d < groups)
        def _():
            up(d).start()

    for d in range(1, groups):

        @pl.when(group - d >= 0)
        def _():
            remote(
                nd.at[top, 4],
                zb.at[group, 4],
                z_send.at[groups + d],
                z_recv.at[group],
                (group - d, me),
            ).start()

    sub = iota((8, 128), 0)
    for c in range(chips):
        pre = jnp.ones((8, 128), F32)
        rows = pre
        for b in range(nb):
            rows = jnp.where(sub >= b, pre, rows)
            if (c >> b) & 1:
                pre = pre * nd[offs[b] + (c >> b) - 1, 4]
        pks[c] = jnp.where(sub >= nb, pre, rows)

    def send_scales(i):
        to = shifted(i)
        remote(
            pks.at[to], pk.at[chip], k_sem.at[0], k_sem.at[1], (group, 2 * to + core)
        ).start()

    loop(1, chips, send_scales)
    pk[chip] = pks[chip]

    def where_on(r):
        if routes[r][2]:
            return xpos, ypos, lambda f, s: f * ydim + s
        return ypos, xpos, lambda f, s: s * ydim + f

    def reads(lev):
        if lev >= nb:
            return bit_of(group, lev - nb)
        return bit_of(chip, lev)

    def when_level(lev, fn):
        if lev >= nb:
            pl.when(bit_of(group, lev - nb))(fn)
        else:
            fn()

    def first_phase(r):
        lev, tiles, rows_first, first, second, users, arrays, slot = routes[r]
        fpos, spos, at = where_on(r)

        def source(a, f):
            if lev >= nb:
                return hz.at[lev - nb, tiles]
            if rows_first:
                return nd.at[offs[lev] + f * (ydim >> lev) + 2 * a, 0:4]
            return nd.at[offs[lev] + 2 * a, 0:4]

        def go():
            for d in range(1, first):
                f = (fpos + d) % first
                for a in range(len(arrays)):
                    remote(
                        source(a, f),
                        ring.at[slot + a, fpos, tiles],
                        r_send.at[slot + a],
                        r_recv.at[slot + a],
                        (group, 2 * at(f, spos) + core),
                    ).start()
            for a in range(len(arrays)):
                ring[slot + a, fpos, tiles] = source(a, fpos)[...]

        if lev >= nb:
            go()
        else:
            when_level(lev, go)

    def second_phase(r):
        lev, tiles, rows_first, first, second, users, arrays, slot = routes[r]
        fpos, spos, at = where_on(r)

        def go():
            if first > 1:
                for a in range(len(arrays)):
                    part = ring.at[slot + a, pl.ds(0, first - 1), tiles]
                    near(part, part, r_send.at[slot + a], r_recv.at[slot + a]).wait_recv()
            for a, readers in enumerate(arrays):
                for s in readers:
                    there = h.at[lev, core, pl.ds(spos * first, first), tiles]

                    @pl.when(spos != s)
                    def _():
                        remote(
                            ring.at[slot + a, pl.ds(0, first), tiles],
                            there,
                            h_send.at[r],
                            h_recv.at[r],
                            (group, 2 * at(fpos, s) + core),
                        ).start()

                    @pl.when(spos == s)
                    def _():
                        there[...] = ring[slot + a, 0:first, tiles]

        when_level(lev, go)

    low = list(range(nb))
    high = list(range(nb, levels))
    low_ways = [r for lev in low for r in ways[lev]]
    high_ways = [r for lev in high for r in ways[lev]]
    for r in low_ways:
        first_phase(r)

    for p in range(pairs // 2, 3 * pairs // 4):
        inside(p)
    for r in low_ways:
        second_phase(r)
    for p in range(3 * pairs // 4, pairs):
        inside(p)

    coef[...] = jnp.ones((8, 128), F32)
    hz[...] = jnp.zeros(hz.shape, F32)
    for d in range(1, groups):
        far = group - d

        @pl.when(far >= 0)
        def _():
            slot = zb.at[far]
            near(slot, slot, z_send.at[0], z_recv.at[far]).wait_recv()
            level = high_level(group, far, nz)
            hz[level] = hz[level] + coef[...][None] * zb[far, 0:4]
            before_far[d] = coef[...]
            coef[...] = coef[...] * zb[far, 4]

        l = log2(d)

        @pl.when(bit_of(group, l) & (group % 2**l + 2**l == d))
        def _():
            for r in ways[nb + l]:
                first_phase(r)

    q_low = qt.astype(BF16).astype(F32)
    q2 = jnp.concatenate([q_low, q_low], axis=1)
    loads[5].wait()
    for j in range(columns // per):
        lam_t[pl.ds(j * per, per)] = lam_ref[:, j * wide : (j + 1) * wide].T.reshape(
            per, heads, TOK
        )
    glam[...] = jnp.zeros(glam.shape, F32)
    rint[...] = jnp.zeros(rint.shape, F32)
    rnear[...] = jnp.zeros(rnear.shape, F32)
    dq_acc[...] = jnp.zeros(dq_acc.shape, F32)
    ids = [ids_ref[0, b] for b in range(1 + levels)]

    def spot(r, p):
        if routes[r][2]:
            return (p % ydim) * xdim + p // ydim
        return p

    def levels_step(group_levels, p):
        gr2 = jnp.exp(crow_ref[pl.ds(2 * p, 2), :])
        mate_scale = jnp.where(core == 1, sibd[p, 0:1], jnp.ones((1, 128), F32))
        helds, ws, scales = [], [], []
        for b in group_levels:
            if b == 0:
                held = sib[p].reshape(64, 128)
                scales.append(None)
            else:
                scales.append(mate_scale * pk[p, b - 1 : b])
                held = jnp.concatenate(
                    [h[b - 1, j, spot(r, p), routes[r][1]] for j in range(2) for r in ways[b - 1]],
                    axis=0,
                )
                held = jnp.where(reads(b - 1), held.reshape(64, 128) * scales[-1], 0.0)
            helds.append(held.astype(BF16))
            ws.append(lam_t[ids[b], pl.ds(2 * p, 2), :] * gr2)
        m = dot(jnp.concatenate(helds, axis=0), bd_t[p])
        wqs = []
        acc = dq_acc[...]
        r2 = jnp.zeros((2, TOK), F32)
        for i, b in enumerate(group_levels):
            mi = m[64 * i : 64 * (i + 1)]
            w = jnp.concatenate([ws[i][0:1], ws[i][1:2]], axis=1)
            gsum = jnp.sum(q2 * mi, axis=0, keepdims=True)
            acc = acc + w * mi
            wqs.append((w * q2).astype(BF16))
            g2 = jnp.concatenate([gsum[:, 0:128], gsum[:, 128:256]], axis=0)
            glam[b, pl.ds(2 * p, 2), :] = gr2 * g2
            r2 = r2 + ws[i] * g2
        dq_acc[...] = acc
        if group_levels == [0]:
            rnear[pl.ds(2 * p, 2), :] = r2
        else:
            rint[pl.ds(2 * p, 2), :] += r2
        grad = dot(jnp.concatenate(wqs, axis=0), bd[p])
        for i, b in enumerate(group_levels):
            gi = grad[64 * i : 64 * (i + 1)]
            if b == 0:
                gn[p] = gi.reshape(2, 4, 8, 128)
            else:
                gi = (gi * scales[i]).reshape(2, 4, 8, 128)
                for r in ways[b - 1]:
                    tiles = routes[r][1]
                    for j in range(2):
                        g[b - 1, j, spot(r, p), tiles] = gi[j, tiles]

    def levels_pass(group_levels):
        def two(i):
            levels_step(group_levels, 2 * i)
            levels_step(group_levels, 2 * i + 1)

        loop(0, pairs // 2, two)

    g0_copy = near(gn, g0, g0_sem.at[0], g0_sem.at[1])

    @pl.when(core == 1)
    def _():
        rest.wait_recv()
        levels_pass([0])
        g0_copy.start()

    for r in high_ways:
        second_phase(r)

    def swap(lev):
        return near(g.at[lev, 1 - core], x.at[lev], x_send.at[lev], x_recv.at[lev])

    def fetch(levs):
        for lev in levs:

            @pl.when(reads(lev))
            def _():
                for r in ways[lev]:
                    _, tiles, _, first, second, _, _, _ = routes[r]
                    if second > 1:
                        part = h.at[lev, core, pl.ds(0, (second - 1) * first), tiles]
                        near(part, part, h_send.at[r], h_recv.at[r]).wait_recv()
                ours = h.at[lev, core]
                near(ours, ours, f_send.at[lev], f_recv.at[lev]).start()

        for lev in levs:

            @pl.when(reads(lev))
            def _():
                theirs = h.at[lev, 1 - core]
                near(theirs, theirs, f_send.at[lev], f_recv.at[lev]).wait_recv()

    def give_back(levs):
        for lev in levs:

            @pl.when(reads(lev))
            def _():
                swap(lev).start()

        def send_back(r):
            lev, tiles, _, first, second, _, _, _ = routes[r]
            fpos, spos, at = where_on(r)
            for d in range(1, second):
                s = (spos + d) % second
                remote(
                    st.at[lev, pl.ds(s * first, first), tiles],
                    back.at[lev, spos, pl.ds(0, first), tiles],
                    b_send.at[r],
                    b_recv.at[r],
                    (group, 2 * at(fpos, s) + core),
                ).start()
            back[lev, spos, 0:first, tiles] = st[lev, pl.ds(spos * first, first), tiles]

        for lev in levs:

            @pl.when(reads(lev))
            def _():
                swap(lev).wait_recv()

                def add(c):
                    st[lev, c] = g[lev, core, c] + x[lev, c]

                loop(0, chips, add)
                for r in ways[lev]:
                    send_back(r)

    def gather_back(r):
        lev, tiles, rows_first, first, second, users, arrays, slot = routes[r]
        fpos, spos, at = where_on(r)

        def arrived(count):
            if count:
                part = back.at[lev, pl.ds(0, count), pl.ds(0, first), tiles]
                near(part, part, b_send.at[r], b_recv.at[r]).wait_recv()

        def go():
            if lev >= nb:
                arrived(second - 1)
            else:

                @pl.when(reads(lev))
                def _():
                    arrived(len(users) - 1)

                @pl.when(jnp.logical_not(reads(lev)))
                def _():
                    arrived(len(users))

            for a, readers in enumerate(arrays):
                for f in range(first):
                    total = back[lev, readers[0], f, tiles]
                    for s in readers[1:]:
                        total = total + back[lev, s, f, tiles]
                    q_sum[slot + a, f, tiles] = total
                for d in range(1, first):
                    f = (fpos + d) % first
                    remote(
                        q_sum.at[slot + a, f, tiles],
                        parts.at[slot + a, fpos, tiles],
                        q_send.at[slot + a],
                        q_recv.at[slot + a],
                        (group, 2 * at(f, spos) + core),
                    ).start()
                parts[slot + a, fpos, tiles] = q_sum[slot + a, fpos, tiles]

        when_level(lev, go)

    def parts_in(r):
        lev, tiles, rows_first, first, second, users, arrays, slot = routes[r]
        if first > 1:
            for a in range(len(arrays)):
                part = parts.at[slot + a, pl.ds(0, first - 1), tiles]
                near(part, part, q_send.at[slot + a], q_recv.at[slot + a]).wait_recv()

    tail_col = jnp.exp(ccol[TOK - 1 : TOK, :] - ccol)
    for p in range(pairs):
        tails[p] = jnp.where(
            col < 64, tail_col[:, 2 * p : 2 * p + 1], tail_col[:, 2 * p + 1 : 2 * p + 2]
        )
        vp = v_ref[:, p * 128 : (p + 1) * 128].astype(F32)
        decayed[p] = (tails[p] * vp).astype(BF16)
    k_low = k.astype(BF16)
    kt_low = kt.astype(BF16).astype(F32)

    k_part = pk.at[pl.ds(0, chips - 1)]
    scales_in = near(k_part, k_part, k_sem.at[0], k_sem.at[1])
    scales_in.wait_recv()
    fetch(low)
    levels_pass([b + 1 for b in low])
    fetch(high)

    @pl.when(group > 0)
    def _():
        levels_pass([b + 1 for b in high])

    give_back(high)

    pulls = rint[...]
    rsum = jnp.broadcast_to(jnp.sum(pulls, axis=1, keepdims=True), (heads, TOK))
    lane = iota((8, 128), 1)
    first_lane = jnp.where((sub == 0) & (lane == 0), 1.0, 0.0)
    mid_lane = jnp.where((sub == 0) & (lane == 64), 1.0, 0.0)
    for p in range(pairs):
        rs[p] = first_lane * rsum[2 * p : 2 * p + 1] + mid_lane * rsum[2 * p + 1 : 2 * p + 2]

    def send_sums(i):
        to = shifted(i)
        remote(
            rs.at[to], rr.at[chip], t_sem.at[0], t_sem.at[1], (group, 2 * to + core)
        ).start()

    loop(1, chips, send_sums)
    rr[chip] = rs[chip]
    for r in high_ways:
        gather_back(r)
    give_back(low)

    def sum_high(r):
        lev, tiles, _, first, _, _, _, slot = routes[r]

        @pl.when(reads(lev))
        def _():
            parts_in(r)
            total = parts[slot, 0, tiles]
            for f in range(1, first):
                total = total + parts[slot, f, tiles]
            u[lev - nb, tiles] = total

    for r in high_ways:
        sum_high(r)

    coef[...] = jnp.zeros((8, 128), F32)
    for d in reversed(range(1, groups)):

        @pl.when(group - d >= 0)
        def _():
            level = high_level(group, group - d, nz)
            grad = u[level]
            z_out[d, 0:4] = grad
            z_out[d, 4] = coef[...]
            remote(
                z_out.at[d], zu.at[group], u_send.at[d], u_recv.at[group], (group - d, me)
            ).start()
            coef[...] = coef[...] + before_far[d] * jnp.sum(grad * zb[group - d, 0:4], axis=0)

    for r in low_ways:
        gather_back(r)

    for j in range(columns // per):
        slabs = []
        for p in range(j * per, (j + 1) * per):
            total = jnp.zeros((heads, TOK), F32)
            for b in range(1 + levels):
                total = total + jnp.where(ids[b] == p, glam[b], 0.0)
            slabs.append(total)
        dlam_ref[:, j * wide : (j + 1) * wide] = jnp.concatenate(slabs, axis=0).T
    results[3].start()
    even = jnp.where(core == 0, 1.0, 0.0)
    dlogt_ref[...] += (
        dot(pulls + rnear[...], (row >= col).astype(F32), precision=highest) - even * rsum
    )
    dqi = (dq_acc[:, 0:128] + dq_acc[:, 128:256]).astype(BF16).astype(F32)
    dst = dsc[...]
    dqt_ref[...] = dqi + dot(kt, dst, precision=highest)
    dkt_ref[...] = dot(dst, q, precision=highest).T
    results[1].start()

    for r in low_ways:
        lev, tiles, rows_first, first, second, users, arrays, slot = routes[r]
        parts_in(r)
        for a in range(len(arrays)):
            if rows_first:
                for f in range(first):
                    dn[offs[lev] + f * (ydim >> lev) + 2 * a, 0:4] = parts[slot + a, f]
            else:
                total = parts[slot + a, 0]
                for f in range(1, first):
                    total = total + parts[slot + a, f]
                dn[offs[lev] + 2 * a, 0:4] = total

    coef[...] = jnp.ones((8, 128), F32)
    dn[top, 0:4] = jnp.zeros((4, 8, 128), F32)
    cown[...] = jnp.zeros((8, 128), F32)
    for l in range(nz):

        @pl.when(bit_of(group, l))
        def _():
            cown[...] = cown[...] + jnp.sum(u[l] * hz[l], axis=0)

    for d in range(1, groups):

        @pl.when(group + d < groups)
        def _():
            far = zb.at[group + d, 4]
            near(far, far, z_send.at[0], z_recv.at[group + d]).wait_recv()
            slot = zu.at[group + d]
            near(slot, slot, u_send.at[d], u_recv.at[group + d]).wait_recv()
            dn[top, 0:4] = dn[top, 0:4] + coef[...][None] * zu[group + d, 0:4]
            cown[...] = cown[...] + zu[group + d, 4]
            coef[...] = coef[...] * zb[group + d, 4]

    loads[6].wait()
    fu = jnp.concatenate([fu_ref[0], fu_ref[1]], axis=1).reshape(4, 8, 128)
    dn[top, 0:4] = dn[top, 0:4] + coef[...][None] * fu
    earlier = hz[0]
    for l in range(1, nz):
        earlier = earlier + hz[l]
    carry = cown[...] + coef[...] * nd[top, 4] * jnp.sum(earlier * fu, axis=0)
    for b in reversed(range(nb)):
        for i in range(0, chips >> b, 2):
            left = offs[b] + i
            parent = dn[offs[b + 1] + i // 2, 0:4]
            dn[left, 0:4] = dn[left, 0:4] + nd[left + 1, 4][None] * parent
            dn[left + 1, 0:4] = parent

    t_part = rr.at[pl.ds(0, chips - 1)]
    sums_in = near(t_part, t_part, t_sem.at[0], t_sem.at[1])
    sums_in.wait_recv()
    now = jnp.sum(carry, axis=0, keepdims=True)
    for c in range(chips):
        step = jnp.sum(nd[c, 0:4] * dn[c, 0:4], axis=0) - rr[c]
        then = now + jnp.sum(step, axis=0, keepdims=True)
        dn[c, 4] = jnp.where(sub == 0, now, jnp.where(sub == 1, then, 0.0))
        now = then

    def give(i, half):
        to = shifted(i)
        remote(
            dn.at[to],
            ds.at[core, half, i % split_at],
            o_sem.at[0],
            o_sem.at[1 + half],
            (group, 2 * to + core),
        ).start()

    split_at = chips // 2
    loop(1, split_at, lambda i: give(i, 0))
    loop(split_at, chips, lambda i: give(i, 1))
    ds[core, 0, 0] = dn[chip, 0:5]
    if split_at > 1:
        part = ds.at[core, 0, pl.ds(0, split_at - 1)]
        near(part, part, o_sem.at[0], o_sem.at[1]).wait_recv()
    near(ds.at[core, 0], ds.at[core, 0], w_sem.at[0], w_sem.at[1]).start()
    part = ds.at[core, 1]
    near(part, part, o_sem.at[0], o_sem.at[2]).wait_recv()
    near(part, part, w_sem.at[2], w_sem.at[3]).start()

    def all_sent(r):
        lev, tiles, rows_first, first, second, users, arrays, slot = routes[r]

        def out_of_ring(count):
            if count:
                part = h.at[lev, core, pl.ds(0, count * first), tiles]
                near(part, part, h_send.at[r], h_recv.at[r]).wait_send()

        def sends():
            if first > 1:
                for a in range(len(arrays)):
                    part = ring.at[slot + a, pl.ds(0, first - 1), tiles]
                    near(part, part, r_send.at[slot + a], r_recv.at[slot + a]).wait_send()
                    near(part, part, q_send.at[slot + a], q_recv.at[slot + a]).wait_send()
            if lev >= nb:
                out_of_ring(second - 1)

        when_level(lev, sends)

        if lev < nb:

            @pl.when(jnp.logical_not(reads(lev)))
            def _():
                out_of_ring(len(users))

        @pl.when(reads(lev))
        def _():
            if lev < nb:
                out_of_ring(len(users) - 1)
            if second > 1:
                part = st.at[lev, pl.ds(0, (second - 1) * first), tiles]
                near(part, part, b_send.at[r], b_recv.at[r]).wait_send()

    for r in range(len(routes)):
        all_sent(r)
    for lev in range(levels):

        @pl.when(reads(lev))
        def _():
            ours = h.at[lev, core]
            near(ours, ours, f_send.at[lev], f_recv.at[lev]).wait_send()
            swap(lev).wait_send()

    for d in range(1, groups):

        @pl.when(group + d < groups)
        def _():
            up(d).wait_send()

        @pl.when(group - d >= 0)
        def _():
            line = nd.at[top, 4]
            near(line, line, z_send.at[groups + d], z_recv.at[0]).wait_send()
            near(z_out.at[d], z_out.at[d], u_send.at[d], u_recv.at[0]).wait_send()

    swap_half.wait_send()
    swap_dec.wait_send()
    scattered.wait_send()
    scales_in.wait_send()
    sums_in.wait_send()

    @pl.when(core == 1)
    def _():
        g0_copy.wait_send()

    @pl.when(core == 0)
    def _():
        rest.wait_send()
        g0_copy.wait_recv()

    part = dn.at[pl.ds(0, chips - 1)]
    near(part, part, o_sem.at[0], o_sem.at[1]).wait_send()

    def finish(a, i):
        at = a * ydim + i
        half, slot = at // split_at, at % split_at
        p = ((xpos + xdim - a) % xdim) * ydim + (ypos + ydim - i) % ydim
        scale = jnp.where(core == 0, sibd[p], jnp.ones((8, 128), F32))
        dld = jnp.zeros((8, 128), F32)
        lows = []
        for j in range(2):
            grad = ds[j, half, slot, 0:4]
            dot_own = jnp.sum(own[p, j] * grad, axis=0)
            dld = dld + jnp.where(sub == core, ds[j, half, slot, 4], 0.0)
            dld = dld - jnp.where(core == 0, 0.0, dot_own)
            extra = jnp.where(core == 0, g0[p, j], 0.0)
            lows.append(grad * scale[None] + extra)
        low = jnp.concatenate(lows, axis=0).reshape(64, 128).astype(BF16)
        dld_ref[pl.ds(p, 1), :] = jnp.sum(dld, axis=0, keepdims=True)
        cols = pl.ds(pl.multiple_of(p * 128, 128), 128)
        dv_out[:, cols] = (dv_ref[:, cols] + tails[p] * dot(k_low, low)).astype(BF16)
        both_heads = jnp.concatenate([low * m0[0:64], low * m1[0:64]], axis=0)
        dk = lax.dot_general(
            both_heads, decayed[p], (((1,), (1,)), ((), ())), preferred_element_type=F32
        )
        dkt_ref[...] += dk[0:64] + dk[64:128]
        lrow[pl.ds(2 * p, 1), :] = jnp.sum(kt_low * dk[0:64], axis=0, keepdims=True)
        lrow[pl.ds(2 * p + 1, 1), :] = jnp.sum(kt_low * dk[64:128], axis=0, keepdims=True)

    def half_in(half):
        theirs = ds.at[1 - core, half]
        both = near(theirs, theirs, w_sem.at[2 * half], w_sem.at[2 * half + 1])
        both.wait_recv()
        both.wait_send()

    for a in range(xdim):
        if a == 0:
            half_in(0)
        if a == xdim // 2:
            half_in(1)
        for i in range(ydim):
            finish(a, i)
        cols = pl.ds(pl.multiple_of(((xpos + xdim - a) % xdim) * ydim * 128, 128), ydim * 128)
        results.append(
            pltpu.make_async_copy(dv_out.at[:, cols], dv_any.at[:, cols], out_sem.at[4 + a])
        )
        results[-1].start()
    results[0].start()
    head = iota((heads, pairs), 0)
    rows = dot((iota((heads, pairs), 1) == head // 2).astype(F32), dld_ref[...], precision=highest)
    side = iota((heads, TOK), 1) // 64 == iota((heads, TOK), 0) % 2
    dd = jnp.sum(jnp.where(side, rows, 0.0), axis=1, keepdims=True)
    dlogt_ref[...] += dot(lrow[...], (row < col).astype(F32), precision=highest) + dd
    results[2].start()
    for c in results:
        c.wait()


def end_kernel(*refs):
    n = (len(refs) - 2) // 3
    in_sem, out_sem = refs[-2:]
    loads, stores = [], []
    for i in range(n):
        src, dst, held = refs[i], refs[n + i], refs[2 * n + i]
        cuts = 4 if i == 0 else 1
        step = src.shape[0] // cuts
        for j in range(cuts):
            part = pl.ds(j * step, step)
            k = len(loads)
            loads.append(pltpu.make_async_copy(src.at[part], held.at[part], in_sem.at[k]))
            stores.append(pltpu.make_async_copy(held.at[part], dst.at[part], out_sem.at[k]))
    for c in loads:
        c.start()
    for load, store in zip(loads, stores):
        load.wait()
        store.start()
    for c in stores:
        c.wait()


def body(
    values, state_input, state_output, log_decay, level_lam, level_ids, upstream, final_upstream
):
    shards, groups = lax.axis_size("shard"), lax.axis_size("grp")
    chips = shards // 2
    nb, nz = log2(chips), log2(groups)
    levels = nb + nz
    heads = log_decay.shape[1]
    columns = level_lam.shape[1] // heads
    params = partial(pltpu.CompilerParams, vmem_limit_bytes=VMEM_CAP)
    dma = pltpu.SemaphoreType.DMA
    tile = (4, 8, 128)
    kt = state_input.T
    ydim = 2 ** ((nb + 1) // 2)
    routes = routes_of(nb, nz, chips // ydim, ydim)
    slots = sum(len(route[6]) for route in routes)
    count = len(routes)

    shapes = (
        jax.ShapeDtypeStruct((TOK, heads * 64), BF16),
        f32(64, TOK),
        f32(64, TOK),
        f32(heads, TOK),
        f32(TOK, columns * heads),
    )
    anywhere = pl.BlockSpec(memory_space=pl.ANY)
    parts = pl.pallas_call(
        partial(main_kernel, shards, groups),
        out_shape=shapes,
        in_specs=[pl.BlockSpec(memory_space=pltpu.SMEM)]
        + [anywhere] * 7,
        out_specs=(anywhere,) * 5,
        scratch_shapes=[
            pltpu.VMEM((TOK, heads * 64), BF16),
            pltpu.VMEM((64, TOK), F32),
            pltpu.VMEM((64, TOK), F32),
            pltpu.VMEM((heads, TOK), F32),
            pltpu.VMEM((TOK, columns * heads), F32),
            dma((4 + chips // ydim,)),
            pltpu.VMEM((TOK, heads * 64), F32),
            pltpu.VMEM((heads, TOK), F32),
            pltpu.VMEM((chips, 128), F32),
            pltpu.VMEM((chips, TOK, 128), F32),
            pltpu.VMEM((chips, TOK, 128), BF16),
            pltpu.VMEM((heads, TOK), F32),
            pltpu.VMEM((TOK, heads * 64), BF16),
            pltpu.VMEM((TOK, heads * 64), BF16),
            pltpu.VMEM((64, TOK), F32),
            pltpu.VMEM((64, TOK), F32),
            pltpu.VMEM((heads, TOK), F32),
            pltpu.VMEM((TOK, columns * heads), F32),
            pltpu.VMEM((2, 32, 64), F32),
            dma((7,)),
            pltpu.VMEM((chips, 128, 256), BF16),
            pltpu.VMEM((chips, 256, 128), BF16),
            pltpu.VMEM((columns, heads, TOK), F32),
            pltpu.VMEM((1 + levels, heads, TOK), F32),
            pltpu.VMEM((heads, TOK), F32),
            pltpu.VMEM((heads, TOK), F32),
            pltpu.VMEM((64, 256), F32),
            pltpu.VMEM((TOK, TOK), F32),
            pltpu.VMEM((levels, 2, chips) + tile, F32),
            pltpu.VMEM((chips, 2) + tile, F32),
            pltpu.VMEM((chips, 2) + tile, F32),
            pltpu.VMEM((chips, 8, 128), F32),
            pltpu.VMEM((chips, 2) + tile, F32),
            pltpu.VMEM((chips, 8, 128), F32),
            pltpu.VMEM((chips, 5, 8, 128), F32),
            pltpu.VMEM((2 * chips, 5, 8, 128), F32),
            pltpu.VMEM((groups, 5, 8, 128), F32),
            pltpu.VMEM((nz,) + tile, F32),
            pltpu.VMEM((chips, 8, 128), F32),
            pltpu.VMEM((chips, 8, 128), F32),
            pltpu.VMEM((8, 128), F32),
            pltpu.VMEM((groups, 8, 128), F32),
            pltpu.VMEM((slots, ydim) + tile, F32),
            pltpu.VMEM((levels, 2, chips) + tile, F32),
            pltpu.VMEM((levels, chips) + tile, F32),
            pltpu.VMEM((levels, chips) + tile, F32),
            pltpu.VMEM((levels, ydim, ydim) + tile, F32),
            pltpu.VMEM((slots, ydim) + tile, F32),
            pltpu.VMEM((slots, ydim) + tile, F32),
            pltpu.VMEM((chips, 8, 128), F32),
            pltpu.VMEM((chips, 8, 128), F32),
            pltpu.VMEM((nz,) + tile, F32),
            pltpu.VMEM((groups, 5, 8, 128), F32),
            pltpu.VMEM((groups, 5, 8, 128), F32),
            pltpu.VMEM((8, 128), F32),
            pltpu.VMEM((2 * chips, 5, 8, 128), F32),
            pltpu.VMEM((2, 2, chips // 2, 5, 8, 128), F32),
            pltpu.VMEM((chips, 2) + tile, F32),
            dma((6,)),
            dma((2,)),
            dma((2 * groups,)),
            dma((groups,)),
            dma((2,)),
            dma((slots,)),
            dma((slots,)),
            dma((count,)),
            dma((count,)),
            dma((levels,)),
            dma((levels,)),
            dma((2,)),
            dma((levels,)),
            dma((levels,)),
            dma((count,)),
            dma((count,)),
            dma((slots,)),
            dma((slots,)),
            dma((2,)),
            dma((groups,)),
            dma((groups,)),
            dma((3,)),
            dma((4,)),
        ],
        compiler_params=params(collective_id=0, has_side_effects=True),
        name="main",
    )(
        level_ids,
        values,
        upstream,
        kt,
        state_output.T,
        log_decay.T,
        level_lam,
        final_upstream.reshape(chips, 2, 2, 32, 64),
    )

    dv, dk, dq, dlog, dlam = pl.pallas_call(
        end_kernel,
        out_shape=shapes,
        in_specs=[anywhere] * 5,
        out_specs=(anywhere,) * 5,
        scratch_shapes=[pltpu.VMEM(x.shape, x.dtype) for x in shapes] + [dma((8,)), dma((8,))],
        compiler_params=params(),
        name="end",
    )(*parts)
    return (dv, dk.T, dq.T, dlog.T, dlam)


def solution(mesh):
    spec = P(("grp", "shard"), None)
    return jax.shard_map(
        body,
        mesh=mesh,
        in_specs=(spec,) * 7 + (P(),),
        out_specs=(spec,) * 5,
        check_vma=False,
    )
```

```python
from functools import partial

import jax
import jax.numpy as jnp
from jax import lax
from jax.experimental import pallas as pl
from jax.experimental.pallas import tpu as pltpu
from jax.sharding import PartitionSpec as P

highest = lax.Precision.HIGHEST
MESH = pl.DeviceIdType.MESH
F32 = jnp.float32
BF16 = jnp.bfloat16
TOK = 128
VMEM_CAP = 62 * 1024 * 1024


def log2(n):
    return n.bit_length() - 1


def f32(*shape):
    return jax.ShapeDtypeStruct(shape, F32)


def iota(shape, dim):
    return lax.broadcasted_iota(jnp.int32, shape, dim)


def dot(a, b, **kw):
    return jnp.dot(a, b, preferred_element_type=F32, **kw)


def place():
    group = lax.axis_index("grp")
    me = lax.axis_index("shard")
    return group, me, me // 2, me % 2


def remote(src, dst, send, recv, device):
    return pltpu.make_async_remote_copy(
        src_ref=src, dst_ref=dst, send_sem=send, recv_sem=recv, device_id=device, device_id_type=MESH
    )


def loop(start, stop, fn):
    def step(i, carry):
        fn(i)
        return carry

    lax.fori_loop(start, stop, step, 0)


def enter(group, me, chip, core, chips, groups):
    barrier = pltpu.get_barrier_semaphore()

    def greet(shard, grp):
        pl.semaphore_signal(barrier, inc=1, device_id=(grp, shard), device_id_type=MESH)

    loop(1, chips, lambda d: greet(2 * ((chip + d) % chips) + core, group))
    loop(1, groups, lambda d: greet(me, (group + d) % groups))
    greet(me + 1 - 2 * core, group)
    return lambda: pl.semaphore_wait(barrier, chips + groups - 1)


def offsets(chips):
    offs, at, n = [], 0, chips
    while n >= 1:
        offs.append(at)
        at += n
        n //= 2
    return offs


def high_level(group, far, bits):
    level = jnp.int32(0)
    for b in range(1, bits):
        level = jnp.where(group // 2**b != far // 2**b, jnp.int32(b), level)
    return level


def bit_of(x, b):
    return (x // 2**b) % 2 == 1


def routes_of(nb, nz, xdim, ydim):
    routes, slot = [], 0
    ybits = log2(ydim)
    split = nb + min(1, nz - 1)
    for lev in range(nb + nz):
        if lev == split:
            ways = [(0, 2, True), (2, 4, False)]
        else:
            ways = [(0, 4, lev < ybits or nb <= lev < split)]
        for t0, t1, rows_first in ways:
            first, second = (xdim, ydim) if rows_first else (ydim, xdim)
            if lev < nb:
                bit = lev if rows_first else lev - ybits
                users = [s for s in range(second) if (s >> bit) & 1]
                arrays = [
                    [s for s in users if s >> (bit + 1) == a] for a in range(second >> (bit + 1))
                ]
            else:
                users = list(range(second))
                arrays = [users]
            routes.append((lev, slice(t0, t1), rows_first, first, second, users, arrays, slot))
            slot += len(arrays)
    return routes


def main_kernel(
    shards,
    groups,
    ids_ref,
    v_any,
    do_any,
    kt_any,
    qt_any,
    ldt_any,
    lam_any,
    fu_any,
    dv_any,
    dkt_any,
    dqt_any,
    dlogt_any,
    dlam_any,
    dv_out,
    dkt_ref,
    dqt_ref,
    dlogt_ref,
    dlam_ref,
    out_sem,
    dv_ref,
    crow_ref,
    dld_ref,
    tails,
    decayed,
    lrow,
    v_ref,
    do_ref,
    kt_ref,
    qt_ref,
    ldt_ref,
    lam_ref,
    fu_ref,
    in_sem,
    bd_t,
    bd,
    lam_t,
    glam,
    rint,
    rnear,
    dq_acc,
    dsc,
    g,
    gn,
    own,
    dec,
    sib,
    sibd,
    blk,
    nd,
    zb,
    hz,
    pks,
    pk,
    coef,
    before_far,
    ring,
    h,
    x,
    st,
    back,
    q_sum,
    parts,
    rs,
    rr,
    u,
    zu,
    z_out,
    cown,
    dn,
    ds,
    g0,
    s_sem,
    a_sem,
    z_send,
    z_recv,
    zd_recv,
    d_sem,
    k_sem,
    r_send,
    r_recv,
    h_send,
    h_recv,
    f_send,
    f_recv,
    g0_sem,
    x_send,
    x_recv,
    b_send,
    b_recv,
    q_send,
    q_recv,
    t_sem,
    u_send,
    u_recv,
    o_sem,
    w_sem,
):
    chips = shards // 2
    pairs = chips
    heads = shards
    nb, nz = log2(chips), log2(groups)
    levels = nb + nz
    columns = lam_t.shape[0]
    ydim = 2 ** ((nb + 1) // 2)
    xdim = chips // ydim
    group, me, chip, core = place()
    mate = me + 1 - 2 * core
    xpos, ypos = chip // ydim, chip % ydim
    offs = offsets(chips)
    top = offs[nb]
    wide = min(128, columns * heads)
    per = wide // heads

    routes = routes_of(nb, nz, xdim, ydim)
    ways = [[r for r in range(len(routes)) if routes[r][0] == lev] for lev in range(levels)]

    def shifted(i):
        return ((xpos + i // ydim) % xdim) * ydim + (ypos + i % ydim) % ydim

    def near(src, dst, send, recv):
        return remote(src, dst, send, recv, (group, mate))

    loads = [
        pltpu.make_async_copy(a, b, in_sem.at[i])
        for i, (a, b) in enumerate(
            [
                (ldt_any, ldt_ref),
                (kt_any, kt_ref),
                (v_any, v_ref),
                (do_any, do_ref),
                (qt_any, qt_ref),
                (lam_any, lam_ref),
                (fu_any.at[chip, :, core], fu_ref),
            ]
        )
    ]
    for c in loads:
        c.start()
    results = [
        pltpu.make_async_copy(a, b, out_sem.at[i])
        for i, (a, b) in enumerate(
            [
                (dkt_ref, dkt_any),
                (dqt_ref, dqt_any),
                (dlogt_ref, dlogt_any),
                (dlam_ref, dlam_any),
            ]
        )
    ]
    wait_entry = enter(group, me, chip, core, chips, groups)

    row = iota((TOK, TOK), 0)
    col = iota((TOK, TOK), 1)
    upto = (row <= col).astype(F32)
    half = (col < 64).astype(F32)
    m0 = half.astype(BF16)
    m1 = (1.0 - half).astype(BF16)
    loads[0].wait()
    crow = dot(ldt_ref[...], upto, precision=highest)
    crow_ref[...] = crow
    last = jnp.broadcast_to(crow[:, TOK - 1 : TOK], (heads, TOK))
    tail = jnp.exp(last - crow)
    full = jnp.exp(last)
    loads[1].wait()
    kt = kt_ref[...]
    loads[2].wait()
    for p in range(pairs):
        k2 = jnp.concatenate(
            [kt * tail[2 * p : 2 * p + 1], kt * tail[2 * p + 1 : 2 * p + 2]], axis=1
        ).astype(BF16)
        vp = v_ref[:, p * 128 : (p + 1) * 128]
        s = dot(k2, jnp.concatenate([vp * m0, vp * m1], axis=0))
        own[p] = s.reshape(2, 4, 8, 128)
        dec[p] = (
            half[0:8] * full[2 * p : 2 * p + 1] + (1.0 - half[0:8]) * full[2 * p + 1 : 2 * p + 2]
        )

    wait_entry()
    swap_half = near(own.at[:, 1 - core], sib.at[:, 1 - core], s_sem.at[0], s_sem.at[1])
    swap_dec = near(dec, sibd, s_sem.at[2], s_sem.at[3])
    rest = near(own.at[:, core], sib.at[:, core], s_sem.at[4], s_sem.at[5])
    swap_dec.start()
    swap_half.start()

    @pl.when(core == 0)
    def _():
        rest.start()

    swap_dec.wait_recv()

    def merge_decays(p):
        blk[p, 4] = dec[p] * sibd[p]

    loop(0, pairs, merge_decays)

    def scatter_decays(i):
        to = shifted(i)
        remote(
            blk.at[to, 4], nd.at[chip, 4], d_sem.at[0], d_sem.at[1], (group, 2 * to + core)
        ).start()

    loop(1, chips, scatter_decays)
    nd[chip, 4] = blk[chip, 4]
    swap_half.wait_recv()

    def merge_cores(p):
        a = own[p, core]
        b = sib[p, core]
        left = jnp.where(core == 0, a, b)
        right = jnp.where(core == 0, b, a)
        drow = jnp.where(core == 0, sibd[p], dec[p])
        blk[p, 0:4] = drow[None] * left + right

    loop(0, pairs, merge_cores)

    def scatter(i):
        to = shifted(i)
        remote(
            blk.at[to, 0:4],
            nd.at[chip, 0:4],
            a_sem.at[0],
            a_sem.at[1],
            (group, 2 * to + core),
        ).start()

    loop(1, chips, scatter)
    nd[chip, 0:4] = blk[chip, 0:4]

    loads[3].wait()
    loads[4].wait()
    qt = qt_ref[...]
    q = qt.T
    k = kt.T
    ccol = crow.T
    causal = row <= col
    scores = jnp.where(causal, dot(k, qt, precision=highest), 0.0)
    b_col = jnp.exp(ccol[TOK // 2 - 1 : TOK // 2, :] - ccol)
    a_row = jnp.exp(crow - crow[:, TOK // 2 - 1 : TOK // 2])
    suffix = (row >= col).astype(F32).astype(BF16)
    before = row < col
    t0 = (row < 64).astype(F32).astype(BF16)
    t1 = (row >= 64).astype(F32).astype(BF16)
    dsc[...] = jnp.zeros(dsc.shape, F32)

    def inside(p):
        sl = slice(p * 128, (p + 1) * 128)
        dop = do_ref[:, sl]
        dot_t = dop.astype(F32).T.astype(BF16)
        bdt = jnp.concatenate([dot_t * t0, dot_t * t1], axis=1)
        bdo = jnp.concatenate([dop * m0, dop * m1], axis=0)
        bd_t[p] = bdt
        bd[p] = bdo
        dmix = dot(v_ref[:, sl], bdt)
        xs = []
        for j in range(2):
            head = 2 * p + j
            dm = dmix[:, j * 128 : (j + 1) * 128]
            e = jnp.where(causal, b_col[:, head : head + 1] * a_row[head : head + 1, :], 0.0)
            mix = e * scores
            dsc[...] += e * dm
            y = dot((mix * dm).astype(BF16), suffix)
            dlogt_ref[head : head + 1, :] = jnp.sum(
                jnp.where(before, y, 0.0), axis=0, keepdims=True
            )
            xs.append(mix.astype(BF16))
        dv_ref[:, sl] = dot(jnp.concatenate(xs, axis=1), bdo)

    for p in range(pairs // 2):
        inside(p)

    part = nd.at[pl.ds(0, chips - 1), 4]
    decays_in = near(part, part, d_sem.at[0], d_sem.at[1])
    decays_in.wait_recv()
    for b in range(1, nb + 1):
        for i in range(chips >> b):
            lo = offs[b - 1] + 2 * i
            nd[offs[b] + i, 4] = nd[lo + 1, 4] * nd[lo, 4]

    def spread_decay(d):
        to = (group + d) % groups
        remote(
            nd.at[top, 4], zb.at[group, 4], z_send.at[groups], zd_recv.at[group], (to, me)
        ).start()

    loop(1, groups, spread_decay)
    sub = iota((8, 128), 0)
    for c in range(chips):
        pre = jnp.ones((8, 128), F32)
        rows = pre
        for b in range(nb):
            rows = jnp.where(sub >= b, pre, rows)
            if (c >> b) & 1:
                pre = pre * nd[offs[b] + (c >> b) - 1, 4]
        pks[c] = jnp.where(sub >= nb, pre, rows)

    def send_scales(i):
        to = shifted(i)
        remote(
            pks.at[to], pk.at[chip], k_sem.at[0], k_sem.at[1], (group, 2 * to + core)
        ).start()

    loop(1, chips, send_scales)
    pk[chip] = pks[chip]

    part = nd.at[pl.ds(0, chips - 1), 0:4]
    scattered = near(part, part, a_sem.at[0], a_sem.at[1])
    scattered.wait_recv()
    for b in range(1, nb + 1):
        for i in range(chips >> b):
            lo = offs[b - 1] + 2 * i
            right = nd[lo + 1, 4]
            nd[offs[b] + i, 0:4] = right[None] * nd[lo, 0:4] + nd[lo + 1, 0:4]

    def up(d):
        return remote(
            nd.at[top, 0:4], zb.at[group, 0:4], z_send.at[d], z_recv.at[group], (group + d, me)
        )

    for d in range(1, groups):

        @pl.when(group + d < groups)
        def _():
            up(d).start()

    def where_on(r):
        if routes[r][2]:
            return xpos, ypos, lambda f, s: f * ydim + s
        return ypos, xpos, lambda f, s: s * ydim + f

    def reads(lev):
        if lev >= nb:
            return bit_of(group, lev - nb)
        return bit_of(chip, lev)

    def when_level(lev, fn):
        if lev >= nb:
            pl.when(bit_of(group, lev - nb))(fn)
        else:
            fn()

    def first_phase(r):
        lev, tiles, rows_first, first, second, users, arrays, slot = routes[r]
        fpos, spos, at = where_on(r)

        def source(a, f):
            if lev >= nb:
                return hz.at[lev - nb, tiles]
            if rows_first:
                return nd.at[offs[lev] + f * (ydim >> lev) + 2 * a, 0:4]
            return nd.at[offs[lev] + 2 * a, 0:4]

        def go():
            for d in range(1, first):
                f = (fpos + d) % first
                for a in range(len(arrays)):
                    remote(
                        source(a, f),
                        ring.at[slot + a, fpos, tiles],
                        r_send.at[slot + a],
                        r_recv.at[slot + a],
                        (group, 2 * at(f, spos) + core),
                    ).start()
            for a in range(len(arrays)):
                ring[slot + a, fpos, tiles] = source(a, fpos)[...]

        if lev >= nb:
            go()
        else:
            when_level(lev, go)

    def second_phase(r):
        lev, tiles, rows_first, first, second, users, arrays, slot = routes[r]
        fpos, spos, at = where_on(r)

        def go():
            if first > 1:
                for a in range(len(arrays)):
                    part = ring.at[slot + a, pl.ds(0, first - 1), tiles]
                    near(part, part, r_send.at[slot + a], r_recv.at[slot + a]).wait_recv()
            for a, readers in enumerate(arrays):
                for s in readers:
                    there = h.at[lev, core, pl.ds(spos * first, first), tiles]

                    @pl.when(spos != s)
                    def _():
                        remote(
                            ring.at[slot + a, pl.ds(0, first), tiles],
                            there,
                            h_send.at[r],
                            h_recv.at[r],
                            (group, 2 * at(fpos, s) + core),
                        ).start()

                    @pl.when(spos == s)
                    def _():
                        there[...] = ring[slot + a, 0:first, tiles]

        when_level(lev, go)

    low = list(range(nb))
    high = list(range(nb, levels))
    low_ways = [r for lev in low for r in ways[lev]]
    high_ways = [r for lev in high for r in ways[lev]]
    for r in low_ways:
        first_phase(r)

    for p in range(pairs // 2, 3 * pairs // 4):
        inside(p)
    for r in low_ways:
        second_phase(r)
    for p in range(3 * pairs // 4, pairs):
        inside(p)

    coef[...] = jnp.ones((8, 128), F32)
    hz[...] = jnp.zeros(hz.shape, F32)
    for d in range(1, groups):
        far = group - d

        @pl.when(far >= 0)
        def _():
            slot = zb.at[far, 4]
            near(slot, slot, z_send.at[0], zd_recv.at[far]).wait_recv()
            slot = zb.at[far, 0:4]
            near(slot, slot, z_send.at[0], z_recv.at[far]).wait_recv()
            level = high_level(group, far, nz)
            hz[level] = hz[level] + coef[...][None] * zb[far, 0:4]
            before_far[d] = coef[...]
            coef[...] = coef[...] * zb[far, 4]

        l = log2(d)

        @pl.when(bit_of(group, l) & (group % 2**l + 2**l == d))
        def _():
            for r in ways[nb + l]:
                first_phase(r)

    q_low = qt.astype(BF16).astype(F32)
    q2 = jnp.concatenate([q_low, q_low], axis=1)
    loads[5].wait()
    for j in range(columns // per):
        lam_t[pl.ds(j * per, per)] = lam_ref[:, j * wide : (j + 1) * wide].T.reshape(
            per, heads, TOK
        )
    glam[...] = jnp.zeros(glam.shape, F32)
    rint[...] = jnp.zeros(rint.shape, F32)
    rnear[...] = jnp.zeros(rnear.shape, F32)
    dq_acc[...] = jnp.zeros(dq_acc.shape, F32)
    ids = [ids_ref[0, b] for b in range(1 + levels)]

    def spot(r, p):
        if routes[r][2]:
            return (p % ydim) * xdim + p // ydim
        return p

    def levels_step(group_levels, p):
        gr2 = jnp.exp(crow_ref[pl.ds(2 * p, 2), :])
        mate_scale = jnp.where(core == 1, sibd[p, 0:1], jnp.ones((1, 128), F32))
        helds, ws, scales = [], [], []
        for b in group_levels:
            if b == 0:
                held = sib[p].reshape(64, 128)
                scales.append(None)
            else:
                scales.append(mate_scale * pk[p, b - 1 : b])
                held = jnp.concatenate(
                    [h[b - 1, j, spot(r, p), routes[r][1]] for j in range(2) for r in ways[b - 1]],
                    axis=0,
                )
                held = jnp.where(reads(b - 1), held.reshape(64, 128) * scales[-1], 0.0)
            helds.append(held.astype(BF16))
            ws.append(lam_t[ids[b], pl.ds(2 * p, 2), :] * gr2)
        m = dot(jnp.concatenate(helds, axis=0), bd_t[p])
        wqs = []
        acc = dq_acc[...]
        r2 = jnp.zeros((2, TOK), F32)
        for i, b in enumerate(group_levels):
            mi = m[64 * i : 64 * (i + 1)]
            w = jnp.concatenate([ws[i][0:1], ws[i][1:2]], axis=1)
            gsum = jnp.sum(q2 * mi, axis=0, keepdims=True)
            acc = acc + w * mi
            wqs.append((w * q2).astype(BF16))
            g2 = jnp.concatenate([gsum[:, 0:128], gsum[:, 128:256]], axis=0)
            glam[b, pl.ds(2 * p, 2), :] = gr2 * g2
            r2 = r2 + ws[i] * g2
        dq_acc[...] = acc
        if group_levels == [0]:
            rnear[pl.ds(2 * p, 2), :] = r2
        else:
            rint[pl.ds(2 * p, 2), :] += r2
        grad = dot(jnp.concatenate(wqs, axis=0), bd[p])
        for i, b in enumerate(group_levels):
            gi = grad[64 * i : 64 * (i + 1)]
            if b == 0:
                gn[p] = gi.reshape(2, 4, 8, 128)
            else:
                gi = (gi * scales[i]).reshape(2, 4, 8, 128)
                for r in ways[b - 1]:
                    tiles = routes[r][1]
                    for j in range(2):
                        g[b - 1, j, spot(r, p), tiles] = gi[j, tiles]

    def levels_pass(group_levels):
        def two(i):
            levels_step(group_levels, 2 * i)
            levels_step(group_levels, 2 * i + 1)

        loop(0, pairs // 2, two)

    g0_copy = near(gn, g0, g0_sem.at[0], g0_sem.at[1])

    for r in high_ways:
        second_phase(r)

    def swap(lev):
        return near(g.at[lev, 1 - core], x.at[lev], x_send.at[lev], x_recv.at[lev])

    def fetch(levs):
        for lev in levs:

            @pl.when(reads(lev))
            def _():
                for r in ways[lev]:
                    _, tiles, _, first, second, _, _, _ = routes[r]
                    if second > 1:
                        part = h.at[lev, core, pl.ds(0, (second - 1) * first), tiles]
                        near(part, part, h_send.at[r], h_recv.at[r]).wait_recv()
                ours = h.at[lev, core]
                near(ours, ours, f_send.at[lev], f_recv.at[lev]).start()

        for lev in levs:

            @pl.when(reads(lev))
            def _():
                theirs = h.at[lev, 1 - core]
                near(theirs, theirs, f_send.at[lev], f_recv.at[lev]).wait_recv()

    def give_back(levs):
        for lev in levs:

            @pl.when(reads(lev))
            def _():
                swap(lev).start()

        def send_back(r):
            lev, tiles, _, first, second, _, _, _ = routes[r]
            fpos, spos, at = where_on(r)
            for d in range(1, second):
                s = (spos + d) % second
                remote(
                    st.at[lev, pl.ds(s * first, first), tiles],
                    back.at[lev, spos, pl.ds(0, first), tiles],
                    b_send.at[r],
                    b_recv.at[r],
                    (group, 2 * at(fpos, s) + core),
                ).start()
            back[lev, spos, 0:first, tiles] = st[lev, pl.ds(spos * first, first), tiles]

        for lev in levs:

            @pl.when(reads(lev))
            def _():
                swap(lev).wait_recv()

                def add(c):
                    st[lev, c] = g[lev, core, c] + x[lev, c]

                loop(0, chips, add)
                for r in ways[lev]:
                    send_back(r)

    def gather_back(r):
        lev, tiles, rows_first, first, second, users, arrays, slot = routes[r]
        fpos, spos, at = where_on(r)

        def arrived(count):
            if count:
                part = back.at[lev, pl.ds(0, count), pl.ds(0, first), tiles]
                near(part, part, b_send.at[r], b_recv.at[r]).wait_recv()

        def go():
            if lev >= nb:
                arrived(second - 1)
            else:

                @pl.when(reads(lev))
                def _():
                    arrived(len(users) - 1)

                @pl.when(jnp.logical_not(reads(lev)))
                def _():
                    arrived(len(users))

            for a, readers in enumerate(arrays):
                for f in range(first):
                    total = back[lev, readers[0], f, tiles]
                    for s in readers[1:]:
                        total = total + back[lev, s, f, tiles]
                    q_sum[slot + a, f, tiles] = total
                for d in range(1, first):
                    f = (fpos + d) % first
                    remote(
                        q_sum.at[slot + a, f, tiles],
                        parts.at[slot + a, fpos, tiles],
                        q_send.at[slot + a],
                        q_recv.at[slot + a],
                        (group, 2 * at(f, spos) + core),
                    ).start()
                parts[slot + a, fpos, tiles] = q_sum[slot + a, fpos, tiles]

        when_level(lev, go)

    def parts_in(r):
        lev, tiles, rows_first, first, second, users, arrays, slot = routes[r]
        if first > 1:
            for a in range(len(arrays)):
                part = parts.at[slot + a, pl.ds(0, first - 1), tiles]
                near(part, part, q_send.at[slot + a], q_recv.at[slot + a]).wait_recv()

    @pl.when(core == 1)
    def _():
        rest.wait_recv()
        levels_pass([0])
        g0_copy.start()

    tail_col = jnp.exp(ccol[TOK - 1 : TOK, :] - ccol)
    for p in range(pairs):
        tails[p] = jnp.where(
            col < 64, tail_col[:, 2 * p : 2 * p + 1], tail_col[:, 2 * p + 1 : 2 * p + 2]
        )
        vp = v_ref[:, p * 128 : (p + 1) * 128].astype(F32)
        decayed[p] = (tails[p] * vp).astype(BF16)
    k_low = k.astype(BF16)
    kt_low = kt.astype(BF16).astype(F32)

    k_part = pk.at[pl.ds(0, chips - 1)]
    scales_in = near(k_part, k_part, k_sem.at[0], k_sem.at[1])
    scales_in.wait_recv()
    fetch(low)
    levels_pass([b + 1 for b in low])
    fetch(high)

    @pl.when(group > 0)
    def _():
        levels_pass([b + 1 for b in high])

    give_back(high)

    pulls = rint[...]
    rsum = jnp.broadcast_to(jnp.sum(pulls, axis=1, keepdims=True), (heads, TOK))
    lane = iota((8, 128), 1)
    first_lane = jnp.where((sub == 0) & (lane == 0), 1.0, 0.0)
    mid_lane = jnp.where((sub == 0) & (lane == 64), 1.0, 0.0)
    for p in range(pairs):
        rs[p] = first_lane * rsum[2 * p : 2 * p + 1] + mid_lane * rsum[2 * p + 1 : 2 * p + 2]

    def send_sums(i):
        to = shifted(i)
        remote(
            rs.at[to], rr.at[chip], t_sem.at[0], t_sem.at[1], (group, 2 * to + core)
        ).start()

    loop(1, chips, send_sums)
    rr[chip] = rs[chip]
    for r in high_ways:
        gather_back(r)
    give_back(low)

    def sum_high(r):
        lev, tiles, _, first, _, _, _, slot = routes[r]

        @pl.when(reads(lev))
        def _():
            parts_in(r)
            total = parts[slot, 0, tiles]
            for f in range(1, first):
                total = total + parts[slot, f, tiles]
            u[lev - nb, tiles] = total

    for r in high_ways:
        sum_high(r)

    coef[...] = jnp.zeros((8, 128), F32)
    for d in reversed(range(1, groups)):

        @pl.when(group - d >= 0)
        def _():
            level = high_level(group, group - d, nz)
            grad = u[level]
            z_out[d, 0:4] = grad
            z_out[d, 4] = coef[...]
            remote(
                z_out.at[d], zu.at[group], u_send.at[d], u_recv.at[group], (group - d, me)
            ).start()
            coef[...] = coef[...] + before_far[d] * jnp.sum(grad * zb[group - d, 0:4], axis=0)

    for r in low_ways:
        gather_back(r)

    for j in range(columns // per):
        slabs = []
        for p in range(j * per, (j + 1) * per):
            total = jnp.zeros((heads, TOK), F32)
            for b in range(1 + levels):
                total = total + jnp.where(ids[b] == p, glam[b], 0.0)
            slabs.append(total)
        dlam_ref[:, j * wide : (j + 1) * wide] = jnp.concatenate(slabs, axis=0).T
    results[3].start()
    even = jnp.where(core == 0, 1.0, 0.0)
    dlogt_ref[...] += (
        dot(pulls + rnear[...], (row >= col).astype(F32), precision=highest) - even * rsum
    )
    dqi = (dq_acc[:, 0:128] + dq_acc[:, 128:256]).astype(BF16).astype(F32)
    dst = dsc[...]
    dqt_ref[...] = dqi + dot(kt, dst, precision=highest)
    dkt_ref[...] = dot(dst, q, precision=highest).T
    results[1].start()

    for r in low_ways:
        lev, tiles, rows_first, first, second, users, arrays, slot = routes[r]
        parts_in(r)
        for a in range(len(arrays)):
            if rows_first:
                for f in range(first):
                    dn[offs[lev] + f * (ydim >> lev) + 2 * a, 0:4] = parts[slot + a, f]
            else:
                total = parts[slot + a, 0]
                for f in range(1, first):
                    total = total + parts[slot + a, f]
                dn[offs[lev] + 2 * a, 0:4] = total

    coef[...] = jnp.ones((8, 128), F32)
    dn[top, 0:4] = jnp.zeros((4, 8, 128), F32)
    cown[...] = jnp.zeros((8, 128), F32)
    for l in range(nz):

        @pl.when(bit_of(group, l))
        def _():
            cown[...] = cown[...] + jnp.sum(u[l] * hz[l], axis=0)

    for d in range(1, groups):

        @pl.when(group + d < groups)
        def _():
            far = zb.at[group + d, 4]
            near(far, far, z_send.at[0], zd_recv.at[group + d]).wait_recv()
            slot = zu.at[group + d]
            near(slot, slot, u_send.at[d], u_recv.at[group + d]).wait_recv()
            dn[top, 0:4] = dn[top, 0:4] + coef[...][None] * zu[group + d, 0:4]
            cown[...] = cown[...] + zu[group + d, 4]
            coef[...] = coef[...] * zb[group + d, 4]

    loads[6].wait()
    fu = jnp.concatenate([fu_ref[0], fu_ref[1]], axis=1).reshape(4, 8, 128)
    dn[top, 0:4] = dn[top, 0:4] + coef[...][None] * fu
    earlier = hz[0]
    for l in range(1, nz):
        earlier = earlier + hz[l]
    carry = cown[...] + coef[...] * nd[top, 4] * jnp.sum(earlier * fu, axis=0)
    for b in reversed(range(nb)):
        for i in range(0, chips >> b, 2):
            left = offs[b] + i
            parent = dn[offs[b + 1] + i // 2, 0:4]
            dn[left, 0:4] = dn[left, 0:4] + nd[left + 1, 4][None] * parent
            dn[left + 1, 0:4] = parent

    t_part = rr.at[pl.ds(0, chips - 1)]
    sums_in = near(t_part, t_part, t_sem.at[0], t_sem.at[1])
    sums_in.wait_recv()
    now = jnp.sum(carry, axis=0, keepdims=True)
    for c in range(chips):
        step = jnp.sum(nd[c, 0:4] * dn[c, 0:4], axis=0) - rr[c]
        then = now + jnp.sum(step, axis=0, keepdims=True)
        dn[c, 4] = jnp.where(sub == 0, now, jnp.where(sub == 1, then, 0.0))
        now = then

    def give(a, i):
        to = shifted(a * ydim + i)
        remote(
            dn.at[to], ds.at[core, a, i], o_sem.at[0], o_sem.at[1 + a], (group, 2 * to + core)
        ).start()

    for a in range(xdim):
        loop(0 if a else 1, ydim, partial(give, a))
    ds[core, 0, 0] = dn[chip, 0:5]
    for a in range(xdim):
        part = ds.at[core, a] if a else ds.at[core, a, pl.ds(0, ydim - 1)]
        near(part, part, o_sem.at[0], o_sem.at[1 + a]).wait_recv()
        row_in = ds.at[core, a]
        near(row_in, row_in, w_sem.at[0, a], w_sem.at[1, a]).start()

    def all_sent(r):
        lev, tiles, rows_first, first, second, users, arrays, slot = routes[r]

        def out_of_ring(count):
            if count:
                part = h.at[lev, core, pl.ds(0, count * first), tiles]
                near(part, part, h_send.at[r], h_recv.at[r]).wait_send()

        def sends():
            if first > 1:
                for a in range(len(arrays)):
                    part = ring.at[slot + a, pl.ds(0, first - 1), tiles]
                    near(part, part, r_send.at[slot + a], r_recv.at[slot + a]).wait_send()
                    near(part, part, q_send.at[slot + a], q_recv.at[slot + a]).wait_send()
            if lev >= nb:
                out_of_ring(second - 1)

        when_level(lev, sends)

        if lev < nb:

            @pl.when(jnp.logical_not(reads(lev)))
            def _():
                out_of_ring(len(users))

        @pl.when(reads(lev))
        def _():
            if lev < nb:
                out_of_ring(len(users) - 1)
            if second > 1:
                part = st.at[lev, pl.ds(0, (second - 1) * first), tiles]
                near(part, part, b_send.at[r], b_recv.at[r]).wait_send()

    for r in range(len(routes)):
        all_sent(r)
    for lev in range(levels):

        @pl.when(reads(lev))
        def _():
            ours = h.at[lev, core]
            near(ours, ours, f_send.at[lev], f_recv.at[lev]).wait_send()
            swap(lev).wait_send()

    for d in range(1, groups):

        @pl.when(group + d < groups)
        def _():
            up(d).wait_send()

        @pl.when(group - d >= 0)
        def _():
            near(z_out.at[d], z_out.at[d], u_send.at[d], u_recv.at[0]).wait_send()

    swap_half.wait_send()
    swap_dec.wait_send()
    scattered.wait_send()
    decays_in.wait_send()
    lines = zb.at[pl.ds(0, groups - 1), 4]
    near(lines, lines, z_send.at[groups], zd_recv.at[0]).wait_send()
    scales_in.wait_send()
    sums_in.wait_send()

    @pl.when(core == 1)
    def _():
        g0_copy.wait_send()

    @pl.when(core == 0)
    def _():
        rest.wait_send()
        g0_copy.wait_recv()

    part = dn.at[pl.ds(0, chips - 1)]
    near(part, part, o_sem.at[0], o_sem.at[1]).wait_send()

    def finish(a, i):
        p = ((xpos + xdim - a) % xdim) * ydim + (ypos + ydim - i) % ydim
        scale = jnp.where(core == 0, sibd[p], jnp.ones((8, 128), F32))
        dld = jnp.zeros((8, 128), F32)
        lows = []
        for j in range(2):
            grad = ds[j, a, i, 0:4]
            dot_own = jnp.sum(own[p, j] * grad, axis=0)
            dld = dld + jnp.where(sub == core, ds[j, a, i, 4], 0.0)
            dld = dld - jnp.where(core == 0, 0.0, dot_own)
            extra = jnp.where(core == 0, g0[p, j], 0.0)
            lows.append(grad * scale[None] + extra)
        low = jnp.concatenate(lows, axis=0).reshape(64, 128).astype(BF16)
        dld_ref[pl.ds(p, 1), :] = jnp.sum(dld, axis=0, keepdims=True)
        cols = pl.ds(pl.multiple_of(p * 128, 128), 128)
        dv_out[:, cols] = (dv_ref[:, cols] + tails[p] * dot(k_low, low)).astype(BF16)
        both_heads = jnp.concatenate([low * m0[0:64], low * m1[0:64]], axis=0)
        dk = lax.dot_general(
            both_heads, decayed[p], (((1,), (1,)), ((), ())), preferred_element_type=F32
        )
        dkt_ref[...] += dk[0:64] + dk[64:128]
        lrow[pl.ds(2 * p, 1), :] = jnp.sum(kt_low * dk[0:64], axis=0, keepdims=True)
        lrow[pl.ds(2 * p + 1, 1), :] = jnp.sum(kt_low * dk[64:128], axis=0, keepdims=True)

    def row_there(a):
        theirs = ds.at[1 - core, a]
        both = near(theirs, theirs, w_sem.at[0, a], w_sem.at[1, a])
        both.wait_recv()
        both.wait_send()

    for a in range(xdim):
        row_there(a)
        for i in range(ydim):
            finish(a, i)
        cols = pl.ds(pl.multiple_of(((xpos + xdim - a) % xdim) * ydim * 128, 128), ydim * 128)
        results.append(
            pltpu.make_async_copy(dv_out.at[:, cols], dv_any.at[:, cols], out_sem.at[4 + a])
        )
        results[-1].start()
    results[0].start()
    head = iota((heads, pairs), 0)
    rows = dot((iota((heads, pairs), 1) == head // 2).astype(F32), dld_ref[...], precision=highest)
    side = iota((heads, TOK), 1) // 64 == iota((heads, TOK), 0) % 2
    dd = jnp.sum(jnp.where(side, rows, 0.0), axis=1, keepdims=True)
    dlogt_ref[...] += dot(lrow[...], (row < col).astype(F32), precision=highest) + dd
    results[2].start()
    for c in results:
        c.wait()


def end_kernel(*refs):
    n = (len(refs) - 2) // 3
    in_sem, out_sem = refs[-2:]
    loads, stores = [], []
    for i in range(n):
        src, dst, held = refs[i], refs[n + i], refs[2 * n + i]
        cuts = 4 if i == 0 else 1
        step = src.shape[0] // cuts
        for j in range(cuts):
            part = pl.ds(j * step, step)
            k = len(loads)
            loads.append(pltpu.make_async_copy(src.at[part], held.at[part], in_sem.at[k]))
            stores.append(pltpu.make_async_copy(held.at[part], dst.at[part], out_sem.at[k]))
    for c in loads:
        c.start()
    for load, store in zip(loads, stores):
        load.wait()
        store.start()
    for c in stores:
        c.wait()


def body(
    values, state_input, state_output, log_decay, level_lam, level_ids, upstream, final_upstream
):
    shards, groups = lax.axis_size("shard"), lax.axis_size("grp")
    chips = shards // 2
    nb, nz = log2(chips), log2(groups)
    levels = nb + nz
    heads = log_decay.shape[1]
    columns = level_lam.shape[1] // heads
    params = partial(pltpu.CompilerParams, vmem_limit_bytes=VMEM_CAP)
    dma = pltpu.SemaphoreType.DMA
    tile = (4, 8, 128)
    kt = state_input.T
    ydim = 2 ** ((nb + 1) // 2)
    routes = routes_of(nb, nz, chips // ydim, ydim)
    slots = sum(len(route[6]) for route in routes)
    count = len(routes)

    shapes = (
        jax.ShapeDtypeStruct((TOK, heads * 64), BF16),
        f32(64, TOK),
        f32(64, TOK),
        f32(heads, TOK),
        f32(TOK, columns * heads),
    )
    anywhere = pl.BlockSpec(memory_space=pl.ANY)
    parts = pl.pallas_call(
        partial(main_kernel, shards, groups),
        out_shape=shapes,
        in_specs=[pl.BlockSpec(memory_space=pltpu.SMEM)]
        + [anywhere] * 7,
        out_specs=(anywhere,) * 5,
        scratch_shapes=[
            pltpu.VMEM((TOK, heads * 64), BF16),
            pltpu.VMEM((64, TOK), F32),
            pltpu.VMEM((64, TOK), F32),
            pltpu.VMEM((heads, TOK), F32),
            pltpu.VMEM((TOK, columns * heads), F32),
            dma((4 + chips // ydim,)),
            pltpu.VMEM((TOK, heads * 64), F32),
            pltpu.VMEM((heads, TOK), F32),
            pltpu.VMEM((chips, 128), F32),
            pltpu.VMEM((chips, TOK, 128), F32),
            pltpu.VMEM((chips, TOK, 128), BF16),
            pltpu.VMEM((heads, TOK), F32),
            pltpu.VMEM((TOK, heads * 64), BF16),
            pltpu.VMEM((TOK, heads * 64), BF16),
            pltpu.VMEM((64, TOK), F32),
            pltpu.VMEM((64, TOK), F32),
            pltpu.VMEM((heads, TOK), F32),
            pltpu.VMEM((TOK, columns * heads), F32),
            pltpu.VMEM((2, 32, 64), F32),
            dma((7,)),
            pltpu.VMEM((chips, 128, 256), BF16),
            pltpu.VMEM((chips, 256, 128), BF16),
            pltpu.VMEM((columns, heads, TOK), F32),
            pltpu.VMEM((1 + levels, heads, TOK), F32),
            pltpu.VMEM((heads, TOK), F32),
            pltpu.VMEM((heads, TOK), F32),
            pltpu.VMEM((64, 256), F32),
            pltpu.VMEM((TOK, TOK), F32),
            pltpu.VMEM((levels, 2, chips) + tile, F32),
            pltpu.VMEM((chips, 2) + tile, F32),
            pltpu.VMEM((chips, 2) + tile, F32),
            pltpu.VMEM((chips, 8, 128), F32),
            pltpu.VMEM((chips, 2) + tile, F32),
            pltpu.VMEM((chips, 8, 128), F32),
            pltpu.VMEM((chips, 5, 8, 128), F32),
            pltpu.VMEM((2 * chips, 5, 8, 128), F32),
            pltpu.VMEM((groups, 5, 8, 128), F32),
            pltpu.VMEM((nz,) + tile, F32),
            pltpu.VMEM((chips, 8, 128), F32),
            pltpu.VMEM((chips, 8, 128), F32),
            pltpu.VMEM((8, 128), F32),
            pltpu.VMEM((groups, 8, 128), F32),
            pltpu.VMEM((slots, ydim) + tile, F32),
            pltpu.VMEM((levels, 2, chips) + tile, F32),
            pltpu.VMEM((levels, chips) + tile, F32),
            pltpu.VMEM((levels, chips) + tile, F32),
            pltpu.VMEM((levels, ydim, ydim) + tile, F32),
            pltpu.VMEM((slots, ydim) + tile, F32),
            pltpu.VMEM((slots, ydim) + tile, F32),
            pltpu.VMEM((chips, 8, 128), F32),
            pltpu.VMEM((chips, 8, 128), F32),
            pltpu.VMEM((nz,) + tile, F32),
            pltpu.VMEM((groups, 5, 8, 128), F32),
            pltpu.VMEM((groups, 5, 8, 128), F32),
            pltpu.VMEM((8, 128), F32),
            pltpu.VMEM((2 * chips, 5, 8, 128), F32),
            pltpu.VMEM((2, chips // ydim, ydim, 5, 8, 128), F32),
            pltpu.VMEM((chips, 2) + tile, F32),
            dma((6,)),
            dma((2,)),
            dma((groups + 1,)),
            dma((groups,)),
            dma((groups,)),
            dma((2,)),
            dma((2,)),
            dma((slots,)),
            dma((slots,)),
            dma((count,)),
            dma((count,)),
            dma((levels,)),
            dma((levels,)),
            dma((2,)),
            dma((levels,)),
            dma((levels,)),
            dma((count,)),
            dma((count,)),
            dma((slots,)),
            dma((slots,)),
            dma((2,)),
            dma((groups,)),
            dma((groups,)),
            dma((1 + chips // ydim,)),
            dma((2, chips // ydim)),
        ],
        compiler_params=params(collective_id=0, has_side_effects=True),
        name="main",
    )(
        level_ids,
        values,
        upstream,
        kt,
        state_output.T,
        log_decay.T,
        level_lam,
        final_upstream.reshape(chips, 2, 2, 32, 64),
    )

    dv, dk, dq, dlog, dlam = pl.pallas_call(
        end_kernel,
        out_shape=shapes,
        in_specs=[anywhere] * 5,
        out_specs=(anywhere,) * 5,
        scratch_shapes=[pltpu.VMEM(x.shape, x.dtype) for x in shapes] + [dma((8,)), dma((8,))],
        compiler_params=params(),
        name="end",
    )(*parts)
    return (dv, dk.T, dq.T, dlog.T, dlam)


def solution(mesh):
    spec = P(("grp", "shard"), None)
    return jax.shard_map(
        body,
        mesh=mesh,
        in_specs=(spec,) * 7 + (P(),),
        out_specs=(spec,) * 5,
        check_vma=False,
    )
```

```python
from functools import partial

import jax
import jax.numpy as jnp
from jax import lax
from jax.experimental import pallas as pl
from jax.experimental.pallas import tpu as pltpu
from jax.sharding import PartitionSpec as P

highest = lax.Precision.HIGHEST
MESH = pl.DeviceIdType.MESH
F32 = jnp.float32
BF16 = jnp.bfloat16
TOK = 128
VMEM_CAP = 62 * 1024 * 1024


def log2(n):
    return n.bit_length() - 1


def f32(*shape):
    return jax.ShapeDtypeStruct(shape, F32)


def iota(shape, dim):
    return lax.broadcasted_iota(jnp.int32, shape, dim)


def dot(a, b, **kw):
    return jnp.dot(a, b, preferred_element_type=F32, **kw)


def place():
    group = lax.axis_index("grp")
    me = lax.axis_index("shard")
    return group, me, me // 2, me % 2


def remote(src, dst, send, recv, device):
    return pltpu.make_async_remote_copy(
        src_ref=src, dst_ref=dst, send_sem=send, recv_sem=recv, device_id=device, device_id_type=MESH
    )


def loop(start, stop, fn):
    def step(i, carry):
        fn(i)
        return carry

    lax.fori_loop(start, stop, step, 0)


def enter(group, me, chip, core, chips, groups):
    barrier = pltpu.get_barrier_semaphore()

    def greet(shard, grp):
        pl.semaphore_signal(barrier, inc=1, device_id=(grp, shard), device_id_type=MESH)

    loop(1, chips, lambda d: greet(2 * ((chip + d) % chips) + core, group))
    loop(1, groups, lambda d: greet(me, (group + d) % groups))
    greet(me + 1 - 2 * core, group)
    return lambda: pl.semaphore_wait(barrier, chips + groups - 1)


def offsets(chips):
    offs, at, n = [], 0, chips
    while n >= 1:
        offs.append(at)
        at += n
        n //= 2
    return offs


def high_level(group, far, bits):
    level = jnp.int32(0)
    for b in range(1, bits):
        level = jnp.where(group // 2**b != far // 2**b, jnp.int32(b), level)
    return level


def bit_of(x, b):
    return (x // 2**b) % 2 == 1


def routes_of(nb, nz, xdim, ydim):
    routes, slot = [], 0
    ybits = log2(ydim)
    split = nb + min(1, nz - 1)
    for lev in range(nb + nz):
        if lev == split:
            ways = [(0, 2, True), (2, 4, False)]
        else:
            ways = [(0, 4, lev < ybits or nb <= lev < split)]
        for t0, t1, rows_first in ways:
            first, second = (xdim, ydim) if rows_first else (ydim, xdim)
            if lev < nb:
                bit = lev if rows_first else lev - ybits
                users = [s for s in range(second) if (s >> bit) & 1]
                arrays = [
                    [s for s in users if s >> (bit + 1) == a] for a in range(second >> (bit + 1))
                ]
            else:
                users = list(range(second))
                arrays = [users]
            routes.append((lev, slice(t0, t1), rows_first, first, second, users, arrays, slot))
            slot += len(arrays)
    return routes


def main_kernel(
    shards,
    groups,
    ids_ref,
    v_any,
    do_any,
    kt_any,
    qt_any,
    ldt_any,
    lam_any,
    fu_any,
    dv_any,
    dkt_any,
    dqt_any,
    dlogt_any,
    dlam_any,
    dv_out,
    dkt_ref,
    dqt_ref,
    dlogt_ref,
    dlam_ref,
    out_sem,
    dv_ref,
    crow_ref,
    dld_ref,
    tails,
    decayed,
    lrow,
    v_ref,
    do_ref,
    kt_ref,
    qt_ref,
    ldt_ref,
    lam_ref,
    fu_ref,
    in_sem,
    bd_t,
    bd,
    lam_t,
    glam,
    rint,
    rnear,
    dq_acc,
    dsc,
    g,
    gn,
    own,
    dec,
    sib,
    sibd,
    blk,
    nd,
    zb,
    hz,
    pks,
    pk,
    coef,
    before_far,
    ring,
    h,
    x,
    st,
    back,
    q_sum,
    parts,
    rs,
    rr,
    u,
    zu,
    z_out,
    cown,
    dn,
    ds,
    g0,
    s_sem,
    a_sem,
    z_send,
    z_recv,
    zd_recv,
    d_sem,
    k_sem,
    r_send,
    r_recv,
    h_send,
    h_recv,
    f_send,
    f_recv,
    g0_sem,
    x_send,
    x_recv,
    b_send,
    b_recv,
    q_send,
    q_recv,
    t_sem,
    u_send,
    u_recv,
    o_sem,
    w_sem,
):
    chips = shards // 2
    pairs = chips
    heads = shards
    nb, nz = log2(chips), log2(groups)
    levels = nb + nz
    columns = lam_t.shape[0]
    ydim = 2 ** ((nb + 1) // 2)
    xdim = chips // ydim
    group, me, chip, core = place()
    mate = me + 1 - 2 * core
    xpos, ypos = chip // ydim, chip % ydim
    offs = offsets(chips)
    top = offs[nb]
    wide = min(128, columns * heads)
    per = wide // heads

    routes = routes_of(nb, nz, xdim, ydim)
    ways = [[r for r in range(len(routes)) if routes[r][0] == lev] for lev in range(levels)]

    def shifted(i):
        return ((xpos + i // ydim) % xdim) * ydim + (ypos + i % ydim) % ydim

    def near(src, dst, send, recv):
        return remote(src, dst, send, recv, (group, mate))

    loads = [
        pltpu.make_async_copy(a, b, in_sem.at[i])
        for i, (a, b) in enumerate(
            [
                (ldt_any, ldt_ref),
                (kt_any, kt_ref),
                (v_any, v_ref),
                (do_any, do_ref),
                (qt_any, qt_ref),
                (lam_any, lam_ref),
                (fu_any.at[chip, :, core], fu_ref),
            ]
        )
    ]
    for c in loads:
        c.start()
    results = [
        pltpu.make_async_copy(a, b, out_sem.at[i])
        for i, (a, b) in enumerate(
            [
                (dkt_ref, dkt_any),
                (dqt_ref, dqt_any),
                (dlogt_ref, dlogt_any),
                (dlam_ref, dlam_any),
            ]
        )
    ]
    wait_entry = enter(group, me, chip, core, chips, groups)

    row = iota((TOK, TOK), 0)
    col = iota((TOK, TOK), 1)
    upto = (row <= col).astype(F32)
    half = (col < 64).astype(F32)
    m0 = half.astype(BF16)
    m1 = (1.0 - half).astype(BF16)
    loads[0].wait()
    crow = dot(ldt_ref[...], upto, precision=highest)
    crow_ref[...] = crow
    last = jnp.broadcast_to(crow[:, TOK - 1 : TOK], (heads, TOK))
    tail = jnp.exp(last - crow)
    full = jnp.exp(last)
    loads[1].wait()
    kt = kt_ref[...]
    loads[2].wait()
    for p in range(pairs):
        k2 = jnp.concatenate(
            [kt * tail[2 * p : 2 * p + 1], kt * tail[2 * p + 1 : 2 * p + 2]], axis=1
        ).astype(BF16)
        vp = v_ref[:, p * 128 : (p + 1) * 128]
        s = dot(k2, jnp.concatenate([vp * m0, vp * m1], axis=0))
        own[p] = s.reshape(2, 4, 8, 128)
        dec[p] = (
            half[0:8] * full[2 * p : 2 * p + 1] + (1.0 - half[0:8]) * full[2 * p + 1 : 2 * p + 2]
        )

    wait_entry()
    swap_half = near(own.at[:, 1 - core], sib.at[:, 1 - core], s_sem.at[0], s_sem.at[1])
    swap_dec = near(dec, sibd, s_sem.at[2], s_sem.at[3])
    rest = near(own.at[:, core], sib.at[:, core], s_sem.at[4], s_sem.at[5])
    swap_dec.start()
    swap_half.start()

    @pl.when(core == 0)
    def _():
        rest.start()

    swap_dec.wait_recv()

    def merge_decays(p):
        blk[p, 4] = dec[p] * sibd[p]

    loop(0, pairs, merge_decays)

    def scatter_decays(i):
        to = shifted(i)
        remote(
            blk.at[to, 4], nd.at[chip, 4], d_sem.at[0], d_sem.at[1], (group, 2 * to + core)
        ).start()

    loop(1, chips, scatter_decays)
    nd[chip, 4] = blk[chip, 4]
    swap_half.wait_recv()

    def merge_cores(p):
        a = own[p, core]
        b = sib[p, core]
        left = jnp.where(core == 0, a, b)
        right = jnp.where(core == 0, b, a)
        drow = jnp.where(core == 0, sibd[p], dec[p])
        blk[p, 0:4] = drow[None] * left + right

    loop(0, pairs, merge_cores)

    def scatter(i):
        to = shifted(i)
        remote(
            blk.at[to, 0:4],
            nd.at[chip, 0:4],
            a_sem.at[0],
            a_sem.at[1],
            (group, 2 * to + core),
        ).start()

    loop(1, chips, scatter)
    nd[chip, 0:4] = blk[chip, 0:4]

    loads[3].wait()
    loads[4].wait()
    qt = qt_ref[...]
    q = qt.T
    k = kt.T
    ccol = crow.T
    causal = row <= col
    scores = jnp.where(causal, dot(k, qt, precision=highest), 0.0)
    b_col = jnp.exp(ccol[TOK // 2 - 1 : TOK // 2, :] - ccol)
    a_row = jnp.exp(crow - crow[:, TOK // 2 - 1 : TOK // 2])
    suffix = (row >= col).astype(F32).astype(BF16)
    before = row < col
    t0 = (row < 64).astype(F32).astype(BF16)
    t1 = (row >= 64).astype(F32).astype(BF16)
    dsc[...] = jnp.zeros(dsc.shape, F32)

    def inside(p):
        sl = slice(p * 128, (p + 1) * 128)
        dop = do_ref[:, sl]
        dot_t = dop.astype(F32).T.astype(BF16)
        bdt = jnp.concatenate([dot_t * t0, dot_t * t1], axis=1)
        bdo = jnp.concatenate([dop * m0, dop * m1], axis=0)
        bd_t[p] = bdt
        bd[p] = bdo
        dmix = dot(v_ref[:, sl], bdt)
        xs = []
        for j in range(2):
            head = 2 * p + j
            dm = dmix[:, j * 128 : (j + 1) * 128]
            e = jnp.where(causal, b_col[:, head : head + 1] * a_row[head : head + 1, :], 0.0)
            mix = e * scores
            dsc[...] += e * dm
            y = dot((mix * dm).astype(BF16), suffix)
            dlogt_ref[head : head + 1, :] = jnp.sum(
                jnp.where(before, y, 0.0), axis=0, keepdims=True
            )
            xs.append(mix.astype(BF16))
        dv_ref[:, sl] = dot(jnp.concatenate(xs, axis=1), bdo)

    for p in range(pairs // 2):
        inside(p)

    part = nd.at[pl.ds(0, chips - 1), 4]
    decays_in = near(part, part, d_sem.at[0], d_sem.at[1])
    decays_in.wait_recv()
    for b in range(1, nb + 1):
        for i in range(chips >> b):
            lo = offs[b - 1] + 2 * i
            nd[offs[b] + i, 4] = nd[lo + 1, 4] * nd[lo, 4]

    def spread_decay(d):
        to = (group + d) % groups
        remote(
            nd.at[top, 4], zb.at[group, 4], z_send.at[groups], zd_recv.at[group], (to, me)
        ).start()

    loop(1, groups, spread_decay)
    sub = iota((8, 128), 0)
    for c in range(chips):
        pre = jnp.ones((8, 128), F32)
        rows = pre
        for b in range(nb):
            rows = jnp.where(sub >= b, pre, rows)
            if (c >> b) & 1:
                pre = pre * nd[offs[b] + (c >> b) - 1, 4]
        pks[c] = jnp.where(sub >= nb, pre, rows)

    def send_scales(i):
        to = shifted(i)
        remote(
            pks.at[to], pk.at[chip], k_sem.at[0], k_sem.at[1], (group, 2 * to + core)
        ).start()

    loop(1, chips, send_scales)
    pk[chip] = pks[chip]

    part = nd.at[pl.ds(0, chips - 1), 0:4]
    scattered = near(part, part, a_sem.at[0], a_sem.at[1])
    scattered.wait_recv()
    for b in range(1, nb + 1):
        for i in range(chips >> b):
            lo = offs[b - 1] + 2 * i
            right = nd[lo + 1, 4]
            nd[offs[b] + i, 0:4] = right[None] * nd[lo, 0:4] + nd[lo + 1, 0:4]

    def up(d):
        return remote(
            nd.at[top, 0:4], zb.at[group, 0:4], z_send.at[d], z_recv.at[group], (group + d, me)
        )

    for d in range(1, groups):

        @pl.when(group + d < groups)
        def _():
            up(d).start()

    def where_on(r):
        if routes[r][2]:
            return xpos, ypos, lambda f, s: f * ydim + s
        return ypos, xpos, lambda f, s: s * ydim + f

    def reads(lev):
        if lev >= nb:
            return bit_of(group, lev - nb)
        return bit_of(chip, lev)

    def when_level(lev, fn):
        if lev >= nb:
            pl.when(bit_of(group, lev - nb))(fn)
        else:
            fn()

    def first_phase(r):
        lev, tiles, rows_first, first, second, users, arrays, slot = routes[r]
        fpos, spos, at = where_on(r)

        def source(a, f):
            if lev >= nb:
                return hz.at[lev - nb, tiles]
            if rows_first:
                return nd.at[offs[lev] + f * (ydim >> lev) + 2 * a, 0:4]
            return nd.at[offs[lev] + 2 * a, 0:4]

        def go():
            for d in range(1, first):
                f = (fpos + d) % first
                for a in range(len(arrays)):
                    remote(
                        source(a, f),
                        ring.at[slot + a, fpos, tiles],
                        r_send.at[slot + a],
                        r_recv.at[slot + a],
                        (group, 2 * at(f, spos) + core),
                    ).start()
            for a in range(len(arrays)):
                ring[slot + a, fpos, tiles] = source(a, fpos)[...]

        if lev >= nb:
            go()
        else:
            when_level(lev, go)

    def second_phase(r):
        lev, tiles, rows_first, first, second, users, arrays, slot = routes[r]
        fpos, spos, at = where_on(r)

        def go():
            if first > 1:
                for a in range(len(arrays)):
                    part = ring.at[slot + a, pl.ds(0, first - 1), tiles]
                    near(part, part, r_send.at[slot + a], r_recv.at[slot + a]).wait_recv()
            for a, readers in enumerate(arrays):
                for s in readers:
                    there = h.at[lev, core, pl.ds(spos * first, first), tiles]

                    @pl.when(spos != s)
                    def _():
                        remote(
                            ring.at[slot + a, pl.ds(0, first), tiles],
                            there,
                            h_send.at[r],
                            h_recv.at[r],
                            (group, 2 * at(fpos, s) + core),
                        ).start()

                    @pl.when(spos == s)
                    def _():
                        there[...] = ring[slot + a, 0:first, tiles]

        when_level(lev, go)

    low = list(range(nb))
    high = list(range(nb, levels))
    low_ways = [r for lev in low for r in ways[lev]]
    high_ways = [r for lev in high for r in ways[lev]]
    for r in low_ways:
        first_phase(r)

    for p in range(pairs // 2, 3 * pairs // 4):
        inside(p)
    for r in low_ways:
        second_phase(r)
    for p in range(3 * pairs // 4, pairs):
        inside(p)

    coef[...] = jnp.ones((8, 128), F32)
    hz[...] = jnp.zeros(hz.shape, F32)
    for d in range(1, groups):
        far = group - d

        @pl.when(far >= 0)
        def _():
            slot = zb.at[far, 4]
            near(slot, slot, z_send.at[0], zd_recv.at[far]).wait_recv()
            slot = zb.at[far, 0:4]
            near(slot, slot, z_send.at[0], z_recv.at[far]).wait_recv()
            level = high_level(group, far, nz)
            hz[level] = hz[level] + coef[...][None] * zb[far, 0:4]
            before_far[d] = coef[...]
            coef[...] = coef[...] * zb[far, 4]

        l = log2(d)

        @pl.when(bit_of(group, l) & (group % 2**l + 2**l == d))
        def _():
            for r in ways[nb + l]:
                first_phase(r)

    q_low = qt.astype(BF16).astype(F32)
    q2 = jnp.concatenate([q_low, q_low], axis=1)
    loads[5].wait()
    for j in range(columns // per):
        lam_t[pl.ds(j * per, per)] = lam_ref[:, j * wide : (j + 1) * wide].T.reshape(
            per, heads, TOK
        )
    glam[...] = jnp.zeros(glam.shape, F32)
    rint[...] = jnp.zeros(rint.shape, F32)
    rnear[...] = jnp.zeros(rnear.shape, F32)
    dq_acc[...] = jnp.zeros(dq_acc.shape, F32)
    ids = [ids_ref[0, b] for b in range(1 + levels)]

    def spot(r, p):
        if routes[r][2]:
            return (p % ydim) * xdim + p // ydim
        return p

    def levels_step(group_levels, p):
        gr2 = jnp.exp(crow_ref[pl.ds(2 * p, 2), :])
        mate_scale = jnp.where(core == 1, sibd[p, 0:1], jnp.ones((1, 128), F32))
        helds, ws, scales = [], [], []
        for b in group_levels:
            if b == 0:
                held = sib[p].reshape(64, 128)
                scales.append(None)
            else:
                scales.append(mate_scale * pk[p, b - 1 : b])
                held = jnp.concatenate(
                    [h[b - 1, j, spot(r, p), routes[r][1]] for j in range(2) for r in ways[b - 1]],
                    axis=0,
                )
                held = jnp.where(reads(b - 1), held.reshape(64, 128) * scales[-1], 0.0)
            helds.append(held.astype(BF16))
            ws.append(lam_t[ids[b], pl.ds(2 * p, 2), :] * gr2)
        m = dot(jnp.concatenate(helds, axis=0), bd_t[p])
        wqs = []
        acc = dq_acc[...]
        r2 = jnp.zeros((2, TOK), F32)
        for i, b in enumerate(group_levels):
            mi = m[64 * i : 64 * (i + 1)]
            w = jnp.concatenate([ws[i][0:1], ws[i][1:2]], axis=1)
            gsum = jnp.sum(q2 * mi, axis=0, keepdims=True)
            acc = acc + w * mi
            wqs.append((w * q2).astype(BF16))
            g2 = jnp.concatenate([gsum[:, 0:128], gsum[:, 128:256]], axis=0)
            glam[b, pl.ds(2 * p, 2), :] = gr2 * g2
            r2 = r2 + ws[i] * g2
        dq_acc[...] = acc
        if group_levels == [0]:
            rnear[pl.ds(2 * p, 2), :] = r2
        else:
            rint[pl.ds(2 * p, 2), :] += r2
        grad = dot(jnp.concatenate(wqs, axis=0), bd[p])
        for i, b in enumerate(group_levels):
            gi = grad[64 * i : 64 * (i + 1)]
            if b == 0:
                gn[p] = gi.reshape(2, 4, 8, 128)
            else:
                gi = (gi * scales[i]).reshape(2, 4, 8, 128)
                for r in ways[b - 1]:
                    tiles = routes[r][1]
                    for j in range(2):
                        g[b - 1, j, spot(r, p), tiles] = gi[j, tiles]

    def levels_pass(group_levels):
        def two(i):
            levels_step(group_levels, 2 * i)
            levels_step(group_levels, 2 * i + 1)

        loop(0, pairs // 2, two)

    g0_copy = near(gn, g0, g0_sem.at[0], g0_sem.at[1])

    for r in high_ways:
        second_phase(r)

    def swap(lev):
        return near(g.at[lev, 1 - core], x.at[lev], x_send.at[lev], x_recv.at[lev])

    def fetch(levs):
        for lev in levs:

            @pl.when(reads(lev))
            def _():
                for r in ways[lev]:
                    _, tiles, _, first, second, _, _, _ = routes[r]
                    if second > 1:
                        part = h.at[lev, core, pl.ds(0, (second - 1) * first), tiles]
                        near(part, part, h_send.at[r], h_recv.at[r]).wait_recv()
                ours = h.at[lev, core]
                near(ours, ours, f_send.at[lev], f_recv.at[lev]).start()

        for lev in levs:

            @pl.when(reads(lev))
            def _():
                theirs = h.at[lev, 1 - core]
                near(theirs, theirs, f_send.at[lev], f_recv.at[lev]).wait_recv()

    def give_back(levs):
        for lev in levs:

            @pl.when(reads(lev))
            def _():
                swap(lev).start()

        def send_back(r):
            lev, tiles, _, first, second, _, _, _ = routes[r]
            fpos, spos, at = where_on(r)
            for d in range(1, second):
                s = (spos + d) % second
                remote(
                    st.at[lev, pl.ds(s * first, first), tiles],
                    back.at[lev, spos, pl.ds(0, first), tiles],
                    b_send.at[r],
                    b_recv.at[r],
                    (group, 2 * at(fpos, s) + core),
                ).start()
            back[lev, spos, 0:first, tiles] = st[lev, pl.ds(spos * first, first), tiles]

        for lev in levs:

            @pl.when(reads(lev))
            def _():
                swap(lev).wait_recv()

                def add(c):
                    st[lev, c] = g[lev, core, c] + x[lev, c]

                loop(0, chips, add)
                for r in ways[lev]:
                    send_back(r)

    def gather_back(r):
        lev, tiles, rows_first, first, second, users, arrays, slot = routes[r]
        fpos, spos, at = where_on(r)

        def arrived(count):
            if count:
                part = back.at[lev, pl.ds(0, count), pl.ds(0, first), tiles]
                near(part, part, b_send.at[r], b_recv.at[r]).wait_recv()

        def go():
            if lev >= nb:
                arrived(second - 1)
            else:

                @pl.when(reads(lev))
                def _():
                    arrived(len(users) - 1)

                @pl.when(jnp.logical_not(reads(lev)))
                def _():
                    arrived(len(users))

            for a, readers in enumerate(arrays):
                for f in range(first):
                    total = back[lev, readers[0], f, tiles]
                    for s in readers[1:]:
                        total = total + back[lev, s, f, tiles]
                    q_sum[slot + a, f, tiles] = total
                for d in range(1, first):
                    f = (fpos + d) % first
                    remote(
                        q_sum.at[slot + a, f, tiles],
                        parts.at[slot + a, fpos, tiles],
                        q_send.at[slot + a],
                        q_recv.at[slot + a],
                        (group, 2 * at(f, spos) + core),
                    ).start()
                parts[slot + a, fpos, tiles] = q_sum[slot + a, fpos, tiles]

        when_level(lev, go)

    def parts_in(r):
        lev, tiles, rows_first, first, second, users, arrays, slot = routes[r]
        if first > 1:
            for a in range(len(arrays)):
                part = parts.at[slot + a, pl.ds(0, first - 1), tiles]
                near(part, part, q_send.at[slot + a], q_recv.at[slot + a]).wait_recv()

    @pl.when(core == 1)
    def _():
        rest.wait_recv()
        levels_pass([0])
        g0_copy.start()

    tail_col = jnp.exp(ccol[TOK - 1 : TOK, :] - ccol)
    for p in range(pairs):
        tails[p] = jnp.where(
            col < 64, tail_col[:, 2 * p : 2 * p + 1], tail_col[:, 2 * p + 1 : 2 * p + 2]
        )
        vp = v_ref[:, p * 128 : (p + 1) * 128].astype(F32)
        decayed[p] = (tails[p] * vp).astype(BF16)
    k_low = k.astype(BF16)
    kt_low = kt.astype(BF16).astype(F32)

    k_part = pk.at[pl.ds(0, chips - 1)]
    scales_in = near(k_part, k_part, k_sem.at[0], k_sem.at[1])
    scales_in.wait_recv()
    fetch(low)
    levels_pass([b + 1 for b in low])
    fetch(high)

    @pl.when(group > 0)
    def _():
        levels_pass([b + 1 for b in high])

    give_back(high)

    pulls = rint[...]
    rsum = jnp.broadcast_to(jnp.sum(pulls, axis=1, keepdims=True), (heads, TOK))
    lane = iota((8, 128), 1)
    first_lane = jnp.where((sub == 0) & (lane == 0), 1.0, 0.0)
    mid_lane = jnp.where((sub == 0) & (lane == 64), 1.0, 0.0)
    for p in range(pairs):
        rs[p] = first_lane * rsum[2 * p : 2 * p + 1] + mid_lane * rsum[2 * p + 1 : 2 * p + 2]

    def send_sums(i):
        to = shifted(i)
        remote(
            rs.at[to], rr.at[chip], t_sem.at[0], t_sem.at[1], (group, 2 * to + core)
        ).start()

    loop(1, chips, send_sums)
    rr[chip] = rs[chip]
    for r in high_ways:
        gather_back(r)
    give_back(low)

    def sum_high(r):
        lev, tiles, _, first, _, _, _, slot = routes[r]

        @pl.when(reads(lev))
        def _():
            parts_in(r)
            total = parts[slot, 0, tiles]
            for f in range(1, first):
                total = total + parts[slot, f, tiles]
            u[lev - nb, tiles] = total

    for r in high_ways:
        sum_high(r)

    coef[...] = jnp.zeros((8, 128), F32)
    for d in reversed(range(1, groups)):

        @pl.when(group - d >= 0)
        def _():
            level = high_level(group, group - d, nz)
            grad = u[level]
            z_out[d, 0:4] = grad
            z_out[d, 4] = coef[...]
            remote(
                z_out.at[d], zu.at[group], u_send.at[d], u_recv.at[group], (group - d, me)
            ).start()
            coef[...] = coef[...] + before_far[d] * jnp.sum(grad * zb[group - d, 0:4], axis=0)

    for r in low_ways:
        gather_back(r)

    for j in range(columns // per):
        slabs = []
        for p in range(j * per, (j + 1) * per):
            total = jnp.zeros((heads, TOK), F32)
            for b in range(1 + levels):
                total = total + jnp.where(ids[b] == p, glam[b], 0.0)
            slabs.append(total)
        dlam_ref[:, j * wide : (j + 1) * wide] = jnp.concatenate(slabs, axis=0).T
    results[3].start()
    even = jnp.where(core == 0, 1.0, 0.0)
    dlogt_ref[...] += (
        dot(pulls + rnear[...], (row >= col).astype(F32), precision=highest) - even * rsum
    )
    dqi = (dq_acc[:, 0:128] + dq_acc[:, 128:256]).astype(BF16).astype(F32)
    dst = dsc[...]
    dqt_ref[...] = dqi + dot(kt, dst, precision=highest)
    dkt_ref[...] = dot(dst, q, precision=highest).T
    results[1].start()

    for r in low_ways:
        lev, tiles, rows_first, first, second, users, arrays, slot = routes[r]
        parts_in(r)
        for a in range(len(arrays)):
            if rows_first:
                for f in range(first):
                    dn[offs[lev] + f * (ydim >> lev) + 2 * a, 0:4] = parts[slot + a, f]
            else:
                total = parts[slot + a, 0]
                for f in range(1, first):
                    total = total + parts[slot + a, f]
                dn[offs[lev] + 2 * a, 0:4] = total

    coef[...] = jnp.ones((8, 128), F32)
    dn[top, 0:4] = jnp.zeros((4, 8, 128), F32)
    cown[...] = jnp.zeros((8, 128), F32)
    for l in range(nz):

        @pl.when(bit_of(group, l))
        def _():
            cown[...] = cown[...] + jnp.sum(u[l] * hz[l], axis=0)

    for d in range(1, groups):

        @pl.when(group + d < groups)
        def _():
            far = zb.at[group + d, 4]
            near(far, far, z_send.at[0], zd_recv.at[group + d]).wait_recv()
            slot = zu.at[group + d]
            near(slot, slot, u_send.at[d], u_recv.at[group + d]).wait_recv()
            dn[top, 0:4] = dn[top, 0:4] + coef[...][None] * zu[group + d, 0:4]
            cown[...] = cown[...] + zu[group + d, 4]
            coef[...] = coef[...] * zb[group + d, 4]

    loads[6].wait()
    fu = jnp.concatenate([fu_ref[0], fu_ref[1]], axis=1).reshape(4, 8, 128)
    dn[top, 0:4] = dn[top, 0:4] + coef[...][None] * fu
    earlier = hz[0]
    for l in range(1, nz):
        earlier = earlier + hz[l]
    carry = cown[...] + coef[...] * nd[top, 4] * jnp.sum(earlier * fu, axis=0)
    for b in reversed(range(nb)):
        for i in range(0, chips >> b, 2):
            left = offs[b] + i
            parent = dn[offs[b + 1] + i // 2, 0:4]
            dn[left, 0:4] = dn[left, 0:4] + nd[left + 1, 4][None] * parent
            dn[left + 1, 0:4] = parent

    def give(tiles, a, i):
        to = shifted(a * ydim + i)
        remote(
            dn.at[to, tiles],
            ds.at[core, a, i, tiles],
            o_sem.at[0],
            o_sem.at[1 + a],
            (group, 2 * to + core),
        ).start()

    for a in range(xdim):
        loop(0 if a else 1, ydim, partial(give, slice(0, 4), a))
    t_part = rr.at[pl.ds(0, chips - 1)]
    sums_in = near(t_part, t_part, t_sem.at[0], t_sem.at[1])
    sums_in.wait_recv()
    now = jnp.sum(carry, axis=0, keepdims=True)
    for c in range(chips):
        step = jnp.sum(nd[c, 0:4] * dn[c, 0:4], axis=0) - rr[c]
        then = now + jnp.sum(step, axis=0, keepdims=True)
        dn[c, 4] = jnp.where(sub == 0, now, jnp.where(sub == 1, then, 0.0))
        now = then

    for a in range(xdim):
        loop(0 if a else 1, ydim, partial(give, slice(4, 5), a))
    ds[core, 0, 0] = dn[chip, 0:5]
    for a in range(xdim):
        part = ds.at[core, a] if a else ds.at[core, a, pl.ds(0, ydim - 1)]
        near(part, part, o_sem.at[0], o_sem.at[1 + a]).wait_recv()
        row_in = ds.at[core, a]
        near(row_in, row_in, w_sem.at[0, a], w_sem.at[1, a]).start()

    def all_sent(r):
        lev, tiles, rows_first, first, second, users, arrays, slot = routes[r]

        def out_of_ring(count):
            if count:
                part = h.at[lev, core, pl.ds(0, count * first), tiles]
                near(part, part, h_send.at[r], h_recv.at[r]).wait_send()

        def sends():
            if first > 1:
                for a in range(len(arrays)):
                    part = ring.at[slot + a, pl.ds(0, first - 1), tiles]
                    near(part, part, r_send.at[slot + a], r_recv.at[slot + a]).wait_send()
                    near(part, part, q_send.at[slot + a], q_recv.at[slot + a]).wait_send()
            if lev >= nb:
                out_of_ring(second - 1)

        when_level(lev, sends)

        if lev < nb:

            @pl.when(jnp.logical_not(reads(lev)))
            def _():
                out_of_ring(len(users))

        @pl.when(reads(lev))
        def _():
            if lev < nb:
                out_of_ring(len(users) - 1)
            if second > 1:
                part = st.at[lev, pl.ds(0, (second - 1) * first), tiles]
                near(part, part, b_send.at[r], b_recv.at[r]).wait_send()

    for r in range(len(routes)):
        all_sent(r)
    for lev in range(levels):

        @pl.when(reads(lev))
        def _():
            ours = h.at[lev, core]
            near(ours, ours, f_send.at[lev], f_recv.at[lev]).wait_send()
            swap(lev).wait_send()

    for d in range(1, groups):

        @pl.when(group + d < groups)
        def _():
            up(d).wait_send()

        @pl.when(group - d >= 0)
        def _():
            near(z_out.at[d], z_out.at[d], u_send.at[d], u_recv.at[0]).wait_send()

    swap_half.wait_send()
    swap_dec.wait_send()
    scattered.wait_send()
    decays_in.wait_send()
    lines = zb.at[pl.ds(0, groups - 1), 4]
    near(lines, lines, z_send.at[groups], zd_recv.at[0]).wait_send()
    scales_in.wait_send()
    sums_in.wait_send()

    @pl.when(core == 1)
    def _():
        g0_copy.wait_send()

    @pl.when(core == 0)
    def _():
        rest.wait_send()
        g0_copy.wait_recv()

    part = dn.at[pl.ds(0, chips - 1)]
    near(part, part, o_sem.at[0], o_sem.at[1]).wait_send()

    def finish(a, i):
        p = ((xpos + xdim - a) % xdim) * ydim + (ypos + ydim - i) % ydim
        scale = jnp.where(core == 0, sibd[p], jnp.ones((8, 128), F32))
        dld = jnp.zeros((8, 128), F32)
        lows = []
        for j in range(2):
            grad = ds[j, a, i, 0:4]
            dot_own = jnp.sum(own[p, j] * grad, axis=0)
            dld = dld + jnp.where(sub == core, ds[j, a, i, 4], 0.0)
            dld = dld - jnp.where(core == 0, 0.0, dot_own)
            extra = jnp.where(core == 0, g0[p, j], 0.0)
            lows.append(grad * scale[None] + extra)
        low = jnp.concatenate(lows, axis=0).reshape(64, 128).astype(BF16)
        dld_ref[pl.ds(p, 1), :] = jnp.sum(dld, axis=0, keepdims=True)
        cols = pl.ds(pl.multiple_of(p * 128, 128), 128)
        dv_out[:, cols] = (dv_ref[:, cols] + tails[p] * dot(k_low, low)).astype(BF16)
        both_heads = jnp.concatenate([low * m0[0:64], low * m1[0:64]], axis=0)
        dk = lax.dot_general(
            both_heads, decayed[p], (((1,), (1,)), ((), ())), preferred_element_type=F32
        )
        dkt_ref[...] += dk[0:64] + dk[64:128]
        lrow[pl.ds(2 * p, 1), :] = jnp.sum(kt_low * dk[0:64], axis=0, keepdims=True)
        lrow[pl.ds(2 * p + 1, 1), :] = jnp.sum(kt_low * dk[64:128], axis=0, keepdims=True)

    def row_there(a):
        theirs = ds.at[1 - core, a]
        both = near(theirs, theirs, w_sem.at[0, a], w_sem.at[1, a])
        both.wait_recv()
        both.wait_send()

    for a in range(xdim):
        row_there(a)
        for i in range(ydim):
            finish(a, i)
        cols = pl.ds(pl.multiple_of(((xpos + xdim - a) % xdim) * ydim * 128, 128), ydim * 128)
        results.append(
            pltpu.make_async_copy(dv_out.at[:, cols], dv_any.at[:, cols], out_sem.at[4 + a])
        )
        results[-1].start()
    results[0].start()
    head = iota((heads, pairs), 0)
    rows = dot((iota((heads, pairs), 1) == head // 2).astype(F32), dld_ref[...], precision=highest)
    side = iota((heads, TOK), 1) // 64 == iota((heads, TOK), 0) % 2
    dd = jnp.sum(jnp.where(side, rows, 0.0), axis=1, keepdims=True)
    dlogt_ref[...] += dot(lrow[...], (row < col).astype(F32), precision=highest) + dd
    results[2].start()
    for c in results:
        c.wait()


def end_kernel(*refs):
    n = (len(refs) - 2) // 3
    in_sem, out_sem = refs[-2:]
    loads, stores = [], []
    for i in range(n):
        src, dst, held = refs[i], refs[n + i], refs[2 * n + i]
        cuts = 4 if i == 0 else 1
        step = src.shape[0] // cuts
        for j in range(cuts):
            part = pl.ds(j * step, step)
            k = len(loads)
            loads.append(pltpu.make_async_copy(src.at[part], held.at[part], in_sem.at[k]))
            stores.append(pltpu.make_async_copy(held.at[part], dst.at[part], out_sem.at[k]))
    for c in loads:
        c.start()
    for load, store in zip(loads, stores):
        load.wait()
        store.start()
    for c in stores:
        c.wait()


def body(
    values, state_input, state_output, log_decay, level_lam, level_ids, upstream, final_upstream
):
    shards, groups = lax.axis_size("shard"), lax.axis_size("grp")
    chips = shards // 2
    nb, nz = log2(chips), log2(groups)
    levels = nb + nz
    heads = log_decay.shape[1]
    columns = level_lam.shape[1] // heads
    params = partial(pltpu.CompilerParams, vmem_limit_bytes=VMEM_CAP)
    dma = pltpu.SemaphoreType.DMA
    tile = (4, 8, 128)
    kt = state_input.T
    ydim = 2 ** ((nb + 1) // 2)
    routes = routes_of(nb, nz, chips // ydim, ydim)
    slots = sum(len(route[6]) for route in routes)
    count = len(routes)

    shapes = (
        jax.ShapeDtypeStruct((TOK, heads * 64), BF16),
        f32(64, TOK),
        f32(64, TOK),
        f32(heads, TOK),
        f32(TOK, columns * heads),
    )
    anywhere = pl.BlockSpec(memory_space=pl.ANY)
    parts = pl.pallas_call(
        partial(main_kernel, shards, groups),
        out_shape=shapes,
        in_specs=[pl.BlockSpec(memory_space=pltpu.SMEM)]
        + [anywhere] * 7,
        out_specs=(anywhere,) * 5,
        scratch_shapes=[
            pltpu.VMEM((TOK, heads * 64), BF16),
            pltpu.VMEM((64, TOK), F32),
            pltpu.VMEM((64, TOK), F32),
            pltpu.VMEM((heads, TOK), F32),
            pltpu.VMEM((TOK, columns * heads), F32),
            dma((4 + chips // ydim,)),
            pltpu.VMEM((TOK, heads * 64), F32),
            pltpu.VMEM((heads, TOK), F32),
            pltpu.VMEM((chips, 128), F32),
            pltpu.VMEM((chips, TOK, 128), F32),
            pltpu.VMEM((chips, TOK, 128), BF16),
            pltpu.VMEM((heads, TOK), F32),
            pltpu.VMEM((TOK, heads * 64), BF16),
            pltpu.VMEM((TOK, heads * 64), BF16),
            pltpu.VMEM((64, TOK), F32),
            pltpu.VMEM((64, TOK), F32),
            pltpu.VMEM((heads, TOK), F32),
            pltpu.VMEM((TOK, columns * heads), F32),
            pltpu.VMEM((2, 32, 64), F32),
            dma((7,)),
            pltpu.VMEM((chips, 128, 256), BF16),
            pltpu.VMEM((chips, 256, 128), BF16),
            pltpu.VMEM((columns, heads, TOK), F32),
            pltpu.VMEM((1 + levels, heads, TOK), F32),
            pltpu.VMEM((heads, TOK), F32),
            pltpu.VMEM((heads, TOK), F32),
            pltpu.VMEM((64, 256), F32),
            pltpu.VMEM((TOK, TOK), F32),
            pltpu.VMEM((levels, 2, chips) + tile, F32),
            pltpu.VMEM((chips, 2) + tile, F32),
            pltpu.VMEM((chips, 2) + tile, F32),
            pltpu.VMEM((chips, 8, 128), F32),
            pltpu.VMEM((chips, 2) + tile, F32),
            pltpu.VMEM((chips, 8, 128), F32),
            pltpu.VMEM((chips, 5, 8, 128), F32),
            pltpu.VMEM((2 * chips, 5, 8, 128), F32),
            pltpu.VMEM((groups, 5, 8, 128), F32),
            pltpu.VMEM((nz,) + tile, F32),
            pltpu.VMEM((chips, 8, 128), F32),
            pltpu.VMEM((chips, 8, 128), F32),
            pltpu.VMEM((8, 128), F32),
            pltpu.VMEM((groups, 8, 128), F32),
            pltpu.VMEM((slots, ydim) + tile, F32),
            pltpu.VMEM((levels, 2, chips) + tile, F32),
            pltpu.VMEM((levels, chips) + tile, F32),
            pltpu.VMEM((levels, chips) + tile, F32),
            pltpu.VMEM((levels, ydim, ydim) + tile, F32),
            pltpu.VMEM((slots, ydim) + tile, F32),
            pltpu.VMEM((slots, ydim) + tile, F32),
            pltpu.VMEM((chips, 8, 128), F32),
            pltpu.VMEM((chips, 8, 128), F32),
            pltpu.VMEM((nz,) + tile, F32),
            pltpu.VMEM((groups, 5, 8, 128), F32),
            pltpu.VMEM((groups, 5, 8, 128), F32),
            pltpu.VMEM((8, 128), F32),
            pltpu.VMEM((2 * chips, 5, 8, 128), F32),
            pltpu.VMEM((2, chips // ydim, ydim, 5, 8, 128), F32),
            pltpu.VMEM((chips, 2) + tile, F32),
            dma((6,)),
            dma((2,)),
            dma((groups + 1,)),
            dma((groups,)),
            dma((groups,)),
            dma((2,)),
            dma((2,)),
            dma((slots,)),
            dma((slots,)),
            dma((count,)),
            dma((count,)),
            dma((levels,)),
            dma((levels,)),
            dma((2,)),
            dma((levels,)),
            dma((levels,)),
            dma((count,)),
            dma((count,)),
            dma((slots,)),
            dma((slots,)),
            dma((2,)),
            dma((groups,)),
            dma((groups,)),
            dma((1 + chips // ydim,)),
            dma((2, chips // ydim)),
        ],
        compiler_params=params(collective_id=0, has_side_effects=True),
        name="main",
    )(
        level_ids,
        values,
        upstream,
        kt,
        state_output.T,
        log_decay.T,
        level_lam,
        final_upstream.reshape(chips, 2, 2, 32, 64),
    )

    dv, dk, dq, dlog, dlam = pl.pallas_call(
        end_kernel,
        out_shape=shapes,
        in_specs=[anywhere] * 5,
        out_specs=(anywhere,) * 5,
        scratch_shapes=[pltpu.VMEM(x.shape, x.dtype) for x in shapes] + [dma((8,)), dma((8,))],
        compiler_params=params(),
        name="end",
    )(*parts)
    return (dv, dk.T, dq.T, dlog.T, dlam)


def solution(mesh):
    spec = P(("grp", "shard"), None)
    return jax.shard_map(
        body,
        mesh=mesh,
        in_specs=(spec,) * 7 + (P(),),
        out_specs=(spec,) * 5,
        check_vma=False,
    )
```
